32 devices in a mesh: wide: 8 (over z, y), seq: 4 (over x, core).
Axes of the slice: x: 2, y: 2, z: 4, core: 2. Of those that a mesh axis runs over, the one named last changes fastest.
Arguments:
- tokens: bfloat16 [48, 580, 512], P('wide', 'seq'), may hold values from -6 to 6
- key_mask: int32 [48, 580], P('wide'), may hold values from 0 to 1, as said below
- expert_ids: int32 [48, 580, 2], P('wide', 'seq'), may hold values from 0 to 3, as said below
- ln1_gain: bfloat16 [512], P('wide'), may hold values from 0.5 to 1.5
- ln1_bias: bfloat16 [512], P('wide'), may hold values from -4 to 4
- qkv_weight: bfloat16 [512, 1536], P('wide'), may hold values from -0.25 to 0.25
- proj_weight: bfloat16 [512, 512], P('wide'), may hold values from -6 to 6
- ln2_gain: bfloat16 [512], P('wide'), may hold values from 0.5 to 1.5
- ln2_bias: bfloat16 [512], P('wide'), may hold values from -4 to 4
- router_weight: bfloat16 [512, 4], P('wide'), may hold values from -0.1875 to 0.1875
- up_weight: bfloat16 [4, 512, 2048], P(None, 'wide'), may hold values from -0.25 to 0.25
- down_weight: bfloat16 [4, 2048, 512], P(None, 'wide'), may hold values from -0.375 to 0.375
- cotangent: bfloat16 [48, 580, 512], P('wide', 'seq'), may hold values from -6 to 6
Outputs:
- layer_out: bfloat16 [48, 580, 512], P('wide', 'seq')
- input_grad: float32 [48, 580, 512], P('wide', 'seq')
- grad_ln1_gain: float32 [512], P('wide')
- grad_ln1_bias: float32 [512], P('wide')
- grad_qkv: float32 [512, 1536], P('wide')
- grad_proj: float32 [512, 512], P('wide')
- grad_ln2_gain: float32 [512], P('wide')
- grad_ln2_bias: float32 [512], P('wide')
- grad_router: float32 [512, 4], P('wide')
- grad_up: float32 [4, 512, 2048], P(None, 'wide')
- grad_down: float32 [4, 2048, 512], P(None, 'wide')
The draws below stay inside these ranges and needn't reach their ends.
Inputs may be any that keep to these rules, and one draw needn't show every extreme that they name: `key_mask`: position 0 of every image is 1, the last 3 positions are 0. `expert_ids`: the two numbers of a token differ. Among the 290 tokens that one device holds of one micro-batch (images m * 2 to (m + 1) * 2 - 1 of its images, all its positions), every expert is named by exactly 145 tokens.
All inputs are finite; a program needn't handle non-finite values.
Results may differ from the reference program's by a relative error of at most 0.0093.
Values may be sent and summed in bfloat16 or wider, within the bound.
No kernel may reach another device: no remote copies, remote signals or barrier semaphores. Data moves between devices by JAX's collectives and lax.ppermute only.
A program may use at most 136 MiB of HBM per device.

```python
import jax
import jax.numpy as jnp
from jax import lax

D = 512
FF = 2048
H = 8
E = 4
L = 580
PADS = 3
IMG_MB = 2
IMAGES = 48
ROWS = 290
N_SEQ = 4


def draw_expert_ids(key, part):
    key = jax.random.fold_in(key, 11)
    blocks = IMAGES // IMG_MB * N_SEQ
    quarter = L // N_SEQ
    keys_all = jax.random.split(key, blocks + 1)
    rank_rows = jax.vmap(lambda subkey: jax.random.permutation(subkey, ROWS))(keys_all[:blocks])
    pair_table = jnp.array([[0, 1], [2, 3], [0, 2], [1, 3], [0, 3], [1, 2]], dtype=jnp.int32)
    chosen_pairs = pair_table[rank_rows % 6]
    flip_bits = jax.random.randint(keys_all[blocks], (blocks, ROWS, 1), 0, 2)
    chosen_pairs = jnp.where(flip_bits > 0, chosen_pairs[..., ::-1], chosen_pairs)
    chosen_pairs = chosen_pairs.reshape(IMAGES // IMG_MB, N_SEQ, IMG_MB, quarter, 2)
    chosen_pairs = jnp.transpose(chosen_pairs, (0, 2, 1, 3, 4))
    return chosen_pairs.reshape(IMAGES, L, 2).astype(jnp.int32)


def draw_key_mask(key, part):
    key = jax.random.fold_in(key, 23)
    places = jnp.arange(L, dtype=jnp.int32)[None, :]
    drawn = jax.random.randint(key, (IMAGES, L), 0, 8)
    keeping = ((drawn > 0) | (places == 0)) & (places < L - PADS)
    return keeping.astype(jnp.int32)


def raised(values, stream_key, source, target, parts, factor):
    def block_of(position):
        return (jnp.arange(values.shape[position]) // (values.shape[position] // parts)).reshape((-1,) + (1,) * (values.ndim - 1 - position))

    one_side = jax.random.permutation(stream_key, parts)[block_of(target)]
    other_side = (block_of(target) + parts // 2) % parts
    return jnp.where((block_of(source) == one_side) | (block_of(source) == other_side), factor * values, values)


def block_levels(own_key, extent, shards, smallest, high):
    factor_of = 1.0
    for axis_at, parts in shards:
        steps = jax.random.uniform(jax.random.fold_in(jax.random.fold_in(own_key, 6), axis_at), (parts,), jnp.float32, smallest / len(shards), high / len(shards))
        factor_of = factor_of * jnp.repeat(jnp.exp(steps), extent[axis_at] // parts).reshape((-1,) + (1,) * (len(extent) - 1 - axis_at))
    return factor_of


def scatter_about(rng, extent, deviation, most, cuts=(), kind=jnp.bfloat16):
    values = deviation * jax.random.normal(rng, extent, jnp.float32)
    if cuts:
        values = values * block_levels(rng, extent, cuts, -0.22, 0.18)
    return jnp.clip(values, -most, most).astype(kind)


def gaussian_with(rng, dims, deviation, most, cuts, heavy, kind=jnp.bfloat16):
    entries = deviation * jax.random.normal(rng, dims, jnp.float32)
    if cuts:
        entries = entries * block_levels(rng, dims, cuts, -0.22, 0.18)
    return jnp.clip(raised(entries, jax.random.fold_in(rng, 3), *heavy), -most, most).astype(kind)


def setup_inputs(seed: int = 0) -> dict:
    streams_of = jax.random.split(jax.random.key(seed), 14)
    return {
        "tokens": gaussian_with(streams_of[0], (IMAGES, L, D), 1.0, 6.0, ((0, 8), (1, 4)), (0, 2, 8, 2.0)),
        "key_mask": draw_key_mask(jax.random.fold_in(streams_of[13], 71), 0),
        "expert_ids": draw_expert_ids(jax.random.fold_in(streams_of[13], 71), 0),
        "ln1_gain": jnp.clip(1.0 + 0.1 * jax.random.normal(streams_of[3], (D,), jnp.float32), 0.5, 1.5).astype(jnp.bfloat16),
        "ln1_bias": scatter_about(streams_of[4], (D,), 0.3, 4.0, ((0, 8),)),
        "qkv_weight": scatter_about(streams_of[5], (D, 3 * D), D ** -0.5, 0.25, ((0, 8),)),
        "proj_weight": scatter_about(streams_of[6], (D, D), (max(2 * D // L, 1)) ** -0.5, 6.0, ((0, 8),)),
        "ln2_gain": jnp.clip(1.0 + 0.1 * jax.random.normal(streams_of[7], (D,), jnp.float32), 0.5, 1.5).astype(jnp.bfloat16),
        "ln2_bias": scatter_about(streams_of[8], (D,), 0.3, 4.0, ((0, 8),)),
        "router_weight": scatter_about(streams_of[9], (D, E), (2 * D) ** -0.5, 0.1875, ((0, 8),)),
        "up_weight": scatter_about(streams_of[10], (E, D, FF), D ** -0.5, 0.25, ((1, 8),)),
        "down_weight": scatter_about(streams_of[11], (E, FF, D), (FF // 8) ** -0.5, 0.375, ((1, 8),)),
        "cotangent": gaussian_with(streams_of[12], (IMAGES, L, D), 1.0, 6.0, ((0, 8), (1, 4)), (0, 2, 8, 2.0)),
    }


@jax.custom_vjp
def low(v):
    return lax.optimization_barrier(v.astype(jnp.bfloat16)).astype(jnp.float32)

@jax.custom_vjp
def low_back(v):
    return v

def low_keep(v):
    return (low(v), None)

def low_pass(kept, grad):
    return (grad,)

def back_keep(v):
    return (v, None)

def back_low(kept, grad):
    return (low(grad),)
low.defvjp(low_keep, low_pass)
low_back.defvjp(back_keep, back_low)
EPSILON = 1e-06
HIGHEST = lax.Precision.HIGHEST

def layer_norm(values, gain, offset):
    center = values - lax.optimization_barrier(jnp.mean(values, axis=-1, keepdims=True))
    spread = lax.optimization_barrier(jnp.mean(center * center, axis=-1, keepdims=True))
    return center * lax.rsqrt(spread + EPSILON) * gain + offset

def attend_image(inputs):
    queries, key_rows, value_rows, valid = inputs
    scaling = 1.0 / jnp.sqrt(jnp.float32(queries.shape[-1]))
    raw_scores = jnp.einsum('qhd,khd->hqk', queries, key_rows, precision=HIGHEST) * scaling
    scores = low_back(raw_scores)
    scores = jnp.where(valid[None, None, :] > 0, scores, -1e+30)
    peak = lax.optimization_barrier(jnp.max(scores, axis=-1, keepdims=True))
    exponent = jnp.exp(scores - peak)
    probs = low(exponent / lax.optimization_barrier(jnp.sum(exponent, axis=-1, keepdims=True)))
    return jnp.einsum('hqk,khd->qhd', probs, value_rows, precision=HIGHEST)

def forward(params, tokens_f, id_block, mask_block):
    gain_one, offset_one, qkv_full, proj_full, gain_two, offset_two, router_full, up_full, down_full = params
    images, length, width = tokens_f.shape
    head_dim = width // H
    hidden_one = low(layer_norm(tokens_f, gain_one, offset_one))
    packed = low(low_back(jnp.einsum('gld,de->gle', hidden_one, qkv_full, precision=HIGHEST)))
    packed = packed.reshape(images, length, 3, H, head_dim)
    attended = lax.map(jax.checkpoint(attend_image), (packed[:, :, 0], packed[:, :, 1], packed[:, :, 2], mask_block))
    attended = low(low_back(attended)).reshape(images, length, width)
    branch = low_back(jnp.einsum('gld,de->gle', attended, proj_full, precision=HIGHEST))
    middle = tokens_f + branch
    hidden_two = low(layer_norm(middle, gain_two, offset_two))
    logits = low_back(jnp.einsum('gld,de->gle', hidden_two, router_full, precision=HIGHEST))
    exponent = jnp.exp(logits - lax.optimization_barrier(jnp.max(logits, axis=-1, keepdims=True)))
    router = exponent / lax.optimization_barrier(jnp.sum(exponent, axis=-1, keepdims=True))
    expert_range = jnp.arange(E, dtype=jnp.int32)
    chosen = (id_block[..., 0:1] == expert_range) | (id_block[..., 1:2] == expert_range)
    combined = router * chosen.astype(router.dtype)
    mixed = middle
    for expert in range(E):
        hidden_pre = low_back(jnp.einsum('gld,df->glf', hidden_two, up_full[expert], precision=HIGHEST))
        activated = low(jax.nn.gelu(hidden_pre, approximate=False))
        returned = low_back(jnp.einsum('glf,fd->gld', activated, down_full[expert], precision=HIGHEST))
        mixed = mixed + combined[..., expert:expert + 1] * returned
    return mixed

def reference(tokens, key_mask, expert_ids, ln1_gain, ln1_bias, qkv_weight, proj_weight, ln2_gain, ln2_bias, router_weight, up_weight, down_weight, cotangent):
    params = tuple((weight.astype(jnp.float32) for weight in (ln1_gain, ln1_bias, qkv_weight, proj_weight, ln2_gain, ln2_bias, router_weight, up_weight, down_weight)))
    groups = IMAGES // IMG_MB

    def shaped(array):
        return array.reshape((groups, IMG_MB) + array.shape[1:])

    def one_group(totals, inputs):
        tok_block, cot_block, id_block, mask_block = inputs

        def run_block(weights, tokens_f):
            return forward(weights, tokens_f, id_block, mask_block)
        result, pullback = jax.vjp(run_block, params, tok_block.astype(jnp.float32))
        grads_weights, grad_tokens = pullback(cot_block.astype(jnp.float32))
        totals = jax.tree.map(jnp.add, totals, grads_weights)
        return (totals, (result.astype(jnp.bfloat16), grad_tokens))
    zeros = jax.tree.map(jnp.zeros_like, params)
    totals, (outputs, grads_in) = lax.scan(one_group, zeros, (shaped(tokens), shaped(cotangent), shaped(expert_ids), shaped(key_mask)))
    return (outputs.reshape(IMAGES, L, D), grads_in.reshape(IMAGES, L, D), totals[0], totals[1], totals[2], totals[3], totals[4], totals[5], totals[6], totals[7], totals[8])
```

```python
import functools
import math

import jax
import jax.numpy as jnp
from jax import lax
from jax.experimental import pallas as pl
from jax.experimental.pallas import tpu as pltpu
from jax.sharding import PartitionSpec as P

H = 8
E = 4
EPSILON = 1e-06
BIG = -1e30
MIB = 1024 * 1024
F32 = jnp.float32
BF16 = jnp.bfloat16


def dot(a, b, dims=((1,), (0,))):
    return lax.dot_general(a, b, (dims, ((), ())), preferred_element_type=F32)


def dot_nt(a, b):
    return dot(a, b, ((1,), (1,)))


def dot_tn(a, b):
    return dot(a, b, ((0,), (0,)))


def norm_parts(values):
    center = values - jnp.mean(values, axis=-1, keepdims=True)
    spread = jnp.mean(center * center, axis=-1, keepdims=True)
    rstd = lax.rsqrt(spread + EPSILON)
    return center * rstd, rstd


def norm_back(grad, xhat, rstd):
    return rstd * (
        grad
        - jnp.mean(grad, axis=-1, keepdims=True)
        - xhat * jnp.mean(grad * xhat, axis=-1, keepdims=True)
    )


def params(limit, **more):
    return pltpu.CompilerParams(vmem_limit_bytes=limit * MIB, **more)


def whole(shape):
    return pl.BlockSpec(shape, lambda *_: (0,) * len(shape))


def per_image(*shape):
    return pl.BlockSpec((1, *shape), lambda i: (i,) + (0,) * len(shape))


def attend_kernel(
    head_dim, own_ref, oth_ref, bias_ref, vec_ref, wq_ref,
    att_m_ref, att_o_ref, qkv_ref, hidden_ref, lse_ref,
):
    rows = own_ref.shape[1]
    gain, offset = vec_ref[0:1, :], vec_ref[1:2, :]
    for half, ref in enumerate((own_ref, oth_ref)):
        xhat, _ = norm_parts(ref[0].astype(F32))
        hidden_ref[0, half * rows : (half + 1) * rows, :] = (xhat * gain + offset).astype(BF16)
    width = wq_ref.shape[1] // 3
    packed = dot(hidden_ref[0], wq_ref[...]).astype(BF16)
    scaling = 1.0 / math.sqrt(head_dim)
    qkv_ref[0, :, :width] = (packed[:, :width].astype(F32) * scaling).astype(BF16)
    qkv_ref[0, :, width:] = packed[:, width:]
    bias = bias_ref[0]
    lane = lax.broadcasted_iota(jnp.int32, (1, 128), 1)
    sub = lax.broadcasted_iota(jnp.int32, (128, 1), 0)
    for pair in range(width // 128):
        cols = slice(pair * 128, pair * 128 + 128)
        q2 = qkv_ref[0, :, cols]
        k2 = qkv_ref[0, :, width + pair * 128 : width + pair * 128 + 128]
        v2 = qkv_ref[0, :, 2 * width + pair * 128 : 2 * width + pair * 128 + 128]
        v_t = v2.T
        both = []
        for part in range(2):
            mine = (lane >= head_dim * part) & (lane < head_dim * (part + 1))
            qm = jnp.where(mine, q2, jnp.zeros_like(q2))
            scores = dot_nt(k2, qm) + bias
            peak = jnp.max(scores, axis=0, keepdims=True)
            expo = jnp.exp(scores - peak)
            total = jnp.sum(expo, axis=0, keepdims=True)
            lse_ref[0, 2 * pair + part : 2 * pair + part + 1, :] = peak + jnp.log(total)
            both.append(dot(v_t, expo.astype(BF16)) * (1.0 / total))
        out = jnp.where(sub < head_dim, both[0], both[1]).astype(BF16).T
        att_m_ref[0, :, cols] = out[:rows]
        att_o_ref[0, :, cols] = out[rows:]


def attend(x_own, x_oth, bias, vecs, wq, head_dim):
    images, rows, width = x_own.shape
    group = wq.shape[1] // 3
    return pl.pallas_call(
        functools.partial(attend_kernel, head_dim),
        grid=(images,),
        in_specs=[
            per_image(rows, width),
            per_image(rows, width),
            per_image(2 * rows, 1),
            whole(vecs.shape),
            whole(wq.shape),
        ],
        out_specs=[
            per_image(rows, group),
            per_image(rows, group),
            per_image(2 * rows, 3 * group),
            per_image(2 * rows, width),
            per_image(8, 2 * rows),
        ],
        out_shape=[
            jax.ShapeDtypeStruct((images, rows, group), BF16),
            jax.ShapeDtypeStruct((images, rows, group), BF16),
            jax.ShapeDtypeStruct((images, 2 * rows, 3 * group), BF16),
            jax.ShapeDtypeStruct((images, 2 * rows, width), BF16),
            jax.ShapeDtypeStruct((images, 8, 2 * rows), F32),
        ],
        compiler_params=params(40),
        name="attend",
    )(x_own, x_oth, bias, vecs, wq)


def project_kernel(att_m_ref, att_r_ref, x_ref, pm_ref, pr_ref, vec_ref, middle_ref, hidden_ref):
    middle = (
        x_ref[0].astype(F32) + dot(att_m_ref[0], pm_ref[...]) + dot(att_r_ref[0], pr_ref[...])
    )
    middle_ref[0] = middle
    xhat, _ = norm_parts(middle)
    hidden_ref[0] = (xhat * vec_ref[2:3, :] + vec_ref[3:4, :]).astype(BF16)


def project(att_m, att_r, x_own, proj_m, proj_r, vecs):
    images, rows, width = x_own.shape
    group = att_m.shape[2]
    return pl.pallas_call(
        project_kernel,
        grid=(images,),
        in_specs=[
            per_image(rows, group),
            per_image(rows, group),
            per_image(rows, width),
            whole(proj_m.shape),
            whole(proj_r.shape),
            whole(vecs.shape),
        ],
        out_specs=[per_image(rows, width), per_image(rows, width)],
        out_shape=[
            jax.ShapeDtypeStruct(x_own.shape, F32),
            jax.ShapeDtypeStruct(x_own.shape, BF16),
        ],
        compiler_params=params(24),
        name="project",
    )(att_m, att_r, x_own, proj_m, proj_r, vecs)


BLOCKS = (
    ((0, 0), (0, 1)),
    ((2, 0), (2, 1)),
    ((1, 0), (1, 1)),
    ((3, 0), (3, 1)),
    ((0, 2), (1, 2)),
    ((2, 2), (3, 2)),
)


def expert_kernel(
    splits, pos_ref, h0, h1, h2, h3, c0, c1, c2, c3, up_ref, down_ref, wr_ref, sel_ref,
    ret_m, ret_o, dh_m, dh_o, xs_ref, g_ref, lg_ref, act_ref, gp_ref,
    cs_ref, ret_ref, dx_ref,
):
    step = pl.program_id(0)
    rows = h0.shape[1]
    hs, cs = (h0, h1, h2, h3), (c0, c1, c2, c3)
    slot = lax.broadcasted_iota(jnp.int32, (rows, rows), 0)
    picks = [
        (slot == pos_ref[0, k : k + 1, :]).astype(F32).astype(BF16) for k in range(2)
    ]
    for number, block in enumerate(BLOCKS):

        @pl.when(step == number)
        def _(block=block):
            (pa, ia), (pb, ib) = block
            xs_ref[...] = (dot(picks[0], hs[pa][ia]) + dot(picks[1], hs[pb][ib])).astype(BF16)
            cs_ref[...] = (dot(picks[0], cs[pa][ia]) + dot(picks[1], cs[pb][ib])).astype(BF16)

    xs = xs_ref[...]
    logits = dot(xs, wr_ref[...])
    lane = lax.broadcasted_iota(jnp.int32, (1, 128), 1)
    logits = jnp.where(lane < E, logits, BIG)
    grown = jnp.exp(logits - jnp.max(logits, axis=-1, keepdims=True))
    router = grown / jnp.sum(grown, axis=-1, keepdims=True)
    sel = sel_ref[...]
    weight = jnp.sum(router * sel, axis=-1, keepdims=True)
    g_ref[...] = (cs_ref[...].astype(F32) * weight).astype(BF16)
    ff = up_ref.shape[1]
    chunk = ff // splits
    for part in range(splits):
        cols = slice(part * chunk, (part + 1) * chunk)
        pre = dot(xs, up_ref[:, cols])
        back = dot_nt(g_ref[...], down_ref[cols, :])
        cdf = 0.5 + 0.5 * lax.erf(pre * math.sqrt(0.5))
        pdf = jnp.exp(-0.5 * pre * pre) * (1.0 / math.sqrt(2.0 * math.pi))
        act = (pre * cdf).astype(BF16)
        gp = (back * (cdf + pre * pdf)).astype(BF16)
        act_ref[:, cols] = act
        gp_ref[:, cols] = gp
        ret = dot(act, down_ref[cols, :])
        dx = dot_nt(gp, up_ref[:, cols])
        if part == 0:
            ret_ref[...] = ret
            dx_ref[...] = dx
        else:
            ret_ref[...] += ret
            dx_ref[...] += dx
    gate = jnp.sum(cs_ref[...].astype(F32) * ret_ref[...], axis=-1, keepdims=True)
    lg = (gate * weight * (sel - router)).astype(BF16)
    lg_ref[...] = lg
    dxb = (dx_ref[...] + dot_nt(lg, wr_ref[...])).astype(BF16)
    retb = (ret_ref[...] * weight).astype(BF16)
    rets, dhs = (ret_m, ret_o), (dh_m, dh_o)
    for number, block in enumerate(BLOCKS):

        @pl.when(step == number)
        def _(block=block):
            for pick, (piece, image) in zip(picks, block):
                rets[piece // 2][piece % 2, image] = dot_tn(pick, retb).astype(BF16)
                dhs[piece // 2][piece % 2, image] = dot_tn(pick, dxb).astype(BF16)


def run_expert(pos, hidden, cots, up, down, wr, sel):
    images, rows, width = hidden[0].shape
    ff = up.shape[1]
    count = len(BLOCKS)
    piece = whole((images, rows, width))
    pairs = whole((2, images, rows, width))
    pair_shape = jax.ShapeDtypeStruct((2, images, rows, width), BF16)

    def slots(cols, dtype=BF16):
        return (
            pl.BlockSpec((rows, cols), lambda i: (i, 0)),
            jax.ShapeDtypeStruct((count * rows, cols), dtype),
        )

    per_slot = [slots(width), slots(width), slots(128), slots(ff), slots(ff)]
    return pl.pallas_call(
        functools.partial(expert_kernel, 4),
        grid=(count,),
        in_specs=[
            pl.BlockSpec((1, 2, rows), lambda i: (i, 0, 0)),
            *[piece] * 8,
            whole(up.shape),
            whole(down.shape),
            whole(wr.shape),
            whole(sel.shape),
        ],
        out_specs=[pairs] * 4 + [spec for spec, _ in per_slot],
        out_shape=[pair_shape] * 4 + [shape for _, shape in per_slot],
        scratch_shapes=[
            pltpu.VMEM((rows, width), BF16),
            pltpu.VMEM((rows, width), F32),
            pltpu.VMEM((rows, width), F32),
        ],
        compiler_params=params(56),
        name="expert",
    )(pos, *hidden, *cots, up, down, wr, sel)


def middle_back_kernel(a_ref, ar_ref, xr_ref, mid_ref, cot_ref, vec_ref, gm_ref, low_ref, sums_ref):
    @pl.when(pl.program_id(0) == 0)
    def _():
        sums_ref[...] = jnp.zeros_like(sums_ref)

    grad = a_ref[0].astype(F32) + ar_ref[0].astype(F32) + xr_ref[0].astype(F32)
    xhat, rstd = norm_parts(mid_ref[0])
    sums_ref[0:1, :] += jnp.sum(grad * xhat, axis=0, keepdims=True)
    sums_ref[1:2, :] += jnp.sum(grad, axis=0, keepdims=True)
    out = cot_ref[0].astype(F32) + norm_back(grad * vec_ref[2:3, :], xhat, rstd)
    gm_ref[0] = out
    low_ref[0] = out.astype(BF16)


def middle_back(a, ar, xr, middle, cot, vecs):
    images, rows, width = middle.shape
    one = per_image(rows, width)
    return pl.pallas_call(
        middle_back_kernel,
        grid=(images,),
        in_specs=[one] * 5 + [whole(vecs.shape)],
        out_specs=[one, one, whole((8, width))],
        out_shape=[
            jax.ShapeDtypeStruct(middle.shape, F32),
            jax.ShapeDtypeStruct(middle.shape, BF16),
            jax.ShapeDtypeStruct((8, width), F32),
        ],
        compiler_params=params(24),
        name="middle_back",
    )(a, ar, xr, middle, cot, vecs)


def attend_back_kernel(
    head_dim, lm_ref, lo_ref, pm_ref, qkv_ref, lse_ref, am_ref, ao_ref, bias_ref, h1_ref, wq_ref,
    dm_ref, do_ref, gq_ref, gp_ref, grad_ref, att_ref, low_ref,
):
    rows = lm_ref.shape[1]
    low_ref[:rows, :] = lm_ref[0]
    low_ref[rows:, :] = lo_ref[0]
    att_ref[:rows, :] = am_ref[0]
    att_ref[rows:, :] = ao_ref[0]
    out_grad = dot_nt(low_ref[...], pm_ref[...]).astype(BF16)
    width = pm_ref.shape[0]
    bias = bias_ref[0]
    lane = lax.broadcasted_iota(jnp.int32, (1, 128), 1)
    sub = lax.broadcasted_iota(jnp.int32, (128, 1), 0)
    scaling = 1.0 / math.sqrt(head_dim)
    for pair in range(width // 128):
        cols = slice(pair * 128, pair * 128 + 128)
        k_cols = slice(width + pair * 128, width + pair * 128 + 128)
        v_cols = slice(2 * width + pair * 128, 2 * width + pair * 128 + 128)
        q2, k2, v2 = qkv_ref[0, :, cols], qkv_ref[0, :, k_cols], qkv_ref[0, :, v_cols]
        o2 = out_grad[:, cols]
        k_t = k2.T
        dv = dk = None
        both = []
        for part in range(2):
            mine = (lane >= head_dim * part) & (lane < head_dim * (part + 1))
            qm = jnp.where(mine, q2, jnp.zeros_like(q2))
            om = jnp.where(mine, o2, jnp.zeros_like(o2))
            head = 2 * pair + part
            probs = jnp.exp(dot_nt(k2, qm) + bias - lse_ref[0, head : head + 1, :])
            prob_grad = dot_nt(v2, om)
            delta = jnp.sum(probs * prob_grad, axis=0, keepdims=True)
            score_grad = (probs * (prob_grad - delta)).astype(BF16)
            dv_part = dot(probs.astype(BF16), om)
            dk_part = dot(score_grad, qm)
            dv = dv_part if dv is None else dv + dv_part
            dk = dk_part if dk is None else dk + dk_part
            both.append(dot(k_t, score_grad))
        dq = (jnp.where(sub < head_dim, both[0], both[1]) * scaling).astype(BF16).T
        grad_ref[:, cols] = dq
        grad_ref[:, k_cols] = dk.astype(BF16)
        grad_ref[:, v_cols] = dv.astype(BF16)
    hidden_grad = dot_nt(grad_ref[...], wq_ref[...]).astype(BF16)
    dm_ref[0] = hidden_grad[:rows]
    do_ref[0] = hidden_grad[rows:]

    @pl.when(pl.program_id(0) == 0)
    def _():
        gq_ref[...] = jnp.zeros_like(gq_ref)
        gp_ref[...] = jnp.zeros_like(gp_ref)

    gq_ref[...] += dot_tn(h1_ref[0], grad_ref[...])
    gp_ref[...] += dot_tn(att_ref[...], low_ref[...])


def attend_back(low_m, low_o, proj_m, qkv, lse, att_m, att_o, bias, hidden_one, wq, head_dim):
    images, rows, width = low_m.shape
    group = att_m.shape[2]
    return pl.pallas_call(
        functools.partial(attend_back_kernel, head_dim),
        grid=(images,),
        in_specs=[
            per_image(rows, width),
            per_image(rows, width),
            whole(proj_m.shape),
            per_image(2 * rows, 3 * group),
            per_image(8, 2 * rows),
            per_image(rows, group),
            per_image(rows, group),
            per_image(2 * rows, 1),
            per_image(2 * rows, width),
            whole(wq.shape),
        ],
        out_specs=[
            per_image(rows, width),
            per_image(rows, width),
            whole((width, 3 * group)),
            whole((group, width)),
        ],
        out_shape=[
            jax.ShapeDtypeStruct((images, rows, width), BF16),
            jax.ShapeDtypeStruct((images, rows, width), BF16),
            jax.ShapeDtypeStruct((width, 3 * group), F32),
            jax.ShapeDtypeStruct((group, width), F32),
        ],
        scratch_shapes=[
            pltpu.VMEM((2 * rows, 3 * group), BF16),
            pltpu.VMEM((2 * rows, group), BF16),
            pltpu.VMEM((2 * rows, width), BF16),
        ],
        compiler_params=params(48),
        name="attend_back",
    )(low_m, low_o, proj_m, qkv, lse, att_m, att_o, bias, hidden_one, wq)


def input_back_kernel(a_ref, ar_ref, x_ref, gm_ref, vec_ref, out_ref, sums_ref):
    @pl.when(pl.program_id(0) == 0)
    def _():
        sums_ref[...] = jnp.zeros_like(sums_ref)

    grad = a_ref[0].astype(F32) + ar_ref[0].astype(F32)
    xhat, rstd = norm_parts(x_ref[0].astype(F32))
    sums_ref[0:1, :] += jnp.sum(grad * xhat, axis=0, keepdims=True)
    sums_ref[1:2, :] += jnp.sum(grad, axis=0, keepdims=True)
    out_ref[0] = gm_ref[0] + norm_back(grad * vec_ref[0:1, :], xhat, rstd)


def input_back(a, ar, x_own, grad_middle, vecs):
    images, rows, width = x_own.shape
    one = per_image(rows, width)
    return pl.pallas_call(
        input_back_kernel,
        grid=(images,),
        in_specs=[one] * 4 + [whole(vecs.shape)],
        out_specs=[one, whole((8, width))],
        out_shape=[
            jax.ShapeDtypeStruct(x_own.shape, F32),
            jax.ShapeDtypeStruct((8, width), F32),
        ],
        compiler_params=params(24),
        name="input_back",
    )(a, ar, x_own, grad_middle, vecs)


def shards(
    tokens,
    key_mask,
    expert_ids,
    ln1_gain,
    ln1_bias,
    qkv_weight,
    proj_weight,
    ln2_gain,
    ln2_bias,
    router_weight,
    up_weight,
    down_weight,
    cotangent,
):
    n_seq = lax.axis_size("seq")
    images, quarter, width = tokens.shape
    head_dim = width // H
    group = width // 2
    rows = -(-2 * quarter // 16) * 16
    place = lax.axis_index("seq")
    chip, core = place // 2, place % 2
    flip_x = [(i, i ^ 2) for i in range(n_seq)]
    flip_core = [(i, i ^ 1) for i in range(n_seq)]

    def over_x(a):
        return lax.ppermute(a, "seq", flip_x)

    def over_core(a):
        return lax.ppermute(a, "seq", flip_core)

    def images_of(a, of_chip):
        pair = lax.dynamic_slice_in_dim(a, of_chip * (images - 2), 2, 0)
        single = lax.dynamic_slice_in_dim(a, images // 2 - 1 + of_chip, 1, 0)
        return jnp.concatenate([pair, single], axis=0)

    def joined(first, second):
        both = jnp.concatenate([first, second], axis=1)
        return jnp.pad(both, ((0, 0), (0, rows - 2 * quarter)) + ((0, 0),) * (both.ndim - 2))

    down_rows = down_weight.shape[1]
    wq_shard = lax.dynamic_slice_in_dim(
        qkv_weight.reshape(-1, 3, 2, group), core, 1, axis=2
    ).reshape(-1, 3 * group)
    vec_shard = jnp.stack([ln1_gain, ln1_bias, ln2_gain, ln2_bias], axis=1)
    pack = jnp.concatenate(
        [
            wq_shard,
            proj_weight,
            vec_shard,
            router_weight,
            jnp.zeros((vec_shard.shape[0], 128 - 4 - E), BF16),
        ],
        axis=1,
    )
    pack = lax.all_gather(pack, "wide", axis=0, tiled=True)
    wq = pack[:, : 3 * group]
    proj = pack[:, 3 * group : 3 * group + width]
    small = pack[:, 3 * group + width :]
    vecs = jnp.pad(small[:, :4].astype(F32).T, ((0, 4), (0, 0)))
    wr = jnp.pad(small[:, 4 : 4 + E], ((0, 0), (0, 128 - E)))
    proj_m = lax.dynamic_slice_in_dim(proj, core * group, group, 0)
    proj_r = lax.dynamic_slice_in_dim(proj, (1 - core) * group, group, 0)
    up = lax.all_gather(
        lax.dynamic_index_in_dim(up_weight, place, 0, False), "wide", axis=0, tiled=True
    )
    down = lax.all_gather(
        lax.dynamic_index_in_dim(down_weight, place, 0, False), "wide", axis=0, tiled=True
    )

    x_own = joined(images_of(tokens, chip), over_x(images_of(tokens, 1 - chip)))
    x_oth = over_core(x_own)
    cot_got = over_x(cotangent)
    cot_a = joined(images_of(cotangent, chip), images_of(cot_got, chip))
    cot_b = joined(images_of(cot_got, 1 - chip), images_of(cotangent, 1 - chip))
    cots = (cot_a, cot_b, over_core(cot_a), over_core(cot_b))

    def cells(quarters, of_chip, of_core):
        first = lax.dynamic_index_in_dim(quarters, 2 * of_chip + of_core, 1, False)
        second = lax.dynamic_index_in_dim(quarters, 2 * (1 - of_chip) + of_core, 1, False)
        return joined(images_of(first, of_chip), images_of(second, of_chip))

    mask = key_mask.reshape(images, n_seq, quarter)
    valid = jnp.concatenate([cells(mask, chip, core), cells(mask, chip, 1 - core)], axis=1)
    bias = jnp.where(valid > 0, 0.0, BIG).astype(F32)[..., None]
    ids = lax.all_gather(expert_ids, "seq", axis=1)
    chosen = jnp.any(ids == place, axis=-1).astype(jnp.int32)
    flags = [
        cells(chosen, a, b)
        for a, b in ((chip, core), (1 - chip, core), (chip, 1 - core), (1 - chip, 1 - core))
    ]
    flags = jnp.stack([jnp.concatenate([flags[p][i] for p, i in block]) for block in BLOCKS])
    before = (
        lax.broadcasted_iota(jnp.int32, (2 * rows, 2 * rows), 0)
        < lax.broadcasted_iota(jnp.int32, (2 * rows, 2 * rows), 1)
    ).astype(BF16)
    rank = dot(flags.astype(BF16), before).astype(jnp.int32)
    pos = jnp.where(flags > 0, rank, -1).reshape(len(BLOCKS), 2, rows)
    sel = (jnp.arange(128, dtype=jnp.int32) == place).astype(F32)[None, :]

    att_m, att_o, qkv, hidden_one, lse = attend(x_own, x_oth, bias, vecs, wq, head_dim)
    att_r = over_core(att_o)
    middle, hidden_two = project(att_m, att_r, x_own, proj_m, proj_r, vecs)

    hidden_b = over_x(hidden_two)
    hidden = (hidden_two, hidden_b, over_core(hidden_two), over_core(hidden_b))
    ret_m, ret_o, dh_m, dh_o, xs, g_slots, lg, act, gp = run_expert(
        pos, hidden, cots, up, down, wr, sel
    )
    dh_r = over_core(dh_o)
    dh_x = over_x(dh_m[1] + dh_r[1])
    ret_r = over_core(ret_o)
    ret_x = over_x(ret_m[1] + ret_r[1])
    grad_up = dot_tn(xs, gp).astype(BF16)
    grad_down = dot_tn(act, g_slots).astype(BF16)
    grad_router = dot_tn(xs, lg)
    layer = (
        middle + ret_m[0].astype(F32) + ret_r[0].astype(F32) + ret_x.astype(F32)
    ).astype(BF16)

    grad_middle, low_m, sums_two = middle_back(dh_m[0], dh_r[0], dh_x, middle, cot_a, vecs)
    low_o = over_core(low_m)
    dh1_m, dh1_o, grad_qkv, grad_proj = attend_back(
        low_m, low_o, proj_m, qkv, lse, att_m, att_o, bias, hidden_one, wq, head_dim
    )
    dh1_r = over_core(dh1_o)
    grad_input, sums_one = input_back(dh1_m, dh1_r, x_own, grad_middle, vecs)

    def settle(a):
        mine, other = a[:, :quarter], a[:, quarter : 2 * quarter]
        got = over_x(other.astype(BF16)).astype(a.dtype)
        pair, rest = slice(0, 2), slice(2, 3)
        return jnp.where(
            chip == 0,
            jnp.concatenate([mine[pair], mine[rest], got[rest], got[pair]], axis=0),
            jnp.concatenate([got[pair], got[rest], mine[rest], mine[pair]], axis=0),
        )

    layer_out = settle(layer)
    input_grad = settle(grad_input)

    def over_wide(a, dim=0):
        return lax.psum_scatter(a, "wide", scatter_dimension=dim, tiled=True)

    grad_up = over_wide(grad_up)
    grad_down = over_wide(grad_down)

    def all_experts(a):
        pairs = jnp.stack([a, over_core(a)])
        four = jnp.concatenate([pairs, over_x(pairs)], axis=0)
        return jnp.stack(
            [lax.dynamic_index_in_dim(four, place ^ e, 0, False) for e in range(E)]
        ).astype(F32)

    grad_up = all_experts(grad_up)
    grad_down = all_experts(grad_down)
    proj_wide = lax.dynamic_update_slice_in_dim(
        jnp.zeros((width, width), F32), grad_proj, core * group, 0
    )
    rest = jnp.concatenate(
        [
            grad_qkv,
            proj_wide,
            sums_one[:2].T,
            sums_two[:2].T,
            grad_router[:, :E],
            jnp.zeros((width, 128 - 4 - E), F32),
        ],
        axis=1,
    ).astype(BF16)
    rest = over_wide(rest).astype(F32)
    rest = rest + over_x(rest.astype(BF16)).astype(F32)
    other = over_core(rest.astype(BF16)).astype(F32)
    group_three = 3 * group
    own_q = rest[:, :group_three].reshape(-1, 3, group)
    oth_q = other[:, :group_three].reshape(-1, 3, group)
    grad_qkv = jnp.where(
        core == 0,
        jnp.stack([own_q, oth_q], axis=2),
        jnp.stack([oth_q, own_q], axis=2),
    ).reshape(-1, 3 * width)
    tail = rest[:, group_three:] + other[:, group_three:]
    grad_proj = tail[:, :width]
    small_grad = tail[:, width:]
    return (
        layer_out,
        input_grad,
        small_grad[:, 0],
        small_grad[:, 1],
        grad_qkv,
        grad_proj,
        small_grad[:, 2],
        small_grad[:, 3],
        small_grad[:, 4 : 4 + E],
        grad_up,
        grad_down,
    )


def solution(mesh):
    placed = (
        P("wide", "seq", None),
        P("wide", None),
        P("wide", "seq", None),
        P("wide"),
        P("wide"),
        P("wide", None),
        P("wide", None),
        P("wide"),
        P("wide"),
        P("wide", None),
        P(None, "wide", None),
        P(None, "wide", None),
        P("wide", "seq", None),
    )
    return jax.shard_map(
        shards,
        mesh=mesh,
        in_specs=placed,
        out_specs=(
            P("wide", "seq", None),
            P("wide", "seq", None),
            P("wide"),
            P("wide"),
            P("wide", None),
            P("wide", None),
            P("wide"),
            P("wide"),
            P("wide", None),
            P(None, "wide", None),
            P(None, "wide", None),
        ),
        check_vma=False,
    )
```

```python
import functools
import math

import jax
import jax.numpy as jnp
from jax import lax
from jax.experimental import pallas as pl
from jax.experimental.pallas import tpu as pltpu
from jax.sharding import PartitionSpec as P

H = 8
E = 4
EPSILON = 1e-06
BIG = -1e30
MIB = 1024 * 1024
F32 = jnp.float32
BF16 = jnp.bfloat16


def dot(a, b, dims=((1,), (0,))):
    return lax.dot_general(a, b, (dims, ((), ())), preferred_element_type=F32)


def dot_nt(a, b):
    return dot(a, b, ((1,), (1,)))


def dot_tn(a, b):
    return dot(a, b, ((0,), (0,)))


def norm_parts(values):
    center = values - jnp.mean(values, axis=-1, keepdims=True)
    spread = jnp.mean(center * center, axis=-1, keepdims=True)
    rstd = lax.rsqrt(spread + EPSILON)
    return center * rstd, rstd


def norm_back(grad, xhat, rstd):
    return rstd * (
        grad
        - jnp.mean(grad, axis=-1, keepdims=True)
        - xhat * jnp.mean(grad * xhat, axis=-1, keepdims=True)
    )


TINY = pl.CostEstimate(flops=1000, bytes_accessed=1000, transcendentals=0)


def params(limit, **more):
    return pltpu.CompilerParams(vmem_limit_bytes=limit * MIB, **more)


def placed(*arrays):
    return [
        pltpu.with_memory_space_constraint(a, pltpu.HBM) if a.size > 1 << 15 else a for a in arrays
    ]


def in_hbm(shape, dtype):
    return pltpu.HBM(shape, dtype)


def whole(shape):
    return pl.BlockSpec(shape, lambda *_: (0,) * len(shape))


def per_image(*shape):
    return pl.BlockSpec((1, *shape), lambda i: (i,) + (0,) * len(shape))


SCALARS = pl.BlockSpec(memory_space=pltpu.SMEM)


def attend_kernel(
    images, head_dim, at_ref, own_ref, oth_ref, bias_ref, parts_ref,
    att_m_ref, mail_ref, qkv_ref, hidden_ref, lse_ref, wq_ref, small_ref, vec_ref,
):
    rows = own_ref.shape[1]
    features = wq_ref.shape[0]

    @pl.when(pl.program_id(0) == 0)
    def _():
        part = features // 8
        vec = jnp.zeros((8, features), F32)
        row = lax.broadcasted_iota(jnp.int32, (part, features), 0)
        col = lax.broadcasted_iota(jnp.int32, (part, features), 1)
        for index in range(8):
            base = index * part
            wq_ref[base : base + part, :] = parts_ref[index, :part, : wq_ref.shape[1]]
            there = slice(images * rows + base, images * rows + base + part)
            mail_ref[there, :] = parts_ref[index, :part, wq_ref.shape[1] :]
            spread = (col == row + base).astype(F32).astype(BF16)
            vec = vec + dot(parts_ref[index, part:, :part], spread)[:8]
        vec_ref[...] = vec
        tall = jnp.concatenate([vec, vec[4:], jnp.zeros((116, features), F32)], axis=0)
        small_ref[...] = tall.T.astype(BF16)

    gain, offset = vec_ref[0:1, :], vec_ref[1:2, :]
    for half, ref in enumerate((own_ref, oth_ref)):
        xhat, _ = norm_parts(ref[0].astype(F32))
        hidden_ref[0, half * rows : (half + 1) * rows, :] = (xhat * gain + offset).astype(BF16)
    width = wq_ref.shape[1] // 3
    packed = dot(hidden_ref[0], wq_ref[...]).astype(BF16)
    scaling = 1.0 / math.sqrt(head_dim)
    qkv_ref[0, :, :width] = (packed[:, :width].astype(F32) * scaling).astype(BF16)
    qkv_ref[0, :, width:] = packed[:, width:]
    bias = bias_ref[0]
    lane = lax.broadcasted_iota(jnp.int32, (1, 128), 1)
    sub = lax.broadcasted_iota(jnp.int32, (128, 1), 0)
    for pair in range(width // 128):
        cols = slice(pair * 128, pair * 128 + 128)
        q2 = qkv_ref[0, :, cols]
        k2 = qkv_ref[0, :, width + pair * 128 : width + pair * 128 + 128]
        v2 = qkv_ref[0, :, 2 * width + pair * 128 : 2 * width + pair * 128 + 128]
        v_t = v2.T
        both = []
        for part in range(2):
            mine = (lane >= head_dim * part) & (lane < head_dim * (part + 1))
            qm = jnp.where(mine, q2, jnp.zeros_like(q2))
            scores = dot_nt(k2, qm) + bias
            peak = jnp.max(scores, axis=0, keepdims=True)
            expo = jnp.exp(scores - peak)
            total = jnp.sum(expo, axis=0, keepdims=True)
            lse_ref[0, 2 * pair + part : 2 * pair + part + 1, :] = peak + jnp.log(total)
            both.append(dot(v_t, (expo * (1.0 / total)).astype(BF16)))
        out = jnp.where(sub < head_dim, both[0], both[1]).astype(BF16).T
        att_m_ref[0, :, cols] = out[:rows]
        mail_ref[pl.ds(pl.multiple_of(pl.program_id(0) * rows, 16), rows), cols] = out[rows:]


def attend(at, x_own, x_oth, bias, parts, head_dim):
    images, rows, width = x_own.shape
    group = width // 2
    return pl.pallas_call(
        functools.partial(attend_kernel, images, head_dim),
        grid=(images,),
        in_specs=[
            SCALARS,
            per_image(rows, width),
            per_image(rows, width),
            per_image(2 * rows, 1),
            whole(parts.shape),
        ],
        out_specs=[
            per_image(rows, group),
            whole((images * rows + width, group)),
            per_image(2 * rows, 3 * group),
            per_image(2 * rows, width),
            per_image(8, 2 * rows),
            whole((width, 3 * group)),
            whole((width, 128)),
            whole((8, width)),
        ],
        out_shape=[
            jax.ShapeDtypeStruct((images, rows, group), BF16),
            jax.ShapeDtypeStruct((images * rows + width, group), BF16),
            in_hbm((images, 2 * rows, 3 * group), BF16),
            in_hbm((images, 2 * rows, width), BF16),
            in_hbm((images, 8, 2 * rows), F32),
            in_hbm((width, 3 * group), BF16),
            in_hbm((width, 128), BF16),
            jax.ShapeDtypeStruct((8, width), F32),
        ],
        compiler_params=params(40),
        cost_estimate=TINY,
        name="attend",
    )(*placed(at, x_own, x_oth, bias, parts))


def project_kernel(
    at_ref, att_m_ref, sent_ref, got_ref, x_ref, vec_ref, middle_ref, hidden_ref, proj_ref
):
    rows, group = att_m_ref.shape[1:]
    core, first = at_ref[1], pl.num_programs(0) * rows
    mine = pl.ds(pl.multiple_of(core * group + first, 16), group)
    other = pl.ds(pl.multiple_of((1 - core) * group + first, 16), group)

    def in_order(a, b):
        return jnp.concatenate([jnp.where(core == 0, a, b), jnp.where(core == 0, b, a)], axis=1)

    @pl.when(pl.program_id(0) == 0)
    def _():
        proj_ref[...] = in_order(sent_ref[mine, :], got_ref[mine, :])

    att_r = got_ref[pl.ds(pl.multiple_of(pl.program_id(0) * rows, 16), rows), :]
    halves = [
        dot(att_m_ref[0], ref[mine, :]) + dot(att_r, ref[other, :]) for ref in (sent_ref, got_ref)
    ]
    middle = x_ref[0].astype(F32) + in_order(*halves)
    middle_ref[0] = middle
    xhat, _ = norm_parts(middle)
    hidden_ref[0] = (xhat * vec_ref[2:3, :] + vec_ref[3:4, :]).astype(BF16)


def project(at, att_m, sent, got, x_own, vecs):
    images, rows, width = x_own.shape
    group = att_m.shape[2]
    return pl.pallas_call(
        project_kernel,
        grid=(images,),
        in_specs=[
            SCALARS,
            per_image(rows, group),
            whole(sent.shape),
            whole(got.shape),
            per_image(rows, width),
            whole(vecs.shape),
        ],
        out_specs=[per_image(rows, width), per_image(rows, width), whole((group, width))],
        out_shape=[
            in_hbm(x_own.shape, F32),
            jax.ShapeDtypeStruct(x_own.shape, BF16),
            in_hbm((group, width), BF16),
        ],
        compiler_params=params(24),
        cost_estimate=TINY,
        name="project",
    )(*placed(at, att_m, sent, got, x_own, vecs))


BLOCKS = (
    ((1, 0), (1, 1)),
    ((3, 0), (3, 1)),
    ((1, 2), (0, 2)),
    ((3, 2), (2, 2)),
    ((0, 0), (0, 1)),
    ((2, 0), (2, 1)),
)
EARLY = 4


def load_weights(parts_ref, up_ref, down_ref, sem):
    part = up_ref.shape[0] // 8
    width, units = down_ref.shape[1], up_ref.shape[1] // 8
    copies = []
    for index in range(8):
        base = slice(index * part, index * part + part)
        for block in range(up_ref.shape[1] // width):
            copies.append(
                pltpu.make_async_copy(
                    parts_ref.at[index, block * part : (block + 1) * part, :],
                    up_ref.at[base, block * width : (block + 1) * width],
                    sem.at[0],
                )
            )
        base = slice(index * units, (index + 1) * units)
        first = up_ref.shape[1] // width * part
        copies.append(
            pltpu.make_async_copy(
                parts_ref.at[index, first : first + units, :], down_ref.at[base, :], sem.at[1]
            )
        )
    return copies


def hidden_units(splits, xs, g_ref, up_ref, down_ref, act_ref, gp_ref):
    ff = up_ref.shape[1]
    chunk = ff // splits
    ret = dx = None
    for part in range(splits):
        cols = slice(part * chunk, (part + 1) * chunk)
        pre = dot(xs, up_ref[:, cols])
        back = dot_nt(g_ref[...], down_ref[cols, :])
        cdf = 0.5 + 0.5 * lax.erf(pre * math.sqrt(0.5))
        pdf = jnp.exp(-0.5 * pre * pre) * (1.0 / math.sqrt(2.0 * math.pi))
        act = (pre * cdf).astype(BF16)
        gp = (back * (cdf + pre * pdf)).astype(BF16)
        act_ref[:, cols] = act
        gp_ref[:, cols] = gp
        ret_part = dot(act, down_ref[cols, :])
        dx_part = dot_nt(gp, up_ref[:, cols])
        ret = ret_part if ret is None else ret + ret_part
        dx = dx_part if dx is None else dx + dx_part
    return ret, dx


def routing(xs, wr_ref, mine):
    logits = dot(xs, wr_ref[...])
    lane = lax.broadcasted_iota(jnp.int32, (1, 128), 1)
    logits = jnp.where((lane >= 4) & (lane < 4 + 2 * E), logits, BIG)
    grown = jnp.exp(logits - jnp.max(logits, axis=-1, keepdims=True))
    once = lane < 4 + E
    router = grown / jnp.sum(jnp.where(once, grown, 0.0), axis=-1, keepdims=True)
    sel = jnp.where((lane == 4 + mine) | (lane == 4 + E + mine), 1.0, 0.0)
    return router, sel, jnp.sum(jnp.where(once, router * sel, 0.0), axis=-1, keepdims=True)


def two_parts(values):
    high = values.astype(BF16)
    return high, (values - high.astype(F32)).astype(BF16)


def expert_first_kernel(
    splits, filled, at_ref, h0, h1, h2, h3, cm, co, wr_ref, parts_ref,
    pos_ref, xs_ref, cs_ref, g_ref, act_ref, gp_ref, ret_ref, dx_ref,
    up_ref, down_ref, sem, piece_ref, piece_sem,
):
    step = pl.program_id(0)
    rows = h0.shape[1]
    hs, cs = (h0, h1, h2, h3), (cm.at[0], cm.at[1], co.at[0], co.at[1])
    mine = at_ref[2]

    def pieces_of(number):
        copies = []
        for k, (piece, image) in enumerate(BLOCKS[number]):
            for j, kind in enumerate((hs, cs)):
                spot = number * 4 + 2 * k + j
                copies.append(
                    pltpu.make_async_copy(
                        kind[piece].at[image], piece_ref.at[spot], piece_sem.at[number]
                    )
                )
        return copies

    def copies():
        return load_weights(parts_ref, up_ref, down_ref, sem)

    @pl.when(step == 0)
    def _():
        for number in range(len(BLOCKS)):
            for copy in pieces_of(number):
                copy.start()
            if number == 0:
                for copy in copies():
                    copy.start()

    token = lax.broadcasted_iota(jnp.int32, (1, rows), 1)
    slot = lax.broadcasted_iota(jnp.int32, (rows, rows), 0)
    before = (slot < lax.broadcasted_iota(jnp.int32, (rows, rows), 1)).astype(F32).astype(BF16)
    for number, block in enumerate(BLOCKS):

        @pl.when(step == number)
        def _(number=number, block=block):
            for copy in pieces_of(number):
                copy.wait()
            base, xs, got = 0.0, None, None
            for k in range(2):
                spot = number * 4 + 2 * k
                code = piece_ref[spot + 1, filled // 16 * 16 : filled // 16 * 16 + 16, :rows]
                code = code.astype(F32)[filled % 16 : filled % 16 + 1, :]
                first = jnp.floor(code * (1.0 / E))
                second = code - E * first
                own = mine.astype(F32)
                named = ((first == own) | (second == own)) & (token < filled)
                flag = jnp.where(named, 1.0, 0.0)
                rank = dot(jnp.broadcast_to(flag, (16, rows)).astype(BF16), before)[0:1, :] + base
                rank = jnp.where(named, rank, -1.0)
                base = base + jnp.sum(flag, axis=-1, keepdims=True)
                pos_ref[k : k + 1, :] = rank
                pick = (slot.astype(F32) == rank).astype(F32).astype(BF16)
                a, b = dot(pick, piece_ref[spot]), dot(pick, piece_ref[spot + 1])
                xs, got = (a, b) if xs is None else (xs + a, got + b)
            xs_ref[...] = xs.astype(BF16)
            cs_ref[...] = got.astype(BF16)

    xs = xs_ref[...]
    _, _, weight = routing(xs, wr_ref, mine)
    g_ref[...] = (cs_ref[...].astype(F32) * weight).astype(BF16)

    @pl.when(step == 0)
    def _():
        for copy in copies():
            copy.wait()

    ret, dx = hidden_units(splits, xs, g_ref, up_ref, down_ref, act_ref, gp_ref)
    ret_ref[...] = ret.astype(BF16)
    dx_ref[...] = dx.astype(BF16)


def slot_block(rows, cols, first=0):
    return pl.BlockSpec((rows, cols), lambda i: (i + first, 0))


def expert_first(at, hidden, cots_m, cots_o, wr, parts, filled):
    images, rows, width = hidden[0].shape
    ff = (parts.shape[1] - 2 * width // 8) * 8
    count = len(BLOCKS)
    outs = [
        (8, rows, F32),
        (rows, width, BF16),
        (rows, width, BF16),
        (rows, width, BF16),
        (rows, ff, BF16),
        (rows, ff, BF16),
        (rows, width, BF16),
        (rows, width, BF16),
    ]
    return pl.pallas_call(
        functools.partial(expert_first_kernel, 2, filled),
        grid=(count,),
        in_specs=[
            SCALARS,
            *[pl.BlockSpec(memory_space=pl.ANY)] * 6,
            whole(wr.shape),
            pl.BlockSpec(memory_space=pl.ANY),
        ],
        out_specs=[slot_block(a, b) for a, b, _ in outs],
        out_shape=[in_hbm((count * a, b), kind) for a, b, kind in outs],
        scratch_shapes=[
            pltpu.VMEM((width, ff), BF16),
            pltpu.VMEM((ff, width), BF16),
            pltpu.SemaphoreType.DMA((2,)),
            pltpu.VMEM((4 * count, rows, width), BF16),
            pltpu.SemaphoreType.DMA((count,)),
        ],
        compiler_params=params(30),
        cost_estimate=TINY,
        name="expert_first",
    )(*placed(at, *hidden, cots_m, cots_o, wr, parts))


def expert_second_kernel(
    splits, step_count, at_ref, pos_ref, xs_ref, cs_ref, g_ref, ret0_ref, dx0_ref, wr_ref,
    parts_ref, *refs,
):
    step = pl.program_id(0)
    rows = xs_ref.shape[0]
    *refs, up_ref, down_ref, sem = refs
    early = step_count == EARLY
    if early:
        act_ref, gp_ref, lg_ref, dh_m, dh_o, ret_m, ret_o, extra_m, extra_o = refs
        firsts = [((dh_m, ret_m), 0), ((dh_o, ret_o), 0)]
        targets = [[(dh, 0, back, 0), (dh, 1, back, 1)] for (dh, back), _ in firsts]
        targets += [
            [(dh, 2, back, 2), (extra, 0, extra, 1)]
            for ((dh, back), _), extra in zip(firsts, (extra_m, extra_o))
        ]
    else:
        extra_m, extra_o, act_ref, gp_ref, lg_ref, dh_m, dh_o, ret_m, ret_o = refs
        targets = [[(a, 0, b, 0), (a, 1, b, 1)] for a, b in ((dh_m, ret_m), (dh_o, ret_o))]

        @pl.when(step == 0)
        def _():
            for extra, dh, back in ((extra_m, dh_m, ret_m), (extra_o, dh_o, ret_o)):
                dh[2] = extra[0]
                back[2] = extra[1]


    @pl.when(step == 0)
    def _():
        copies = load_weights(parts_ref, up_ref, down_ref, sem)
        for copy in copies:
            copy.start()
        for copy in copies:
            copy.wait()

    ret, dx = hidden_units(splits, xs_ref[...], g_ref, up_ref, down_ref, act_ref, gp_ref)
    ret = ret + ret0_ref[...].astype(F32)
    router, sel, weight = routing(xs_ref[...], wr_ref, at_ref[2])
    gate = jnp.sum(cs_ref[...].astype(F32) * ret, axis=-1, keepdims=True)
    high, low = two_parts(gate * weight * (sel - router))
    lg = jnp.where(lax.broadcasted_iota(jnp.int32, (1, 128), 1) < 4 + E, high, low)
    lg_ref[...] = lg
    dxb = (dx + dx0_ref[...].astype(F32) + dot_nt(lg, wr_ref[...])).astype(BF16)
    retb = (ret * weight).astype(BF16)
    slot = lax.broadcasted_iota(jnp.int32, (rows, rows), 0).astype(F32)
    picks = [(slot == pos_ref[k : k + 1, :]).astype(F32).astype(BF16) for k in range(2)]
    for number, target in enumerate(targets):

        @pl.when(step == number)
        def _(target=target):
            for pick, (dh, i, back, j) in zip(picks, target):
                dh[i] = dot_tn(pick, dxb).astype(BF16)
                back[j] = dot_tn(pick, retb).astype(BF16)


def expert_second(at, first, wr, parts, start, count, extras=()):
    pos, xs, cs, g, _, _, ret, dx = first
    rows, width = xs.shape[0] // len(BLOCKS), xs.shape[1]
    ff = (parts.shape[1] - 2 * width // 8) * 8
    sizes = (3, 3, 3, 3) if extras else (3, 3, 3, 3, 2, 2)
    return pl.pallas_call(
        functools.partial(expert_second_kernel, 2, count),
        grid=(count,),
        in_specs=[
            SCALARS,
            slot_block(8, rows, start),
            slot_block(rows, width, start),
            slot_block(rows, width, start),
            slot_block(rows, width, start),
            slot_block(rows, width, start),
            slot_block(rows, width, start),
            whole(wr.shape),
            pl.BlockSpec(memory_space=pl.ANY),
            *[whole(e.shape) for e in extras],
        ],
        out_specs=[slot_block(rows, ff), slot_block(rows, ff), slot_block(rows, 128)]
        + [whole((n, rows, width)) for n in sizes],
        out_shape=[
            in_hbm((count * rows, ff), BF16),
            in_hbm((count * rows, ff), BF16),
            in_hbm((count * rows, 128), BF16),
        ]
        + [jax.ShapeDtypeStruct((n, rows, width), BF16) for n in sizes],
        scratch_shapes=[
            pltpu.VMEM((width, ff), BF16),
            pltpu.VMEM((ff, width), BF16),
            pltpu.SemaphoreType.DMA((2,)),
        ],
        compiler_params=params(30),
        cost_estimate=TINY,
        name="expert_second",
    )(*placed(at, pos, xs, cs, g, ret, dx, wr, parts, *extras))


def weight_grad_kernel(ends, *refs):
    count = len(ends)
    _, xs_ref, g_ref = refs[:3]
    lgs, gps, acts = refs[3 : 3 + count], refs[3 + count : 3 + 2 * count], refs[3 + 2 * count : 3 + 3 * count]
    out_ref, router_ref, xs_t, g_t, turned = refs[3 + 3 * count :]
    step = pl.program_id(0)
    width = xs_t.shape[0]
    part, cols = width // 8, gps[0].shape[1]
    spans = list(zip((0, *ends[:-1]), ends))

    @pl.when(step == 0)
    def _():
        xs_t[...] = xs_ref[...].T
        g_t[...] = g_ref[...].T
        total = None
        for (low, high), lg in zip(spans, lgs):
            one = dot(xs_t[:, low:high], lg[...])
            total = one if total is None else total + one
        router_ref[...] = total

    up = down = None
    for (low, high), gp, act in zip(spans, gps, acts):
        one, two = dot(xs_t[:, low:high], gp[...]), dot(g_t[:, low:high], act[...])
        up, down = (one, two) if up is None else (up + one, down + two)
    turned[:width, :] = up.astype(BF16)
    block = step * cols // width
    lanes = pl.ds(pl.multiple_of(step * cols % width, cols), cols)
    into = pl.ds(pl.multiple_of(block * part, part), part)
    for index in range(8):
        out_ref[index, into, lanes] = turned[index * part : (index + 1) * part, :]
    half = cols // 2
    first = out_ref.shape[1] - half
    tall = down.T.astype(BF16)
    out_ref[2 * step, first:, :] = tall[:half]
    out_ref[2 * step + 1, first:, :] = tall[half:]


def weight_grad(at, xs, g, lgs, gps, acts):
    slots, width = xs.shape
    ff = gps[0].shape[1]
    cols = ff // 4
    out = (8, ff // width * (width // 8) + ff // 8, width)
    ends = []
    for gp in gps:
        ends.append(gp.shape[0] + (ends[-1] if ends else 0))
    return pl.pallas_call(
        functools.partial(weight_grad_kernel, tuple(ends)),
        grid=(4,),
        in_specs=[SCALARS, whole(xs.shape), whole(g.shape)]
        + [whole(a.shape) for a in lgs]
        + [pl.BlockSpec((a.shape[0], cols), lambda i: (0, i)) for a in (*gps, *acts)],
        out_specs=[whole(out), whole((width, 128))],
        out_shape=[jax.ShapeDtypeStruct(out, BF16), in_hbm((width, 128), F32)],
        scratch_shapes=[
            pltpu.VMEM((width, slots), BF16),
            pltpu.VMEM((width, slots), BF16),
            pltpu.VMEM((width, cols), BF16),
        ],
        compiler_params=params(30),
        cost_estimate=TINY,
        name="weight_grad",
    )(*placed(at, xs, g, *lgs, *gps, *acts))


def settle_kernel(at_ref, zero_ref, one_ref, up_ref, down_ref):
    part, units = up_ref.shape[1], zero_ref.shape[1] - 2 * up_ref.shape[1]
    for half, ref in enumerate((zero_ref, one_ref)):
        for index in range(8):
            rows = slice(index // 4 * part, index // 4 * part + part)
            to = (2 * index + half) * units
            from_ = index % 4 * units
            up_ref[0, :, to : to + units] = ref[0, rows, from_ : from_ + units].astype(F32)
        down_ref[0, half * units : (half + 1) * units, :] = ref[0, 2 * part :, :].astype(F32)


def settle_experts(at, zero, one):
    _, rows, width = zero.shape
    part = width // 8
    units = rows - 2 * part
    piece = pl.BlockSpec((1, rows, width), lambda i, at: (i ^ at[2], 0, 0))
    return pl.pallas_call(
        settle_kernel,
        grid_spec=pltpu.PrefetchScalarGridSpec(
            num_scalar_prefetch=1,
            grid=(E,),
            in_specs=[piece, piece],
            out_specs=[
                pl.BlockSpec((1, part, 16 * units), lambda i, at: (i, 0, 0)),
                pl.BlockSpec((1, 2 * units, width), lambda i, at: (i, 0, 0)),
            ],
        ),
        out_shape=[
            jax.ShapeDtypeStruct((E, part, 16 * units), F32),
            jax.ShapeDtypeStruct((E, 2 * units, width), F32),
        ],
        compiler_params=params(24),
        cost_estimate=TINY,
        name="settle_experts",
    )(*placed(at, zero, one))


def middle_back_kernel(
    filled, at_ref, a_ref, ar_ref, xr_ref, mid_ref, cot_ref, vec_ref, am_ref,
    got_ref, r0_ref, r1_ref,
    gm_ref, low_ref, send_ref, keep_ref, sums_ref, proj_ref,
):
    rows, width = mid_ref.shape[1:]
    group = am_ref.shape[2]

    @pl.when(pl.program_id(0) == 0)
    def _():
        sums_ref[...] = jnp.zeros_like(sums_ref)
        proj_ref[...] = jnp.zeros_like(proj_ref)

    grad = a_ref[0].astype(F32) + ar_ref[0].astype(F32) + xr_ref[0].astype(F32)
    xhat, rstd = norm_parts(mid_ref[0])
    sums_ref[2:3, :] += jnp.sum(grad * xhat, axis=0, keepdims=True)
    sums_ref[3:4, :] += jnp.sum(grad, axis=0, keepdims=True)
    out = cot_ref[0, 0].astype(F32) + norm_back(grad * vec_ref[2:3, :], xhat, rstd)
    row = lax.broadcasted_iota(jnp.int32, (rows, 1), 0)
    out = jnp.where(row < filled, out, 0.0)
    gm_ref[0] = out
    low = out.astype(BF16)
    low_ref[0] = low
    proj_ref[:group, :] += dot_tn(am_ref[0], low)
    att_r = got_ref[pl.ds(pl.multiple_of(pl.program_id(0) * rows, 16), rows), :]
    proj_ref[group:, :] += dot_tn(att_r, low)

    @pl.when(pl.program_id(0) == pl.num_programs(0) - 1)
    def _():
        part = width // 8
        router = (r0_ref[...] + r1_ref[...]).T
        router = jnp.concatenate([jnp.zeros((4, width), F32), router[4:8] + router[8:12]], axis=0)
        lines = jnp.concatenate(two_parts(sums_ref[...] + router), axis=0)
        row = lax.broadcasted_iota(jnp.int32, (width, 128), 0)
        col = lax.broadcasted_iota(jnp.int32, (width, 128), 1)
        for ref, side in ((send_ref, 1 - at_ref[3]), (keep_ref, at_ref[3])):
            for z in range(4):
                base = (2 * z + side) * part
                from_ = pl.multiple_of(base ^ (at_ref[1] * group), part)
                ref[z, :part, :] = proj_ref[pl.ds(from_, part), :].astype(BF16)
                pick = ((row == col + base) & (col < part)).astype(F32).astype(BF16)
                ref[z, part:, :128] = dot(lines, pick).astype(BF16)
                ref[z, part:, 128:] = jnp.zeros((16, width - 128), BF16)


def middle_back(at, mine, near, from_x, middle, cots, vecs, att_m, got, routers, filled):
    images, rows, width = middle.shape
    one = per_image(rows, width)
    cot = pl.BlockSpec((1, 1, rows, width), lambda i: (0, i, 0, 0))
    group = att_m.shape[2]
    piece = (4, width // 8 + 16, width)
    return pl.pallas_call(
        functools.partial(middle_back_kernel, filled),
        grid=(images,),
        in_specs=[SCALARS]
        + [one] * 4
        + [cot, whole(vecs.shape), per_image(rows, group), whole(got.shape)]
        + [whole(routers[0].shape)] * 2,
        out_specs=[one, one, whole(piece), whole(piece)],
        out_shape=[
            in_hbm(middle.shape, F32),
            jax.ShapeDtypeStruct(middle.shape, BF16),
            in_hbm(piece, BF16),
            in_hbm(piece, BF16),
        ],
        scratch_shapes=[
            pltpu.VMEM((8, width), F32),
            pltpu.VMEM((width, width), F32),
        ],
        compiler_params=params(32),
        cost_estimate=TINY,
        name="middle_back",
    )(*placed(at, mine, near, from_x, middle, cots, vecs, att_m, got, *routers))


def layer_kernel(mid_ref, a_ref, ar_ref, xr_ref, mine_ref, send_ref):
    total = mid_ref[0] + a_ref[0].astype(F32) + ar_ref[0].astype(F32) + xr_ref[0].astype(F32)
    count = mine_ref.shape[1]
    mine_ref[0] = total[:count].astype(BF16)
    send_ref[0] = total[count : 2 * count].astype(BF16)


def layer_sum(middle, mine, near, from_x, quarter):
    images, rows, width = middle.shape
    one, part = per_image(rows, width), per_image(quarter, width)
    return pl.pallas_call(
        layer_kernel,
        grid=(images,),
        in_specs=[one] * 4,
        out_specs=[part, part],
        out_shape=[jax.ShapeDtypeStruct((images, quarter, width), BF16)] * 2,
        compiler_params=params(24),
        cost_estimate=TINY,
        name="layer_sum",
    )(*placed(middle, mine, near, from_x))


def attend_back_kernel(
    head_dim, at_ref, lm_ref, lo_ref, pm_ref, qkv_ref, lse_ref, bias_ref, h1_ref, wq_ref,
    dm_ref, do_ref, gq_ref, grad_ref, low_ref,
):
    rows = lm_ref.shape[1]
    low_ref[:rows, :] = lm_ref[0]
    low_ref[rows:, :] = lo_ref[0]
    out_grad = dot_nt(low_ref[...], pm_ref[...]).astype(BF16)
    width = pm_ref.shape[0]
    bias = bias_ref[0]
    lane = lax.broadcasted_iota(jnp.int32, (1, 128), 1)
    sub = lax.broadcasted_iota(jnp.int32, (128, 1), 0)
    scaling = 1.0 / math.sqrt(head_dim)
    for pair in range(width // 128):
        cols = slice(pair * 128, pair * 128 + 128)
        k_cols = slice(width + pair * 128, width + pair * 128 + 128)
        v_cols = slice(2 * width + pair * 128, 2 * width + pair * 128 + 128)
        q2, k2, v2 = qkv_ref[0, :, cols], qkv_ref[0, :, k_cols], qkv_ref[0, :, v_cols]
        o2 = out_grad[:, cols]
        k_t = k2.T
        dv = dk = None
        both = []
        for part in range(2):
            mine = (lane >= head_dim * part) & (lane < head_dim * (part + 1))
            qm = jnp.where(mine, q2, jnp.zeros_like(q2))
            om = jnp.where(mine, o2, jnp.zeros_like(o2))
            head = 2 * pair + part
            probs = jnp.exp(dot_nt(k2, qm) + bias - lse_ref[0, head : head + 1, :])
            prob_grad = dot_nt(v2, om)
            delta = jnp.sum(probs * prob_grad, axis=0, keepdims=True)
            score_grad = (probs * (prob_grad - delta)).astype(BF16)
            dv_part = dot(probs.astype(BF16), om)
            dk_part = dot(score_grad, qm)
            dv = dv_part if dv is None else dv + dv_part
            dk = dk_part if dk is None else dk + dk_part
            both.append(dot(k_t, score_grad))
        dq = (jnp.where(sub < head_dim, both[0], both[1]) * scaling).astype(BF16).T
        grad_ref[:, cols] = dq
        grad_ref[:, k_cols] = dk.astype(BF16)
        grad_ref[:, v_cols] = dv.astype(BF16)
    hidden_grad = dot_nt(grad_ref[...], wq_ref[...]).astype(BF16)
    dm_ref[0] = hidden_grad[:rows]
    do_ref[0] = hidden_grad[rows:]
    grad_qkv = dot_tn(h1_ref[0], grad_ref[...])

    @pl.when(pl.program_id(0) == 0)
    def _():
        gq_ref[...] = grad_qkv

    @pl.when(pl.program_id(0) > 0)
    def _():
        gq_ref[...] += grad_qkv


def attend_back(at, low_m, low_o, proj_m, qkv, lse, bias, hidden_one, wq, head_dim):
    images, rows, width = low_m.shape
    group = proj_m.shape[0]
    return pl.pallas_call(
        functools.partial(attend_back_kernel, head_dim),
        grid=(images,),
        in_specs=[
            SCALARS,
            per_image(rows, width),
            per_image(rows, width),
            whole(proj_m.shape),
            per_image(2 * rows, 3 * group),
            per_image(8, 2 * rows),
            per_image(2 * rows, 1),
            per_image(2 * rows, width),
            whole(wq.shape),
        ],
        out_specs=[
            per_image(rows, width),
            per_image(rows, width),
            whole((width, 3 * group)),
        ],
        out_shape=[
            in_hbm((images, rows, width), BF16),
            jax.ShapeDtypeStruct((images, rows, width), BF16),
            in_hbm((width, 3 * group), F32),
        ],
        scratch_shapes=[
            pltpu.VMEM((2 * rows, 3 * group), BF16),
            pltpu.VMEM((2 * rows, width), BF16),
        ],
        compiler_params=params(48),
        cost_estimate=TINY,
        name="attend_back",
    )(*placed(at, low_m, low_o, proj_m, qkv, lse, bias, hidden_one, wq))


def input_back_kernel(
    at_ref, x_ref, gm_ref, vec_ref, a_ref, ar_ref, gq_ref, r_send_ref, r_keep_ref,
    out_ref, go_ref, send_ref, keep_ref, sums_ref,
):
    step, images = pl.program_id(0), pl.num_programs(0)
    grad = a_ref[0].astype(F32) + ar_ref[0].astype(F32)
    xhat, rstd = norm_parts(x_ref[0].astype(F32))
    out = gm_ref[0] + norm_back(grad * vec_ref[0:1, :], xhat, rstd)
    count = out_ref.shape[1]
    out_ref[0] = out[:count]
    go_ref[0] = out[count : 2 * count].astype(BF16)

    @pl.when(step == 0)
    def _():
        sums_ref[...] = jnp.zeros_like(sums_ref)

    sums_ref[0:1, :] += jnp.sum(grad * xhat, axis=0, keepdims=True)
    sums_ref[1:2, :] += jnp.sum(grad, axis=0, keepdims=True)

    @pl.when(step == images - 1)
    def _():
        total = gq_ref[...]
        width = grad.shape[1]
        part = width // 8
        lines = jnp.concatenate(two_parts(sums_ref[...]), axis=0)
        row = lax.broadcasted_iota(jnp.int32, (width, 128), 0)
        col = lax.broadcasted_iota(jnp.int32, (width, 128), 1)
        for index in range(8):
            base = index * part
            own = total[base : base + part].astype(BF16)
            half = jnp.concatenate([own[: part // 2, width:], own[part // 2 :, width:]], axis=1)
            pick_line = ((row == col + base) & (col < part)).astype(F32).astype(BF16)
            line = dot(lines, pick_line).astype(BF16)
            tail = jnp.concatenate([line, jnp.zeros((16, width - 128), BF16)], axis=1)
            block = jnp.concatenate([own[:, :width], half], axis=0)
            last = part + block.shape[0]

            def put(ref, block=block, tail=tail, z=index // 2, last=last):
                ref[z, part:last] = block
                ref[z, last + 16 :] = tail

            @pl.when(at_ref[3] == index % 2)
            def _(put=put):
                put(keep_ref)

            @pl.when(at_ref[3] != index % 2)
            def _(put=put):
                put(send_ref)

        last = send_ref.shape[1] - 32
        for ref, from_ in ((send_ref, r_send_ref), (keep_ref, r_keep_ref)):
            ref[:, :part] = from_[:, :part]
            ref[:, last : last + 16] = from_[:, part:]


def input_back(at, x_own, grad_middle, vecs, mine, near, grads, r_parts, quarter):
    images, rows, width = x_own.shape
    one, part = per_image(rows, width), per_image(quarter, width)
    first = r_parts[0].shape[1]
    more = (4, first + width // 8 + (grads.shape[1] - width) * (width // 8) // width + 16, width)
    return pl.pallas_call(
        input_back_kernel,
        grid=(images,),
        in_specs=[SCALARS, one, one, whole(vecs.shape), one, one, whole(grads.shape)]
        + [whole(r.shape) for r in r_parts],
        out_specs=[part, part, whole(more), whole(more)],
        out_shape=[
            jax.ShapeDtypeStruct((images, quarter, width), F32),
            jax.ShapeDtypeStruct((images, quarter, width), BF16),
            jax.ShapeDtypeStruct(more, BF16),
            jax.ShapeDtypeStruct(more, BF16),
        ],
        scratch_shapes=[pltpu.VMEM((8, width), F32)],
        compiler_params=params(32),
        cost_estimate=TINY,
        name="input_back",
    )(*placed(at, x_own, grad_middle, vecs, mine, near, grads, *r_parts))


def shards(
    tokens,
    key_mask,
    expert_ids,
    ln1_gain,
    ln1_bias,
    qkv_weight,
    proj_weight,
    ln2_gain,
    ln2_bias,
    router_weight,
    up_weight,
    down_weight,
    cotangent,
):
    n_seq, n_wide = lax.axis_size("seq"), lax.axis_size("wide")
    images, quarter, width = tokens.shape
    head_dim = width // H
    group = width // 2
    filled = 2 * quarter
    rows = -(-(filled + 1) // 16) * 16
    place = lax.axis_index("seq")
    chip, core = place // 2, place % 2
    direct = n_wide == 8
    spot = lax.axis_index("wide") if direct else 0
    at = jnp.stack([jnp.int32(spot), core, place, jnp.int32(spot) % 2])
    part = width // 8

    def over_seq(a, turn):
        return lax.ppermute(a, "seq", [(i, i ^ turn) for i in range(n_seq)])

    def over_x(a):
        return over_seq(a, 2)

    def over_core(a):
        return over_seq(a, 1)

    def over_wide(a, turn):
        return lax.ppermute(a, "wide", [(i, i ^ turn) for i in range(n_wide)])

    def after(value, *first):
        return lax.optimization_barrier((value, *first))[0]

    def images_of(a, of_chip):
        pair = lax.dynamic_slice_in_dim(a, of_chip * (images - 2), 2, 0)
        single = lax.dynamic_slice_in_dim(a, images // 2 - 1 + of_chip, 1, 0)
        return jnp.concatenate([pair, single], axis=0)

    def joined(first, second):
        both = jnp.concatenate([first, second], axis=1)
        return jnp.pad(both, ((0, 0), (0, rows - filled)) + ((0, 0),) * (both.ndim - 2))

    def cells(quarters, of_chip, of_core):
        first = lax.dynamic_index_in_dim(quarters, 2 * of_chip + of_core, 1, False)
        second = lax.dynamic_index_in_dim(quarters, 2 * (1 - of_chip) + of_core, 1, False)
        return joined(images_of(first, of_chip), images_of(second, of_chip))

    mask = key_mask.reshape(images, n_seq, quarter)
    valid = jnp.concatenate([cells(mask, chip, core), cells(mask, chip, 1 - core)], axis=1)
    bias = jnp.where(valid > 0, 0.0, BIG).astype(F32)[..., None]

    def heads_of(a):
        return jnp.concatenate(
            [lax.dynamic_slice_in_dim(a, (2 * i + core) * group, group, 1) for i in range(3)],
            axis=1,
        )

    wq = heads_of(qkv_weight)
    proj = lax.dynamic_slice_in_dim(proj_weight, core * group, group, 1)
    lines = jnp.stack([ln1_gain, ln1_bias, ln2_gain, ln2_bias])
    lines = jnp.concatenate([lines, router_weight.T], axis=0)
    up = lax.dynamic_index_in_dim(up_weight, place, 0, False)
    down = lax.dynamic_index_in_dim(down_weight, place, 0, False)
    units = down.shape[0] // 2

    def first_parts(wq, proj, lines):
        both = jnp.concatenate([wq, proj], axis=1)
        fill = ((0, 16 - lines.shape[0]), (0, both.shape[1] - lines.shape[1]))
        return jnp.concatenate([both, jnp.pad(lines, fill)], axis=0)

    def half_of(up, down, half):
        cols = up.reshape(up.shape[0], n_wide, 2, units)[:, :, half].reshape(up.shape[0], -1)
        down = down.reshape(-1, 2, units, width)[:, half].reshape(-1, width)
        blocks = [cols[:, i : i + width] for i in range(0, cols.shape[1], width)]
        return jnp.concatenate([*blocks, down], axis=0)

    one_all = first_parts(wq, proj, lines)
    one_all = jnp.broadcast_to(one_all[None], (8, *one_all.shape))
    codes = (expert_ids[..., 0] * E + expert_ids[..., 1]).astype(BF16)
    codes = jnp.pad(codes, ((0, 0), (0, width - quarter)))[:, None, :]
    cot = jnp.concatenate([cotangent, codes], axis=1)
    x_got = over_x(images_of(after(tokens, one_all), 1 - chip))
    x_own = joined(images_of(tokens, chip), x_got)
    x_oth = over_core(after(x_own, bias, cot))
    cot_got = over_x(after(cot, x_got))

    def cot_of(first, second):
        code = jnp.concatenate(
            [first[:, quarter:, :quarter], second[:, quarter:, :quarter]], axis=2
        )
        code = jnp.pad(code, ((0, 0), (0, rows - filled - 1), (0, width - filled)))
        return jnp.concatenate([first[:, :quarter], second[:, :quarter], code], axis=1)

    z_groups = [[y + 2 * z for z in range(4)] for y in range(2)]

    def all_of(a, axis=0):
        return lax.all_gather(a, "wide", axis=axis, tiled=True)

    if direct:
        ones = lax.all_to_all(one_all, "wide", 0, 0, tiled=True)
        twos, threes = (
            lax.all_gather(after(half_of(up, down, half), ones, x_oth), "wide") for half in range(2)
        )
    else:

        def eight(a, axis=0):
            return jnp.split(a, 8, axis=axis)

        ones = jnp.stack([first_parts(*a) for a in zip(eight(all_of(wq)), eight(all_of(proj)), eight(all_of(lines, 1), 1))])
        ups, downs = eight(all_of(up)), eight(all_of(down))
        twos, threes = (
            jnp.stack([half_of(a, b, half) for a, b in zip(ups, downs)]) for half in range(2)
        )

    att_m, mail, qkv, hidden_one, lse, wq, small, vecs = attend(
        at, x_own, x_oth, bias, ones, head_dim
    )
    mail_got = over_core(mail)
    middle, hidden_two, proj_m = project(at, att_m, mail, mail_got, x_own, vecs)
    cot_got = after(cot_got, hidden_two)
    cots_m = jnp.stack(
        [
            cot_of(images_of(cot, chip), images_of(cot_got, chip)),
            cot_of(images_of(cot_got, 1 - chip), images_of(cot, 1 - chip)),
        ]
    )
    cots_o = over_core(cots_m)
    hidden_b = over_x(hidden_two)
    hidden = (hidden_two, hidden_b, over_core(hidden_two), over_core(hidden_b))
    first = expert_first(at, hidden, cots_m, cots_o, small, twos, filled)
    _, xs, _, g_slots, act0, gp0, _, _ = first
    no_lg = jnp.zeros((xs.shape[0], 128), BF16)
    parts0, router0 = weight_grad(at, xs, g_slots, [no_lg], [gp0], [act0])
    act1, gp1, lg1, dh_m, dh_o, ret_m, ret_o, *extras = expert_second(
        after(at, parts0), first, small, threes, 0, EARLY
    )
    dh_r = over_core(dh_o)
    dh_b = dh_m + dh_r
    dh_x = over_x(dh_b)
    ret_r = over_core(ret_o)
    def over_y(send, keep, *first):
        if not direct:
            return jnp.stack([keep, send], axis=1)
        got = over_wide(send, 1)
        return after(keep, *first) + after(got, *first)

    def over_z(both):
        return lax.all_to_all(both, "wide", 0, 0, axis_index_groups=z_groups, tiled=True)

    def expert_sum(both):
        both = both.reshape(8, -1, width)
        cut = 2 * part
        cols = jnp.moveaxis(both[:, :cut].reshape(8, 2, part, width), 1, 2).reshape(width, -1)
        rows = both[:, cut:].reshape(-1, width)
        return tuple(
            lax.psum_scatter(a, "wide", scatter_dimension=0, tiled=True) for a in (cols, rows)
        )

    def near_pair(a):
        return jnp.stack([a, over_core(a)])

    def near_experts(pairs):
        return jnp.concatenate([pairs, over_x(pairs)], axis=0)

    act2, gp2, lg2, late_m, late_o, late_ret_m, late_ret_o = expert_second(
        after(at, dh_b), first, small, threes, EARLY, len(BLOCKS) - EARLY, extras
    )
    late_r = over_core(late_o)
    late_ret_r = over_core(late_ret_o)
    if direct:
        sum0 = lax.all_to_all(parts0, "wide", 0, 0, tiled=True)
    ret_b = after(ret_m, act2) + ret_r
    parts1, router1 = weight_grad(
        after(at, ret_b), xs, g_slots, [lg1, lg2], [gp1, gp2], [act1, act2]
    )
    ret_x = over_x(after(ret_b, dh_x))

    grad_middle, low_m, *r_parts = middle_back(
        at,
        late_m,
        late_r,
        dh_x,
        middle,
        cots_m,
        vecs,
        att_m,
        mail_got,
        (router0, router1),
        filled,
    )
    low_o = over_core(low_m)
    hold = after(at, ret_x)
    if direct:
        sum1 = lax.all_to_all(after(parts1, dh_x, ret_b), "wide", 0, 0, tiled=True)
        sum0 = jnp.sum(after(sum0, low_m).astype(F32), axis=0).astype(BF16)
        pair0 = near_pair(sum0)
        near0 = near_experts(pair0)
        hold = after(hold, pair0)
    layer_mine, layer_send = layer_sum(middle, late_ret_m, late_ret_r, ret_x, quarter)
    layer_got = over_x(layer_send)
    dh1_m, dh1_o, grad_qkv = attend_back(
        after(hold, layer_send), low_m, low_o, proj_m, qkv, lse, bias, hidden_one, wq, head_dim
    )
    dh1_o = after(dh1_o, layer_got)
    if direct:
        dh1_o = after(dh1_o, near0)
    dh1_r = over_core(dh1_o)
    input_mine, input_send, q_send, q_keep = input_back(
        at, x_own, grad_middle, vecs, dh1_m, dh1_r, grad_qkv, r_parts, quarter
    )
    input_got = over_x(input_send)
    if direct:
        sum1 = jnp.sum(after(sum1, q_send).astype(F32), axis=0).astype(BF16)
        pair1 = near_pair(sum1)
        near1 = near_experts(pair1)
        got = after(over_wide(q_send, 1), pair1)
        last = q_send.shape[1] - 32
        q_both = jnp.concatenate(
            [q_keep[:, :last] + got[:, :last], q_keep[:, last:], got[:, last:]], axis=1
        )
    else:
        q_both = over_y(q_send, q_keep)
        sum0 = expert_sum(parts0)
        sum1 = expert_sum(parts1)

    def settle(mine, got):
        got = got.astype(mine.dtype)
        pair, rest = slice(0, 2), slice(2, 3)
        return jnp.where(
            chip == 0,
            jnp.concatenate([mine[pair], mine[rest], got[rest], got[pair]], axis=0),
            jnp.concatenate([got[pair], got[rest], mine[rest], mine[pair]], axis=0),
        )

    input_grad = settle(input_mine, after(input_got, q_both))
    if not direct:

        def in_order(a):
            four = near_experts(near_pair(a))
            return jnp.stack(
                [lax.dynamic_index_in_dim(four, place ^ e, 0, False) for e in range(E)]
            ).astype(F32)

        up0, up1, down0, down1 = (in_order(s[i]) for i in range(2) for s in (sum0, sum1))
        halves = [a.reshape(E, -1, n_wide, units) for a in (up0, up1)]
        grad_up = jnp.stack(halves, axis=3).reshape(E, -1, up.shape[1])
        grad_down = jnp.concatenate([down0, down1], axis=1)

    def over_seq_group(rows, lines):
        count = rows.shape[0]

        def sent(over, rows, lines):
            got = over(jnp.concatenate([rows.astype(BF16), *two_parts(lines)])).astype(F32)
            low = got[count : count + lines.shape[0]] + got[count + lines.shape[0] :]
            return got[:count], lines + low

        got, lines = sent(over_x, rows, lines)
        rows = rows + got
        other, lines = sent(over_core, rows, lines)
        return rows, other, lines

    owned = proj_weight.shape[0]
    if direct:
        rest = jnp.sum(over_z(q_both).astype(F32), axis=0)
        rows, lines = rest[:last], rest[last:].reshape(2, 2, 2, 8, width)
        lines = jnp.sum(lines, axis=(0, 2)).reshape(16, width)
    else:
        both = q_both.reshape(8, -1, width).astype(F32)
        last = both.shape[1] - 32
        rows = [both[:, :part], both[:, part : 2 * part]]
        halves = both[:, 2 * part : last].reshape(8, -1, 2, group)
        rows.append(jnp.moveaxis(halves, 2, 1).reshape(8, part, group))
        lines = jnp.sum(both[:, last:, :part].reshape(8, 2, 2, 8, part), axis=2)
        rows.append(jnp.moveaxis(lines.reshape(8, 16, part), 1, 2))
        rows = jnp.concatenate(rows, axis=2).reshape(width, -1)
        rows = lax.psum_scatter(rows, "wide", scatter_dimension=0, tiled=True)
        lines = jnp.pad(rows[:, -16:].T, ((0, 0), (0, width - owned)))
        more = rows[:, 2 * width : -16]
        more = jnp.concatenate([more[: owned // 2], more[owned // 2 :]], axis=1)
        rows = jnp.concatenate([rows[:, :width], rows[:, width : 2 * width], more])
    total, other, lines = over_seq_group(rows, lines)
    if direct:
        grad_up, grad_down = settle_experts(after(at, total), near0, near1)
    layer_out = settle(layer_mine, after(layer_got, total))
    grad_proj = total[:owned] + other[:owned]

    def thirds(a):
        more = a[2 * owned :]
        more = jnp.concatenate([more[:, :group], more[:, group:]])
        return [a[owned : 2 * owned, :group], a[owned : 2 * owned, group:], more]

    lines = lines[:, :owned]
    pairs = zip(thirds(total), thirds(other))
    ordered = [(jnp.where(core == 0, a, b), jnp.where(core == 0, b, a)) for a, b in pairs]
    grad_qkv = jnp.concatenate([a for pair in ordered for a in pair], axis=1)
    return (
        layer_out,
        input_grad,
        lines[8],
        lines[9],
        grad_qkv,
        grad_proj,
        lines[2],
        lines[3],
        lines[4 : 4 + E].T,
        grad_up,
        grad_down,
    )


def solution(mesh):
    placed = (
        P("wide", "seq", None),
        P("wide", None),
        P("wide", "seq", None),
        P("wide"),
        P("wide"),
        P("wide", None),
        P("wide", None),
        P("wide"),
        P("wide"),
        P("wide", None),
        P(None, "wide", None),
        P(None, "wide", None),
        P("wide", "seq", None),
    )
    return jax.shard_map(
        shards,
        mesh=mesh,
        in_specs=placed,
        out_specs=(
            P("wide", "seq", None),
            P("wide", "seq", None),
            P("wide"),
            P("wide"),
            P("wide", None),
            P("wide", None),
            P("wide"),
            P("wide"),
            P("wide", None),
            P(None, "wide", None),
            P(None, "wide", None),
        ),
        check_vma=False,
    )
```

```python
import functools
import math

import jax
import jax.numpy as jnp
from jax import lax
from jax.experimental import pallas as pl
from jax.experimental.pallas import tpu as pltpu
from jax.sharding import PartitionSpec as P

H = 8
E = 4
EPSILON = 1e-06
BIG = -1e30
MIB = 1024 * 1024
F32 = jnp.float32
BF16 = jnp.bfloat16


def dot(a, b, dims=((1,), (0,))):
    return lax.dot_general(a, b, (dims, ((), ())), preferred_element_type=F32)


def dot_nt(a, b):
    return dot(a, b, ((1,), (1,)))


def dot_tn(a, b):
    return dot(a, b, ((0,), (0,)))


def norm_parts(values):
    center = values - jnp.mean(values, axis=-1, keepdims=True)
    spread = jnp.mean(center * center, axis=-1, keepdims=True)
    rstd = lax.rsqrt(spread + EPSILON)
    return center * rstd, rstd


def norm_back(grad, xhat, rstd):
    return rstd * (
        grad
        - jnp.mean(grad, axis=-1, keepdims=True)
        - xhat * jnp.mean(grad * xhat, axis=-1, keepdims=True)
    )


TINY = pl.CostEstimate(flops=1000, bytes_accessed=1000, transcendentals=0)


def params(limit, **more):
    return pltpu.CompilerParams(vmem_limit_bytes=limit * MIB, **more)


def placed(*arrays):
    return [
        pltpu.with_memory_space_constraint(a, pltpu.HBM) if a.size > 1 << 15 else a for a in arrays
    ]


def in_hbm(shape, dtype):
    return pltpu.HBM(shape, dtype)


def whole(shape):
    return pl.BlockSpec(shape, lambda *_: (0,) * len(shape))


def per_image(*shape):
    return pl.BlockSpec((1, *shape), lambda i: (i,) + (0,) * len(shape))


SCALARS = pl.BlockSpec(memory_space=pltpu.SMEM)


def attend_kernel(
    images, head_dim, at_ref, own_ref, oth_ref, bias_ref, here_ref, there_ref,
    att_m_ref, mail_ref, qkv_ref, hidden_ref, lse_ref, wq_ref, small_ref, vec_ref,
):
    rows = own_ref.shape[1]
    features = wq_ref.shape[0]

    @pl.when(pl.program_id(0) == 0)
    def _():
        part = features // 8
        vec = jnp.zeros((8, features), F32)
        row = lax.broadcasted_iota(jnp.int32, (part, features), 0)
        col = lax.broadcasted_iota(jnp.int32, (part, features), 1)
        for index in range(8):
            side = at_ref[3] if index % 2 == 0 else 1 - at_ref[3]
            ref = (here_ref, there_ref)[index % 2].at[index // 2]
            base = pl.multiple_of((index // 2 * 2 + side) * part, part)
            wq_ref[pl.ds(base, part), :] = ref[:part, : wq_ref.shape[1]]
            mail_ref[pl.ds(images * rows + base, part), :] = ref[:part, wq_ref.shape[1] :]
            spread = (col == row + base).astype(F32).astype(BF16)
            vec = vec + dot(ref[part:, :part], spread)[:8]
        vec_ref[...] = vec
        tall = jnp.concatenate([vec, jnp.zeros((120, features), F32)], axis=0)
        small_ref[...] = tall.T.astype(BF16)

    gain, offset = vec_ref[0:1, :], vec_ref[1:2, :]
    for half, ref in enumerate((own_ref, oth_ref)):
        xhat, _ = norm_parts(ref[0].astype(F32))
        hidden_ref[0, half * rows : (half + 1) * rows, :] = (xhat * gain + offset).astype(BF16)
    width = wq_ref.shape[1] // 3
    packed = dot(hidden_ref[0], wq_ref[...]).astype(BF16)
    scaling = 1.0 / math.sqrt(head_dim)
    qkv_ref[0, :, :width] = (packed[:, :width].astype(F32) * scaling).astype(BF16)
    qkv_ref[0, :, width:] = packed[:, width:]
    bias = bias_ref[0]
    lane = lax.broadcasted_iota(jnp.int32, (1, 128), 1)
    sub = lax.broadcasted_iota(jnp.int32, (128, 1), 0)
    for pair in range(width // 128):
        cols = slice(pair * 128, pair * 128 + 128)
        q2 = qkv_ref[0, :, cols]
        k2 = qkv_ref[0, :, width + pair * 128 : width + pair * 128 + 128]
        v2 = qkv_ref[0, :, 2 * width + pair * 128 : 2 * width + pair * 128 + 128]
        v_t = v2.T
        both = []
        for part in range(2):
            mine = (lane >= head_dim * part) & (lane < head_dim * (part + 1))
            qm = jnp.where(mine, q2, jnp.zeros_like(q2))
            scores = dot_nt(k2, qm) + bias
            peak = jnp.max(scores, axis=0, keepdims=True)
            expo = jnp.exp(scores - peak)
            total = jnp.sum(expo, axis=0, keepdims=True)
            lse_ref[0, 2 * pair + part : 2 * pair + part + 1, :] = peak + jnp.log(total)
            both.append(dot(v_t, (expo * (1.0 / total)).astype(BF16)))
        out = jnp.where(sub < head_dim, both[0], both[1]).astype(BF16).T
        att_m_ref[0, :, cols] = out[:rows]
        mail_ref[pl.ds(pl.multiple_of(pl.program_id(0) * rows, 16), rows), cols] = out[rows:]


def attend(at, x_own, x_oth, bias, here, there, head_dim):
    images, rows, width = x_own.shape
    group = width // 2
    return pl.pallas_call(
        functools.partial(attend_kernel, images, head_dim),
        grid=(images,),
        in_specs=[
            SCALARS,
            per_image(rows, width),
            per_image(rows, width),
            per_image(2 * rows, 1),
            whole(here.shape),
            whole(there.shape),
        ],
        out_specs=[
            per_image(rows, group),
            whole((images * rows + width, group)),
            per_image(2 * rows, 3 * group),
            per_image(2 * rows, width),
            per_image(8, 2 * rows),
            whole((width, 3 * group)),
            whole((width, 128)),
            whole((8, width)),
        ],
        out_shape=[
            jax.ShapeDtypeStruct((images, rows, group), BF16),
            jax.ShapeDtypeStruct((images * rows + width, group), BF16),
            in_hbm((images, 2 * rows, 3 * group), BF16),
            in_hbm((images, 2 * rows, width), BF16),
            in_hbm((images, 8, 2 * rows), F32),
            in_hbm((width, 3 * group), BF16),
            in_hbm((width, 128), BF16),
            jax.ShapeDtypeStruct((8, width), F32),
        ],
        compiler_params=params(40),
        cost_estimate=TINY,
        name="attend",
    )(*placed(at, x_own, x_oth, bias, here, there))


def project_kernel(
    at_ref, att_m_ref, sent_ref, got_ref, x_ref, vec_ref, middle_ref, hidden_ref, proj_ref
):
    rows, group = att_m_ref.shape[1:]
    core, first = at_ref[1], pl.num_programs(0) * rows
    mine = pl.ds(pl.multiple_of(core * group + first, 16), group)
    other = pl.ds(pl.multiple_of((1 - core) * group + first, 16), group)

    def in_order(a, b):
        return jnp.concatenate([jnp.where(core == 0, a, b), jnp.where(core == 0, b, a)], axis=1)

    @pl.when(pl.program_id(0) == 0)
    def _():
        proj_ref[...] = in_order(sent_ref[mine, :], got_ref[mine, :])

    att_r = got_ref[pl.ds(pl.multiple_of(pl.program_id(0) * rows, 16), rows), :]
    halves = [
        dot(att_m_ref[0], ref[mine, :]) + dot(att_r, ref[other, :]) for ref in (sent_ref, got_ref)
    ]
    middle = x_ref[0].astype(F32) + in_order(*halves)
    middle_ref[0] = middle
    xhat, _ = norm_parts(middle)
    hidden_ref[0] = (xhat * vec_ref[2:3, :] + vec_ref[3:4, :]).astype(BF16)


def project(at, att_m, sent, got, x_own, vecs):
    images, rows, width = x_own.shape
    group = att_m.shape[2]
    return pl.pallas_call(
        project_kernel,
        grid=(images,),
        in_specs=[
            SCALARS,
            per_image(rows, group),
            whole(sent.shape),
            whole(got.shape),
            per_image(rows, width),
            whole(vecs.shape),
        ],
        out_specs=[per_image(rows, width), per_image(rows, width), whole((group, width))],
        out_shape=[
            in_hbm(x_own.shape, F32),
            jax.ShapeDtypeStruct(x_own.shape, BF16),
            in_hbm((group, width), BF16),
        ],
        compiler_params=params(24),
        cost_estimate=TINY,
        name="project",
    )(*placed(at, att_m, sent, got, x_own, vecs))


def join_kernel(at_ref, cot_ref, got_ref, out_ref):
    ours = pl.program_id(0) < pl.num_programs(0) // 2
    first = jnp.where(ours, cot_ref[0], got_ref[0])
    second = jnp.where(ours, got_ref[0], cot_ref[0])
    count = first.shape[0] - 1
    rows, width = out_ref.shape[1:]
    codes = jnp.concatenate(
        [first[count:, :count], second[count:, :count], jnp.zeros((1, width - 2 * count), BF16)],
        axis=1,
    )
    fill = jnp.zeros((rows - 2 * count - 1, width), BF16)
    out_ref[0] = jnp.concatenate([first[:count], second[:count], codes, fill], axis=0)


def join_cots(at, cot, got, rows):
    images, _, width = cot.shape
    half = images // 2

    def image(i, at):
        chip = (at[2] // 2 + i // half) % 2
        k = i % half
        return (jnp.where(k < half - 1, chip * (images - 2) + k, half - 1 + chip), 0, 0)

    one = pl.BlockSpec((1, *cot.shape[1:]), image)
    return pl.pallas_call(
        join_kernel,
        grid_spec=pltpu.PrefetchScalarGridSpec(
            num_scalar_prefetch=1,
            grid=(images,),
            in_specs=[one, one],
            out_specs=pl.BlockSpec((1, rows, width), lambda i, at: (i, 0, 0)),
        ),
        out_shape=in_hbm((images, rows, width), BF16),
        compiler_params=params(24),
        cost_estimate=TINY,
        name="join_cots",
    )(*placed(at, cot, got))


BLOCKS = (
    ((1, 0), (1, 1)),
    ((3, 0), (3, 1)),
    ((1, 2), (0, 2)),
    ((3, 2), (2, 2)),
    ((0, 0), (0, 1)),
    ((2, 0), (2, 1)),
)
EARLY = 4


def load_weights(parts_ref, up_ref, down_ref, sem):
    part = up_ref.shape[0] // 8
    width, units = down_ref.shape[1], up_ref.shape[1] // 8
    copies = []
    for index in range(8):
        base = slice(index * part, index * part + part)
        for block in range(up_ref.shape[1] // width):
            copies.append(
                pltpu.make_async_copy(
                    parts_ref.at[index, block * part : (block + 1) * part, :],
                    up_ref.at[base, block * width : (block + 1) * width],
                    sem.at[0],
                )
            )
        base = slice(index * units, (index + 1) * units)
        first = up_ref.shape[1] // width * part
        copies.append(
            pltpu.make_async_copy(
                parts_ref.at[index, first : first + units, :], down_ref.at[base, :], sem.at[1]
            )
        )
    return copies


def hidden_units(splits, xs, g_ref, up_ref, down_ref, act_ref, gp_ref):
    ff = up_ref.shape[1]
    chunk = ff // splits
    ret = dx = None
    for part in range(splits):
        cols = slice(part * chunk, (part + 1) * chunk)
        pre = dot(xs, up_ref[:, cols])
        back = dot_nt(g_ref[...], down_ref[cols, :])
        cdf = 0.5 + 0.5 * lax.erf(pre * math.sqrt(0.5))
        pdf = jnp.exp(-0.5 * pre * pre) * (1.0 / math.sqrt(2.0 * math.pi))
        act = (pre * cdf).astype(BF16)
        gp = (back * (cdf + pre * pdf)).astype(BF16)
        act_ref[:, cols] = act
        gp_ref[:, cols] = gp
        ret_part = dot(act, down_ref[cols, :])
        dx_part = dot_nt(gp, up_ref[:, cols])
        ret = ret_part if ret is None else ret + ret_part
        dx = dx_part if dx is None else dx + dx_part
    return ret, dx


def routing(hidden, wr_ref):
    logits = dot(hidden, wr_ref[...])
    lane = lax.broadcasted_iota(jnp.int32, (1, 128), 1)
    logits = jnp.where((lane >= 4) & (lane < 4 + E), logits, BIG)
    grown = jnp.exp(logits - jnp.max(logits, axis=-1, keepdims=True))
    return grown / jnp.sum(grown, axis=-1, keepdims=True)


def weight_of(hidden, wr_ref, mine):
    lane = lax.broadcasted_iota(jnp.int32, (1, 128), 1)
    router = jnp.where(lane == 4 + mine, routing(hidden, wr_ref), 0.0)
    return jnp.sum(router, axis=-1, keepdims=True)


def two_parts(values):
    high = values.astype(BF16)
    return high, (values - high.astype(F32)).astype(BF16)


def expert_first_kernel(
    splits, filled, blocks, kinds, at_ref, wr_ref, parts_ref, *refs
):
    step = pl.program_id(0)
    hs = dict(zip(kinds, refs))
    cots = refs[len(kinds) : len(kinds) + 2]
    cs = {k: cots[k // 2].at[pl.ds(k % 2 * (cots[0].shape[0] // 2), cots[0].shape[0] // 2)] for k in kinds}
    refs = refs[len(kinds) + 2 :]
    *refs, up_ref, down_ref, sem, piece_ref, piece_sem, act_ref, gp_ref, gu_ref, gd_ref = refs
    late = len(blocks) == EARLY
    if late:
        gu_in, gd_in, pos_ref, xs_ref, cs_ref, g_ref, ret_ref, dx_ref, out_ref = refs
    else:
        pos_ref, xs_ref, cs_ref, g_ref, ret_ref, dx_ref, gu_out, gd_out = refs
    rows = xs_ref.shape[0]
    mine = at_ref[2]

    def pieces_of(number):
        copies = []
        for k, (piece, image) in enumerate(blocks[number]):
            for j, kind in enumerate((hs, cs)):
                spot = number * 4 + 2 * k + j
                copies.append(
                    pltpu.make_async_copy(
                        kind[piece].at[image], piece_ref.at[spot], piece_sem.at[number]
                    )
                )
        return copies

    def sum_copies():
        return [
            pltpu.make_async_copy(gu_in, gu_ref, sem.at[2]),
            pltpu.make_async_copy(gd_in, gd_ref, sem.at[3]),
        ]

    def copies():
        return load_weights(parts_ref, up_ref, down_ref, sem)

    @pl.when(step == 0)
    def _():
        for number in range(len(blocks)):
            for copy in pieces_of(number):
                copy.start()
            if number == 0:
                for copy in copies():
                    copy.start()
        if late:
            for copy in sum_copies():
                copy.start()

    token = lax.broadcasted_iota(jnp.int32, (1, rows), 1)
    slot = lax.broadcasted_iota(jnp.int32, (rows, rows), 0)
    before = (slot < lax.broadcasted_iota(jnp.int32, (rows, rows), 1)).astype(F32).astype(BF16)
    for number, block in enumerate(blocks):

        @pl.when(step == number)
        def _(number=number, block=block):
            for copy in pieces_of(number):
                copy.wait()
            base, xs, got = 0.0, None, None
            for k in range(2):
                spot = number * 4 + 2 * k
                code = piece_ref[spot + 1, filled // 16 * 16 : filled // 16 * 16 + 16, :rows]
                code = code.astype(F32)[filled % 16 : filled % 16 + 1, :]
                first = jnp.floor(code * (1.0 / E))
                second = code - E * first
                own = mine.astype(F32)
                named = ((first == own) | (second == own)) & (token < filled)
                flag = jnp.where(named, 1.0, 0.0)
                rank = dot(jnp.broadcast_to(flag, (16, rows)).astype(BF16), before)[0:1, :] + base
                rank = jnp.where(named, rank, -1.0)
                base = base + jnp.sum(flag, axis=-1, keepdims=True)
                pos_ref[k : k + 1, :] = rank
                pick = (slot.astype(F32) == rank).astype(F32).astype(BF16)
                a, b = dot(pick, piece_ref[spot]), dot(pick, piece_ref[spot + 1])
                xs, got = (a, b) if xs is None else (xs + a, got + b)
            xs_ref[...] = xs.astype(BF16)
            cs_ref[...] = got.astype(BF16)

    xs = xs_ref[...]
    weight = weight_of(xs, wr_ref, mine)
    g_ref[...] = (cs_ref[...].astype(F32) * weight).astype(BF16)

    @pl.when(step == 0)
    def _():
        for copy in copies():
            copy.wait()

    ret, dx = hidden_units(splits, xs, g_ref, up_ref, down_ref, act_ref, gp_ref)
    ret_ref[...] = ret.astype(BF16)
    dx_ref[...] = dx.astype(BF16)
    gu, gd = dot_tn(xs, gp_ref[...]), dot_tn(g_ref[...], act_ref[...])

    @pl.when(step == 0)
    def _():
        if late:
            for copy in sum_copies():
                copy.wait()
            gu_ref[...] += gu
            gd_ref[...] += gd
        else:
            gu_ref[...] = gu
            gd_ref[...] = gd

    @pl.when(step > 0)
    def _():
        gu_ref[...] += gu
        gd_ref[...] += gd

    if not late:

        @pl.when(step == len(blocks) - 1)
        def _():
            gu_out[...] = gu_ref[...]
            gd_out[...] = gd_ref[...]

        return

    @pl.when(step == len(blocks) - 1)
    def _():
        width, ff = gu_ref.shape
        part, units = width // 8, ff // 8
        for index in range(8):
            own = gu_ref[index * part : (index + 1) * part, :].astype(BF16)
            for block in range(ff // width):
                into = slice(block * part, (block + 1) * part)
                out_ref[index, into, :] = own[:, block * width : (block + 1) * width]
            down = gd_ref[:, index * units : (index + 1) * units].T.astype(BF16)
            out_ref[index, ff // width * part :, :] = down


def slot_block(rows, cols, first=0):
    return pl.BlockSpec((rows, cols), lambda i: (i + first, 0))


def expert_first(at, hidden, cots, wr, parts, filled, start, count, sums=()):
    _, rows, width = hidden[0].shape
    ff = (parts.shape[1] - 2 * width // 8) * 8
    blocks = BLOCKS[start : start + count]
    kinds = tuple(sorted({piece for block in blocks for piece, _ in block}))
    outs = [(8, rows, F32), *[(rows, width, BF16)] * 5]
    anywhere = pl.BlockSpec(memory_space=pl.ANY)
    if sums:
        more_specs, more = [whole(parts.shape)], [in_hbm(parts.shape, BF16)]
    else:
        more_specs, more = [whole((width, ff))] * 2, [in_hbm((width, ff), F32)] * 2
    return pl.pallas_call(
        functools.partial(expert_first_kernel, 2, filled, blocks, kinds),
        grid=(count,),
        in_specs=[
            SCALARS,
            whole(wr.shape),
            *[anywhere] * (3 + len(kinds) + len(sums)),
        ],
        out_specs=[slot_block(a, b) for a, b, _ in outs] + more_specs,
        out_shape=[in_hbm((count * a, b), kind) for a, b, kind in outs] + more,
        scratch_shapes=[
            pltpu.VMEM((width, ff), BF16),
            pltpu.VMEM((ff, width), BF16),
            pltpu.SemaphoreType.DMA((4,)),
            pltpu.VMEM((4 * count, rows, width), BF16),
            pltpu.SemaphoreType.DMA((count,)),
            pltpu.VMEM((rows, ff), BF16),
            pltpu.VMEM((rows, ff), BF16),
            pltpu.VMEM((width, ff), F32),
            pltpu.VMEM((width, ff), F32),
        ],
        compiler_params=params(48),
        cost_estimate=TINY,
        name="expert_first",
    )(*placed(at, wr, parts, *[hidden[k] for k in kinds], *cots, *sums))


def expert_second_kernel(
    splits, step_count, filled, at_ref, pos_ref, xs_ref, cs_ref, g_ref, ret0_ref, dx0_ref, wr_ref,
    parts_ref, *refs,
):
    step = pl.program_id(0)
    rows = xs_ref.shape[0]
    *refs, up_ref, down_ref, sem = refs
    early = step_count == EARLY
    if early:
        act_ref, gp_ref, dh_m, dh_o, ret_m, ret_o, extra_m, extra_o = refs
        firsts = [((dh_m, ret_m), 0), ((dh_o, ret_o), 0)]
        targets = [[(dh, 0, back, 0), (dh, 1, back, 1)] for (dh, back), _ in firsts]
        targets += [
            [(dh, 2, back, 2), (extra, 0, extra, 1)]
            for ((dh, back), _), extra in zip(firsts, (extra_m, extra_o))
        ]
    else:
        act_ref, gp_ref, dh_m, dh_o, ret_m, ret_o = refs
        targets = [[(a, 0, b, 0), (a, 1, b, 1)] for a, b in ((dh_m, ret_m), (dh_o, ret_o))]

    @pl.when(step == 0)
    def _():
        copies = load_weights(parts_ref, up_ref, down_ref, sem)
        for copy in copies:
            copy.start()
        for copy in copies:
            copy.wait()

    ret, dx = hidden_units(splits, xs_ref[...], g_ref, up_ref, down_ref, act_ref, gp_ref)
    ret = ret + ret0_ref[...].astype(F32)
    weight = weight_of(xs_ref[...], wr_ref, at_ref[2])
    gate = jnp.sum(cs_ref[...].astype(F32) * ret, axis=-1, keepdims=True)
    dxb = (dx + dx0_ref[...].astype(F32)).astype(BF16)
    high, middle = two_parts(gate)
    low = (gate - high.astype(F32) - middle.astype(F32)).astype(BF16)
    lane = lax.broadcasted_iota(jnp.int32, (1, 128), 1) - filled % 16 - 3 * at_ref[2]
    gates = jnp.where(lane == 0, high.astype(F32), 0.0)
    gates = jnp.where(lane == 1, middle.astype(F32), gates)
    gates = jnp.where(lane == 2, low.astype(F32), gates).astype(BF16)
    retb = (ret * weight).astype(BF16)
    slot = lax.broadcasted_iota(jnp.int32, (rows, rows), 0).astype(F32)
    picks = [(slot == pos_ref[k : k + 1, :]).astype(F32).astype(BF16) for k in range(2)]
    for number, target in enumerate(targets):

        @pl.when(step == number)
        def _(target=target):
            for pick, (dh, i, back, j) in zip(picks, target):
                back[j] = dot_tn(pick, retb).astype(BF16)
                out = dot_tn(pick, dxb)
                dh[i] = out.astype(BF16)
                tail = dot_tn(gates, pick)[:16]
                tail = jnp.concatenate(
                    [tail, jnp.zeros((16, out.shape[1] - rows), F32)], axis=1
                )
                start = filled // 16 * 16
                dh[i, start : start + 16, :] = (out[start : start + 16] + tail).astype(BF16)


def expert_second(at, first, wr, parts, filled):
    pos, xs, cs, g, ret, dx = first
    rows, width = pos.shape[1], xs.shape[1]
    count = xs.shape[0] // rows
    ff = (parts.shape[1] - 2 * width // 8) * 8
    sizes = (3, 3, 3, 3, 2, 2) if count == EARLY else (2, 2, 2, 2)
    return pl.pallas_call(
        functools.partial(expert_second_kernel, 2, count, filled),
        grid=(count,),
        in_specs=[
            SCALARS,
            slot_block(8, rows),
            slot_block(rows, width),
            slot_block(rows, width),
            slot_block(rows, width),
            slot_block(rows, width),
            slot_block(rows, width),
            whole(wr.shape),
            pl.BlockSpec(memory_space=pl.ANY),
        ],
        out_specs=[slot_block(rows, ff), slot_block(rows, ff)]
        + [whole((n, rows, width)) for n in sizes],
        out_shape=[
            in_hbm((count * rows, ff), BF16),
            in_hbm((count * rows, ff), BF16),
        ]
        + [jax.ShapeDtypeStruct((n, rows, width), BF16) for n in sizes],
        scratch_shapes=[
            pltpu.VMEM((width, ff), BF16),
            pltpu.VMEM((ff, width), BF16),
            pltpu.SemaphoreType.DMA((2,)),
        ],
        compiler_params=params(30),
        cost_estimate=TINY,
        name="expert_second",
    )(*placed(at, pos, xs, cs, g, ret, dx, wr, parts))


def weight_grad_kernel(ends, *refs):
    count = len(ends)
    xs, gs, gps, acts = (refs[i * count : (i + 1) * count] for i in range(4))
    out_ref, xs_t, g_t, turned = refs[4 * count :]
    step = pl.program_id(0)
    width = xs_t.shape[0]
    part, cols = width // 8, gps[0].shape[1]
    spans = list(zip((0, *ends[:-1]), ends))

    @pl.when(step == 0)
    def _():
        for (low, high), x_ref, g_ref in zip(spans, xs, gs):
            xs_t[:, low:high] = x_ref[...].T
            g_t[:, low:high] = g_ref[...].T

    up = down = None
    for (low, high), gp, act in zip(spans, gps, acts):
        one, two = dot(xs_t[:, low:high], gp[...]), dot(g_t[:, low:high], act[...])
        up, down = (one, two) if up is None else (up + one, down + two)
    turned[:width, :] = up.astype(BF16)
    block = step * cols // width
    lanes = pl.ds(pl.multiple_of(step * cols % width, cols), cols)
    into = pl.ds(pl.multiple_of(block * part, part), part)
    for index in range(8):
        out_ref[index, into, lanes] = turned[index * part : (index + 1) * part, :]
    half = cols // 2
    first = out_ref.shape[1] - half
    tall = down.T.astype(BF16)
    out_ref[2 * step, first:, :] = tall[:half]
    out_ref[2 * step + 1, first:, :] = tall[half:]


def weight_grad(xs, g, gps, acts):
    width, ff = xs[0].shape[1], gps[0].shape[1]
    cols = ff // 4
    out = (8, ff // width * (width // 8) + ff // 8, width)
    ends = []
    for gp in gps:
        ends.append(gp.shape[0] + (ends[-1] if ends else 0))
    slots = ends[-1]
    return pl.pallas_call(
        functools.partial(weight_grad_kernel, tuple(ends)),
        grid=(4,),
        in_specs=[whole(a.shape) for a in (*xs, *g)]
        + [pl.BlockSpec((a.shape[0], cols), lambda i: (0, i)) for a in (*gps, *acts)],
        out_specs=whole(out),
        out_shape=in_hbm(out, BF16),
        scratch_shapes=[
            pltpu.VMEM((width, slots), BF16),
            pltpu.VMEM((width, slots), BF16),
            pltpu.VMEM((width, cols), BF16),
        ],
        compiler_params=params(30),
        cost_estimate=TINY,
        name="weight_grad",
    )(*placed(*xs, *g, *gps, *acts))


def settle_kernel(at_ref, zero_ref, one_ref, up_ref, down_ref):
    part, units = up_ref.shape[1], zero_ref.shape[1] - 2 * up_ref.shape[1]
    for half, ref in enumerate((zero_ref, one_ref)):
        for index in range(8):
            rows = slice(index // 4 * part, index // 4 * part + part)
            to = (2 * index + half) * units
            from_ = index % 4 * units
            up_ref[0, :, to : to + units] = ref[0, rows, from_ : from_ + units].astype(F32)
        down_ref[0, half * units : (half + 1) * units, :] = ref[0, 2 * part :, :].astype(F32)


def settle_experts(at, zero, one):
    _, rows, width = zero.shape
    part = width // 8
    units = rows - 2 * part
    piece = pl.BlockSpec((1, rows, width), lambda i, at: (i ^ at[2], 0, 0))
    return pl.pallas_call(
        settle_kernel,
        grid_spec=pltpu.PrefetchScalarGridSpec(
            num_scalar_prefetch=1,
            grid=(E,),
            in_specs=[piece, piece],
            out_specs=[
                pl.BlockSpec((1, part, 16 * units), lambda i, at: (i, 0, 0)),
                pl.BlockSpec((1, 2 * units, width), lambda i, at: (i, 0, 0)),
            ],
        ),
        out_shape=[
            jax.ShapeDtypeStruct((E, part, 16 * units), F32),
            jax.ShapeDtypeStruct((E, 2 * units, width), F32),
        ],
        compiler_params=params(24),
        cost_estimate=TINY,
        name="settle_experts",
    )(*placed(at, zero, one))


def early_images(images, rows, width):
    return pl.BlockSpec((1, rows, width), lambda i: (jnp.minimum(i, images - 2), 0, 0))


def middle_back_kernel(
    filled, at_ref, a_ref, ar_ref, b_ref, br_ref, xr_ref, mid_ref, cot_ref, vec_ref, am_ref,
    got_ref, hidden_ref, wr_ref,
    gm_ref, low_ref, parts_ref, sums_ref, proj_ref, router_ref,
):
    rows, width = mid_ref.shape[1:]
    group = am_ref.shape[2]

    @pl.when(pl.program_id(0) == 0)
    def _():
        sums_ref[...] = jnp.zeros_like(sums_ref)
        proj_ref[...] = jnp.zeros_like(proj_ref)
        router_ref[...] = jnp.zeros_like(router_ref)

    last = pl.program_id(0) == pl.num_programs(0) - 1
    grad = jnp.where(
        last,
        b_ref[0].astype(F32) + br_ref[0].astype(F32),
        a_ref[0].astype(F32) + ar_ref[0].astype(F32),
    )
    grad = grad + xr_ref[0].astype(F32)
    gates = [grad[filled + 3 * e : filled + 3 * e + 3, :384] for e in range(E)]
    gates = [jnp.sum(g, axis=0, keepdims=True) for g in gates]
    gates = jnp.concatenate([jnp.zeros((4, 384), F32), *gates, jnp.zeros((120, 384), F32)], axis=0)
    gates = gates.T[:rows]
    router = routing(hidden_ref[0], wr_ref)
    mean = jnp.sum(router * gates, axis=-1, keepdims=True)
    logit_grad = (router * (gates - mean)).astype(BF16)
    row = lax.broadcasted_iota(jnp.int32, (rows, 1), 0)
    grad = jnp.where(row < filled, grad, 0.0) + dot_nt(logit_grad, wr_ref[...])
    router_ref[...] += dot_tn(hidden_ref[0], logit_grad)
    xhat, rstd = norm_parts(mid_ref[0])
    sums_ref[2:3, :] += jnp.sum(grad * xhat, axis=0, keepdims=True)
    sums_ref[3:4, :] += jnp.sum(grad, axis=0, keepdims=True)
    out = cot_ref[0].astype(F32) + norm_back(grad * vec_ref[2:3, :], xhat, rstd)
    out = jnp.where(row < filled, out, 0.0)
    gm_ref[0] = out
    low = out.astype(BF16)
    low_ref[0] = low
    proj_ref[:group, :] += dot_tn(am_ref[0], low)
    att_r = got_ref[pl.ds(pl.multiple_of(pl.program_id(0) * rows, 16), rows), :]
    proj_ref[group:, :] += dot_tn(att_r, low)

    @pl.when(pl.program_id(0) == pl.num_programs(0) - 1)
    def _():
        part = width // 8
        router = router_ref[...].T[:8]
        lines = jnp.concatenate(two_parts(sums_ref[...] + router), axis=0)
        row = lax.broadcasted_iota(jnp.int32, (width, 128), 0)
        col = lax.broadcasted_iota(jnp.int32, (width, 128), 1)
        for index in range(8):
            base = index * part
            from_ = pl.multiple_of(base ^ (at_ref[1] * group), part)
            parts_ref[index, :part, :] = proj_ref[pl.ds(from_, part), :].astype(BF16)
            pick = ((row == col + base) & (col < part)).astype(F32).astype(BF16)
            parts_ref[index, part:, :128] = dot(lines, pick).astype(BF16)
            parts_ref[index, part:, 128:] = jnp.zeros((16, width - 128), BF16)


def middle_back(at, mine, near, extra, extra_near, from_x, middle, cots, vecs, att_m, got, hidden, wr, filled):
    images, rows, width = middle.shape
    one = per_image(rows, width)
    group = att_m.shape[2]
    piece = (8, width // 8 + 16, width)
    return pl.pallas_call(
        functools.partial(middle_back_kernel, filled),
        grid=(images,),
        in_specs=[SCALARS]
        + [early_images(images, rows, width)] * 2
        + [pl.BlockSpec((1, rows, width), lambda i: (0, 0, 0))] * 2
        + [one] * 2
        + [one, whole(vecs.shape), per_image(rows, group), whole(got.shape)]
        + [one, whole(wr.shape)],
        out_specs=[one, one, whole(piece)],
        out_shape=[
            in_hbm(middle.shape, F32),
            jax.ShapeDtypeStruct(middle.shape, BF16),
            in_hbm(piece, BF16),
        ],
        scratch_shapes=[
            pltpu.VMEM((8, width), F32),
            pltpu.VMEM((width, width), F32),
            pltpu.VMEM((width, 128), F32),
        ],
        compiler_params=params(32),
        cost_estimate=TINY,
        name="middle_back",
    )(*placed(at, mine, near, extra, extra_near, from_x, middle, cots, vecs, att_m, got, hidden, wr))


def layer_kernel(mid_ref, a_ref, ar_ref, b_ref, br_ref, xr_ref, mine_ref, send_ref):
    last = pl.program_id(0) == pl.num_programs(0) - 1
    total = jnp.where(
        last,
        b_ref[0].astype(F32) + br_ref[0].astype(F32),
        a_ref[0].astype(F32) + ar_ref[0].astype(F32),
    )
    total = total + mid_ref[0] + xr_ref[0].astype(F32)
    count = mine_ref.shape[1]
    mine_ref[0] = total[:count].astype(BF16)
    send_ref[0] = total[count : 2 * count].astype(BF16)


def layer_sum(middle, mine, near, extra, extra_near, from_x, quarter):
    images, rows, width = middle.shape
    one, part = per_image(rows, width), per_image(quarter, width)
    return pl.pallas_call(
        layer_kernel,
        grid=(images,),
        in_specs=[
            one,
            *[early_images(images, rows, width)] * 2,
            *[pl.BlockSpec((1, rows, width), lambda i: (1, 0, 0))] * 2,
            one,
        ],
        out_specs=[part, part],
        out_shape=[jax.ShapeDtypeStruct((images, quarter, width), BF16)] * 2,
        compiler_params=params(24),
        cost_estimate=TINY,
        name="layer_sum",
    )(*placed(middle, mine, near, extra, extra_near, from_x))


def attend_back_kernel(
    head_dim, at_ref, lm_ref, lo_ref, pm_ref, qkv_ref, lse_ref, bias_ref, h1_ref, wq_ref,
    dm_ref, do_ref, gq_ref, grad_ref, low_ref,
):
    rows = lm_ref.shape[1]
    low_ref[:rows, :] = lm_ref[0]
    low_ref[rows:, :] = lo_ref[0]
    out_grad = dot_nt(low_ref[...], pm_ref[...]).astype(BF16)
    width = pm_ref.shape[0]
    bias = bias_ref[0]
    lane = lax.broadcasted_iota(jnp.int32, (1, 128), 1)
    sub = lax.broadcasted_iota(jnp.int32, (128, 1), 0)
    scaling = 1.0 / math.sqrt(head_dim)
    for pair in range(width // 128):
        cols = slice(pair * 128, pair * 128 + 128)
        k_cols = slice(width + pair * 128, width + pair * 128 + 128)
        v_cols = slice(2 * width + pair * 128, 2 * width + pair * 128 + 128)
        q2, k2, v2 = qkv_ref[0, :, cols], qkv_ref[0, :, k_cols], qkv_ref[0, :, v_cols]
        o2 = out_grad[:, cols]
        k_t = k2.T
        dv = dk = None
        both = []
        for part in range(2):
            mine = (lane >= head_dim * part) & (lane < head_dim * (part + 1))
            qm = jnp.where(mine, q2, jnp.zeros_like(q2))
            om = jnp.where(mine, o2, jnp.zeros_like(o2))
            head = 2 * pair + part
            probs = jnp.exp(dot_nt(k2, qm) + bias - lse_ref[0, head : head + 1, :])
            prob_grad = dot_nt(v2, om)
            delta = jnp.sum(probs * prob_grad, axis=0, keepdims=True)
            score_grad = (probs * (prob_grad - delta)).astype(BF16)
            dv_part = dot(probs.astype(BF16), om)
            dk_part = dot(score_grad, qm)
            dv = dv_part if dv is None else dv + dv_part
            dk = dk_part if dk is None else dk + dk_part
            both.append(dot(k_t, score_grad))
        dq = (jnp.where(sub < head_dim, both[0], both[1]) * scaling).astype(BF16).T
        grad_ref[:, cols] = dq
        grad_ref[:, k_cols] = dk.astype(BF16)
        grad_ref[:, v_cols] = dv.astype(BF16)
    hidden_grad = dot_nt(grad_ref[...], wq_ref[...]).astype(BF16)
    dm_ref[0] = hidden_grad[:rows]
    do_ref[0] = hidden_grad[rows:]
    grad_qkv = dot_tn(h1_ref[0], grad_ref[...])

    @pl.when(pl.program_id(0) == 0)
    def _():
        gq_ref[...] = grad_qkv

    @pl.when(pl.program_id(0) > 0)
    def _():
        gq_ref[...] += grad_qkv


def attend_back(at, low_m, low_o, proj_m, qkv, lse, bias, hidden_one, wq, head_dim):
    images, rows, width = low_m.shape
    group = proj_m.shape[0]
    return pl.pallas_call(
        functools.partial(attend_back_kernel, head_dim),
        grid=(images,),
        in_specs=[
            SCALARS,
            per_image(rows, width),
            per_image(rows, width),
            whole(proj_m.shape),
            per_image(2 * rows, 3 * group),
            per_image(8, 2 * rows),
            per_image(2 * rows, 1),
            per_image(2 * rows, width),
            whole(wq.shape),
        ],
        out_specs=[
            per_image(rows, width),
            per_image(rows, width),
            whole((width, 3 * group)),
        ],
        out_shape=[
            in_hbm((images, rows, width), BF16),
            jax.ShapeDtypeStruct((images, rows, width), BF16),
            in_hbm((width, 3 * group), F32),
        ],
        scratch_shapes=[
            pltpu.VMEM((2 * rows, 3 * group), BF16),
            pltpu.VMEM((2 * rows, width), BF16),
        ],
        compiler_params=params(48),
        cost_estimate=TINY,
        name="attend_back",
    )(*placed(at, low_m, low_o, proj_m, qkv, lse, bias, hidden_one, wq))


def input_back_kernel(
    at_ref, x_ref, gm_ref, vec_ref, a_ref, ar_ref, gq_ref,
    out_ref, go_ref, send_ref, keep_ref, sums_ref,
):
    step, images = pl.program_id(0), pl.num_programs(0)
    grad = a_ref[0].astype(F32) + ar_ref[0].astype(F32)
    xhat, rstd = norm_parts(x_ref[0].astype(F32))
    out = gm_ref[0] + norm_back(grad * vec_ref[0:1, :], xhat, rstd)
    count = out_ref.shape[1]
    out_ref[0] = out[:count]
    go_ref[0] = out[count : 2 * count].astype(BF16)

    @pl.when(step == 0)
    def _():
        sums_ref[...] = jnp.zeros_like(sums_ref)

    sums_ref[0:1, :] += jnp.sum(grad * xhat, axis=0, keepdims=True)
    sums_ref[1:2, :] += jnp.sum(grad, axis=0, keepdims=True)

    @pl.when(step == images - 1)
    def _():
        total = gq_ref[...]
        width = grad.shape[1]
        part = width // 8
        lines = jnp.concatenate(two_parts(sums_ref[...]), axis=0)
        row = lax.broadcasted_iota(jnp.int32, (width, 128), 0)
        col = lax.broadcasted_iota(jnp.int32, (width, 128), 1)
        for index in range(8):
            base = index * part
            own = total[base : base + part].astype(BF16)
            half = jnp.concatenate([own[: part // 2, width:], own[part // 2 :, width:]], axis=1)
            pick_line = ((row == col + base) & (col < part)).astype(F32).astype(BF16)
            line = dot(lines, pick_line).astype(BF16)
            tail = jnp.concatenate([line, jnp.zeros((16, width - 128), BF16)], axis=1)
            block = jnp.concatenate([own[:, :width], half], axis=0)
            last = block.shape[0]

            def put(ref, block=block, tail=tail, z=index // 2, last=last):
                ref[z, :last] = block
                ref[z, last:] = tail

            @pl.when(at_ref[3] == index % 2)
            def _(put=put):
                put(keep_ref)

            @pl.when(at_ref[3] != index % 2)
            def _(put=put):
                put(send_ref)


def input_back(at, x_own, grad_middle, vecs, mine, near, grads, quarter):
    images, rows, width = x_own.shape
    one, part = per_image(rows, width), per_image(quarter, width)
    more = (4, width // 8 + (grads.shape[1] - width) * (width // 8) // width + 16, width)
    return pl.pallas_call(
        input_back_kernel,
        grid=(images,),
        in_specs=[SCALARS, one, one, whole(vecs.shape), one, one, whole(grads.shape)],
        out_specs=[part, part, whole(more), whole(more)],
        out_shape=[
            jax.ShapeDtypeStruct((images, quarter, width), F32),
            jax.ShapeDtypeStruct((images, quarter, width), BF16),
            jax.ShapeDtypeStruct(more, BF16),
            jax.ShapeDtypeStruct(more, BF16),
        ],
        scratch_shapes=[pltpu.VMEM((8, width), F32)],
        compiler_params=params(32),
        cost_estimate=TINY,
        name="input_back",
    )(*placed(at, x_own, grad_middle, vecs, mine, near, grads))


def shards(
    tokens,
    key_mask,
    expert_ids,
    ln1_gain,
    ln1_bias,
    qkv_weight,
    proj_weight,
    ln2_gain,
    ln2_bias,
    router_weight,
    up_weight,
    down_weight,
    cotangent,
):
    n_seq, n_wide = lax.axis_size("seq"), lax.axis_size("wide")
    images, quarter, width = tokens.shape
    head_dim = width // H
    group = width // 2
    filled = 2 * quarter
    rows = -(-(filled + 3 * E) // 16) * 16
    place = lax.axis_index("seq")
    chip, core = place // 2, place % 2
    direct = n_wide == 8
    spot = lax.axis_index("wide") if direct else 0
    at = jnp.stack([jnp.int32(spot), core, place, jnp.int32(spot) % 2])
    part = width // 8

    def over_seq(a, turn):
        return lax.ppermute(a, "seq", [(i, i ^ turn) for i in range(n_seq)])

    def over_x(a):
        return over_seq(a, 2)

    def over_core(a):
        return over_seq(a, 1)

    def over_wide(a, turn):
        return lax.ppermute(a, "wide", [(i, i ^ turn) for i in range(n_wide)])

    def after(value, *first):
        return lax.optimization_barrier((value, *first))[0]

    def images_of(a, of_chip):
        pair = lax.dynamic_slice_in_dim(a, of_chip * (images - 2), 2, 0)
        single = lax.dynamic_slice_in_dim(a, images // 2 - 1 + of_chip, 1, 0)
        return jnp.concatenate([pair, single], axis=0)

    def joined(first, second):
        both = jnp.concatenate([first, second], axis=1)
        return jnp.pad(both, ((0, 0), (0, rows - filled)) + ((0, 0),) * (both.ndim - 2))

    def cells(quarters, of_chip, of_core):
        first = lax.dynamic_index_in_dim(quarters, 2 * of_chip + of_core, 1, False)
        second = lax.dynamic_index_in_dim(quarters, 2 * (1 - of_chip) + of_core, 1, False)
        return joined(images_of(first, of_chip), images_of(second, of_chip))

    mask = key_mask.reshape(images, n_seq, quarter)
    valid = jnp.concatenate([cells(mask, chip, core), cells(mask, chip, 1 - core)], axis=1)
    bias = jnp.where(valid > 0, 0.0, BIG).astype(F32)[..., None]

    def heads_of(a):
        return jnp.concatenate(
            [lax.dynamic_slice_in_dim(a, (2 * i + core) * group, group, 1) for i in range(3)],
            axis=1,
        )

    wq = heads_of(qkv_weight)
    proj = lax.dynamic_slice_in_dim(proj_weight, core * group, group, 1)
    lines = jnp.stack([ln1_gain, ln1_bias, ln2_gain, ln2_bias])
    lines = jnp.concatenate([lines, router_weight.T], axis=0)
    up = lax.dynamic_index_in_dim(up_weight, place, 0, False)
    down = lax.dynamic_index_in_dim(down_weight, place, 0, False)
    units = down.shape[0] // 2

    def first_parts(wq, proj, lines):
        both = jnp.concatenate([wq, proj], axis=1)
        fill = ((0, 16 - lines.shape[0]), (0, both.shape[1] - lines.shape[1]))
        return jnp.concatenate([both, jnp.pad(lines, fill)], axis=0)

    def half_of(up, down, half):
        cols = up.reshape(up.shape[0], n_wide, 2, units)[:, :, half].reshape(up.shape[0], -1)
        down = down.reshape(-1, 2, units, width)[:, half].reshape(-1, width)
        blocks = [cols[:, i : i + width] for i in range(0, cols.shape[1], width)]
        return jnp.concatenate([*blocks, down], axis=0)

    one_all = first_parts(wq, proj, lines)
    one_all = jnp.broadcast_to(one_all[None], (4, *one_all.shape))
    codes = (expert_ids[..., 0] * E + expert_ids[..., 1]).astype(BF16)
    codes = jnp.pad(codes, ((0, 0), (0, width - quarter)))[:, None, :]
    cot = jnp.concatenate([cotangent, codes], axis=1)
    x_got = over_x(images_of(after(tokens, one_all), 1 - chip))
    x_own = joined(images_of(tokens, chip), x_got)
    x_oth = over_core(after(x_own, bias, cot))
    cot_got = over_x(after(cot, x_got))

    z_groups = [[y + 2 * z for z in range(4)] for y in range(2)]

    def all_of(a, axis=0):
        return lax.all_gather(a, "wide", axis=axis, tiled=True)

    if direct:
        ones = lax.all_to_all(one_all, "wide", 0, 0, axis_index_groups=z_groups, tiled=True)
        ones_y = over_wide(ones, 1)
        twos, threes = (
            lax.all_gather(after(half_of(up, down, half), ones, x_oth), "wide") for half in range(2)
        )
    else:

        def eight(a, axis=0):
            return jnp.split(a, 8, axis=axis)

        ones = jnp.stack([first_parts(*a) for a in zip(eight(all_of(wq)), eight(all_of(proj)), eight(all_of(lines, 1), 1))])
        ones, ones_y = ones[::2], ones[1::2]
        ups, downs = eight(all_of(up)), eight(all_of(down))
        twos, threes = (
            jnp.stack([half_of(a, b, half) for a, b in zip(ups, downs)]) for half in range(2)
        )

    att_m, mail, qkv, hidden_one, lse, wq, small, vecs = attend(
        at, x_own, x_oth, bias, ones, ones_y, head_dim
    )
    mail_got = over_core(mail)
    middle, hidden_two, proj_m = project(at, att_m, mail, mail_got, x_own, vecs)
    cot_got = after(cot_got, hidden_two)
    cots_m = join_cots(at, cot, cot_got, rows)
    cots_o = over_core(cots_m)

    hidden_b = over_x(hidden_two)
    hidden_c = over_core(hidden_two)
    ours = (hidden_two, None, hidden_c, None)
    *first_a, gu_a, gd_a = expert_first(
        at, ours, (cots_m, cots_o), small, twos, filled, EARLY, len(BLOCKS) - EARLY
    )
    hidden_d = over_core(after(hidden_b, gu_a))
    hidden = (hidden_two, hidden_b, hidden_c, hidden_d)
    *first_b, parts0 = expert_first(
        at, hidden, (cots_m, cots_o), small, twos, filled, 0, EARLY, (gu_a, gd_a)
    )
    act1, gp1, dh_m, dh_o, ret_m, ret_o, extra_m, extra_o = expert_second(
        after(at, parts0), first_b, small, threes, filled
    )
    dh_r = over_core(dh_o)
    dh_b = dh_m + dh_r
    dh_x = over_x(dh_b)
    ret_r = over_core(ret_o)
    def over_y(send, keep, *first):
        if not direct:
            return jnp.stack([keep, send], axis=1)
        got = over_wide(send, 1)
        return after(keep, *first) + after(got, *first)

    def over_z(both):
        return lax.all_to_all(both, "wide", 0, 0, axis_index_groups=z_groups, tiled=True)

    def expert_sum(both):
        both = both.reshape(8, -1, width)
        cut = 2 * part
        cols = jnp.moveaxis(both[:, :cut].reshape(8, 2, part, width), 1, 2).reshape(width, -1)
        rows = both[:, cut:].reshape(-1, width)
        return tuple(
            lax.psum_scatter(a, "wide", scatter_dimension=0, tiled=True) for a in (cols, rows)
        )

    def near_pair(a):
        return jnp.stack([a, over_core(a)])

    def near_experts(pairs):
        return jnp.concatenate([pairs, over_x(pairs)], axis=0)

    extra_r = over_core(extra_o)
    act2, gp2, late_m, late_o, late_ret_m, late_ret_o = expert_second(
        after(at, dh_b), first_a, small, threes, filled
    )
    late_r = over_core(late_o)
    late_ret_r = over_core(late_ret_o)
    if direct:
        sum0 = lax.all_to_all(parts0, "wide", 0, 0, tiled=True)
    ret_b = after(ret_m, act2) + ret_r
    xs = (after(first_b[1], ret_b), first_a[1])
    parts1 = weight_grad(xs, (first_b[3], first_a[3]), [gp1, gp2], [act1, act2])
    ret_x = over_x(after(ret_b, dh_x))

    grad_middle, low_m, r_parts = middle_back(
        at,
        late_m,
        late_r,
        extra_m,
        extra_r,
        dh_x,
        middle,
        cots_m,
        vecs,
        att_m,
        mail_got,
        hidden_two,
        small,
        filled,
    )
    low_o = over_core(low_m)
    if direct:
        sum1 = lax.all_to_all(after(parts1, dh_x, ret_b), "wide", 0, 0, tiled=True)
    dh1_m, dh1_o, grad_qkv = attend_back(
        at, low_m, low_o, proj_m, qkv, lse, bias, hidden_one, wq, head_dim
    )
    dh1_o = after(dh1_o, ret_x)
    dh1_r = over_core(dh1_o)
    input_mine, input_send, q_send, q_keep = input_back(
        at, x_own, grad_middle, vecs, dh1_m, dh1_r, grad_qkv, quarter
    )
    input_got = over_x(input_send)
    layer_mine, layer_send = layer_sum(
        middle, after(late_ret_m, q_send), late_ret_r, extra_m, extra_r, ret_x, quarter
    )
    layer_got = over_x(layer_send)
    if direct:
        r_sum = lax.all_to_all(after(r_parts, q_send), "wide", 0, 0, tiled=True)
        sum0 = jnp.sum(after(sum0, q_send).astype(F32), axis=0).astype(BF16)
        sum1 = jnp.sum(after(sum1, q_send).astype(F32), axis=0).astype(BF16)
        pair0, pair1 = near_pair(sum0), near_pair(sum1)
        near0, near1 = near_experts(pair0), near_experts(pair1)
        got = after(over_wide(q_send, 1), pair0, pair1, layer_send)
        last = q_send.shape[1] - 16
        q_both = jnp.concatenate(
            [q_keep[:, :last] + got[:, :last], q_keep[:, last:], got[:, last:]], axis=1
        )
    else:
        q_both = over_y(q_send, q_keep)
        sum0 = expert_sum(parts0)
        sum1 = expert_sum(parts1)

    def settle(mine, got):
        got = got.astype(mine.dtype)
        pair, rest = slice(0, 2), slice(2, 3)
        return jnp.where(
            chip == 0,
            jnp.concatenate([mine[pair], mine[rest], got[rest], got[pair]], axis=0),
            jnp.concatenate([got[pair], got[rest], mine[rest], mine[pair]], axis=0),
        )

    input_grad = settle(input_mine, after(input_got, q_both))
    if not direct:

        def in_order(a):
            four = near_experts(near_pair(a))
            return jnp.stack(
                [lax.dynamic_index_in_dim(four, place ^ e, 0, False) for e in range(E)]
            ).astype(F32)

        up0, up1, down0, down1 = (in_order(s[i]) for i in range(2) for s in (sum0, sum1))
        halves = [a.reshape(E, -1, n_wide, units) for a in (up0, up1)]
        grad_up = jnp.stack(halves, axis=3).reshape(E, -1, up.shape[1])
        grad_down = jnp.concatenate([down0, down1], axis=1)

    def over_seq_group(rows, lines):
        count = rows.shape[0]

        def sent(over, rows, lines):
            got = over(jnp.concatenate([rows.astype(BF16), *two_parts(lines)])).astype(F32)
            low = got[count : count + lines.shape[0]] + got[count + lines.shape[0] :]
            return got[:count], lines + low

        got, lines = sent(over_x, rows, lines)
        rows = rows + got
        other, lines = sent(over_core, rows, lines)
        return rows, other, lines

    owned = proj_weight.shape[0]
    if direct:
        rest = jnp.sum(after(over_z(q_both), near0, near1).astype(F32), axis=0)
        r_sum = jnp.sum(after(r_sum, q_both).astype(F32), axis=0)
        rows = jnp.concatenate([r_sum[:part], rest[:last]])
        lines = jnp.concatenate(
            [r_sum[part : part + 8] + r_sum[part + 8 :], jnp.sum(rest[last:].reshape(4, 8, width), 0)]
        )
    else:
        q_all, r_all = q_both.reshape(8, -1, width).astype(F32), r_parts.astype(F32)
        last = q_all.shape[1] - 16
        rows = [r_all[:, :part], q_all[:, :part]]
        halves = q_all[:, part:last].reshape(8, -1, 2, group)
        rows.append(jnp.moveaxis(halves, 2, 1).reshape(8, part, group))
        for a in (r_all[:, part:], q_all[:, last:]):
            rows.append(jnp.moveaxis(a[:, :8, :part] + a[:, 8:, :part], 1, 2))
        rows = jnp.concatenate(rows, axis=2).reshape(width, -1)
        rows = lax.psum_scatter(rows, "wide", scatter_dimension=0, tiled=True)
        lines = jnp.pad(rows[:, -16:].T, ((0, 0), (0, width - owned)))
        more = rows[:, 2 * width : -16]
        more = jnp.concatenate([more[: owned // 2], more[owned // 2 :]], axis=1)
        rows = jnp.concatenate([rows[:, :width], rows[:, width : 2 * width], more])
    total, other, lines = over_seq_group(rows, lines)
    if direct:
        grad_up, grad_down = settle_experts(after(at, rows), near0, near1)
    layer_out = settle(layer_mine, after(layer_got, rows))
    grad_proj = total[:owned] + other[:owned]

    def thirds(a):
        more = a[2 * owned :]
        more = jnp.concatenate([more[:, :group], more[:, group:]])
        return [a[owned : 2 * owned, :group], a[owned : 2 * owned, group:], more]

    lines = lines[:, :owned]
    pairs = zip(thirds(total), thirds(other))
    ordered = [(jnp.where(core == 0, a, b), jnp.where(core == 0, b, a)) for a, b in pairs]
    grad_qkv = jnp.concatenate([a for pair in ordered for a in pair], axis=1)
    return (
        layer_out,
        input_grad,
        lines[8],
        lines[9],
        grad_qkv,
        grad_proj,
        lines[2],
        lines[3],
        lines[4 : 4 + E].T,
        grad_up,
        grad_down,
    )


def solution(mesh):
    placed = (
        P("wide", "seq", None),
        P("wide", None),
        P("wide", "seq", None),
        P("wide"),
        P("wide"),
        P("wide", None),
        P("wide", None),
        P("wide"),
        P("wide"),
        P("wide", None),
        P(None, "wide", None),
        P(None, "wide", None),
        P("wide", "seq", None),
    )
    return jax.shard_map(
        shards,
        mesh=mesh,
        in_specs=placed,
        out_specs=(
            P("wide", "seq", None),
            P("wide", "seq", None),
            P("wide"),
            P("wide"),
            P("wide", None),
            P("wide", None),
            P("wide"),
            P("wide"),
            P("wide", None),
            P(None, "wide", None),
            P(None, "wide", None),
        ),
        check_vma=False,
    )
```

```python
import functools
import math

import jax
import jax.numpy as jnp
from jax import lax
from jax.experimental import pallas as pl
from jax.experimental.pallas import tpu as pltpu
from jax.sharding import PartitionSpec as P

H = 8
E = 4
EPSILON = 1e-06
BIG = -1e30
MIB = 1024 * 1024
F32 = jnp.float32
BF16 = jnp.bfloat16


def dot(a, b, dims=((1,), (0,))):
    return lax.dot_general(a, b, (dims, ((), ())), preferred_element_type=F32)


def dot_nt(a, b):
    return dot(a, b, ((1,), (1,)))


def dot_tn(a, b):
    return dot(a, b, ((0,), (0,)))


def norm_parts(values):
    center = values - jnp.mean(values, axis=-1, keepdims=True)
    spread = jnp.mean(center * center, axis=-1, keepdims=True)
    rstd = lax.rsqrt(spread + EPSILON)
    return center * rstd, rstd


def norm_back(grad, xhat, rstd):
    return rstd * (
        grad
        - jnp.mean(grad, axis=-1, keepdims=True)
        - xhat * jnp.mean(grad * xhat, axis=-1, keepdims=True)
    )


TINY = pl.CostEstimate(flops=1000, bytes_accessed=1000, transcendentals=0)


def params(limit, **more):
    return pltpu.CompilerParams(vmem_limit_bytes=limit * MIB, **more)


def placed(*arrays):
    return [
        pltpu.with_memory_space_constraint(a, pltpu.HBM) if a.size > 1 << 15 else a for a in arrays
    ]


def in_hbm(shape, dtype):
    return pltpu.HBM(shape, dtype)


def whole(shape):
    return pl.BlockSpec(shape, lambda *_: (0,) * len(shape))


def per_image(*shape):
    return pl.BlockSpec((1, *shape), lambda i: (i,) + (0,) * len(shape))


SCALARS = pl.BlockSpec(memory_space=pltpu.SMEM)


def attend_kernel(
    images, head_dim, at_ref, own_ref, oth_ref, bias_ref, here_ref, there_ref,
    att_m_ref, mail_ref, qkv_ref, hidden_ref, lse_ref, wq_ref, small_ref, vec_ref,
):
    rows = own_ref.shape[1]
    features = wq_ref.shape[0]

    @pl.when(pl.program_id(0) == 0)
    def _():
        part = features // 8
        vec = jnp.zeros((8, features), F32)
        row = lax.broadcasted_iota(jnp.int32, (part, features), 0)
        col = lax.broadcasted_iota(jnp.int32, (part, features), 1)
        for index in range(8):
            side = at_ref[3] if index % 2 == 0 else 1 - at_ref[3]
            ref = (here_ref, there_ref)[index % 2].at[index // 2]
            base = pl.multiple_of((index // 2 * 2 + side) * part, part)
            wq_ref[pl.ds(base, part), :] = ref[:part, : wq_ref.shape[1]]
            mail_ref[pl.ds(images * rows + base, part), :] = ref[:part, wq_ref.shape[1] :]
            spread = (col == row + base).astype(F32).astype(BF16)
            vec = vec + dot(ref[part:, :part], spread)[:8]
        vec_ref[...] = vec
        tall = jnp.concatenate([vec, jnp.zeros((120, features), F32)], axis=0)
        small_ref[...] = tall.T.astype(BF16)

    gain, offset = vec_ref[0:1, :], vec_ref[1:2, :]
    for half, ref in enumerate((own_ref, oth_ref)):
        xhat, _ = norm_parts(ref[0].astype(F32))
        hidden_ref[0, half * rows : (half + 1) * rows, :] = (xhat * gain + offset).astype(BF16)
    width = wq_ref.shape[1] // 3
    packed = dot(hidden_ref[0], wq_ref[...]).astype(BF16)
    scaling = 1.0 / math.sqrt(head_dim)
    qkv_ref[0, :, :width] = (packed[:, :width].astype(F32) * scaling).astype(BF16)
    qkv_ref[0, :, width:] = packed[:, width:]
    bias = bias_ref[0]
    lane = lax.broadcasted_iota(jnp.int32, (1, 128), 1)
    sub = lax.broadcasted_iota(jnp.int32, (128, 1), 0)
    for pair in range(width // 128):
        cols = slice(pair * 128, pair * 128 + 128)
        q2 = qkv_ref[0, :, cols]
        k2 = qkv_ref[0, :, width + pair * 128 : width + pair * 128 + 128]
        v2 = qkv_ref[0, :, 2 * width + pair * 128 : 2 * width + pair * 128 + 128]
        v_t = v2.T
        both = []
        for part in range(2):
            mine = (lane >= head_dim * part) & (lane < head_dim * (part + 1))
            qm = jnp.where(mine, q2, jnp.zeros_like(q2))
            scores = dot_nt(k2, qm) + bias
            peak = jnp.max(scores, axis=0, keepdims=True)
            expo = jnp.exp(scores - peak)
            total = jnp.sum(expo, axis=0, keepdims=True)
            lse_ref[0, 2 * pair + part : 2 * pair + part + 1, :] = peak + jnp.log(total)
            both.append(dot(v_t, (expo * (1.0 / total)).astype(BF16)))
        out = jnp.where(sub < head_dim, both[0], both[1]).astype(BF16).T
        att_m_ref[0, :, cols] = out[:rows]
        mail_ref[pl.ds(pl.multiple_of(pl.program_id(0) * rows, 16), rows), cols] = out[rows:]


def attend(at, x_own, x_oth, bias, here, there, head_dim):
    images, rows, width = x_own.shape
    group = width // 2
    return pl.pallas_call(
        functools.partial(attend_kernel, images, head_dim),
        grid=(images,),
        in_specs=[
            SCALARS,
            per_image(rows, width),
            per_image(rows, width),
            per_image(2 * rows, 1),
            whole(here.shape),
            whole(there.shape),
        ],
        out_specs=[
            per_image(rows, group),
            whole((images * rows + width, group)),
            per_image(2 * rows, 3 * group),
            per_image(2 * rows, width),
            per_image(8, 2 * rows),
            whole((width, 3 * group)),
            whole((width, 128)),
            whole((8, width)),
        ],
        out_shape=[
            jax.ShapeDtypeStruct((images, rows, group), BF16),
            jax.ShapeDtypeStruct((images * rows + width, group), BF16),
            in_hbm((images, 2 * rows, 3 * group), BF16),
            in_hbm((images, 2 * rows, width), BF16),
            in_hbm((images, 8, 2 * rows), F32),
            in_hbm((width, 3 * group), BF16),
            in_hbm((width, 128), BF16),
            jax.ShapeDtypeStruct((8, width), F32),
        ],
        compiler_params=params(40),
        cost_estimate=TINY,
        name="attend",
    )(*placed(at, x_own, x_oth, bias, here, there))


def project_kernel(
    at_ref, att_m_ref, sent_ref, got_ref, x_ref, vec_ref, middle_ref, hidden_ref, proj_ref
):
    rows, group = att_m_ref.shape[1:]
    core, first = at_ref[1], pl.num_programs(0) * rows
    mine = pl.ds(pl.multiple_of(core * group + first, 16), group)
    other = pl.ds(pl.multiple_of((1 - core) * group + first, 16), group)

    def in_order(a, b):
        return jnp.concatenate([jnp.where(core == 0, a, b), jnp.where(core == 0, b, a)], axis=1)

    @pl.when(pl.program_id(0) == 0)
    def _():
        proj_ref[...] = in_order(sent_ref[mine, :], got_ref[mine, :])

    att_r = got_ref[pl.ds(pl.multiple_of(pl.program_id(0) * rows, 16), rows), :]
    halves = [
        dot(att_m_ref[0], ref[mine, :]) + dot(att_r, ref[other, :]) for ref in (sent_ref, got_ref)
    ]
    middle = x_ref[0].astype(F32) + in_order(*halves)
    middle_ref[0] = middle
    xhat, _ = norm_parts(middle)
    hidden_ref[0] = (xhat * vec_ref[2:3, :] + vec_ref[3:4, :]).astype(BF16)


def project(at, att_m, sent, got, x_own, vecs):
    images, rows, width = x_own.shape
    group = att_m.shape[2]
    return pl.pallas_call(
        project_kernel,
        grid=(images,),
        in_specs=[
            SCALARS,
            per_image(rows, group),
            whole(sent.shape),
            whole(got.shape),
            per_image(rows, width),
            whole(vecs.shape),
        ],
        out_specs=[per_image(rows, width), per_image(rows, width), whole((group, width))],
        out_shape=[
            in_hbm(x_own.shape, F32),
            jax.ShapeDtypeStruct(x_own.shape, BF16),
            in_hbm((group, width), BF16),
        ],
        compiler_params=params(24),
        cost_estimate=TINY,
        name="project",
    )(*placed(at, att_m, sent, got, x_own, vecs))


def join_kernel(at_ref, cot_ref, got_ref, out_ref):
    ours = pl.program_id(0) < pl.num_programs(0) // 2
    first = jnp.where(ours, cot_ref[0], got_ref[0])
    second = jnp.where(ours, got_ref[0], cot_ref[0])
    count = first.shape[0] - 1
    rows, width = out_ref.shape[1:]
    codes = jnp.concatenate(
        [first[count:, :count], second[count:, :count], jnp.zeros((1, width - 2 * count), BF16)],
        axis=1,
    )
    fill = jnp.zeros((rows - 2 * count - 1, width), BF16)
    out_ref[0] = jnp.concatenate([first[:count], second[:count], codes, fill], axis=0)


def join_cots(at, cot, got, rows):
    images, _, width = cot.shape
    half = images // 2

    def image(i, at):
        chip = (at[2] // 2 + i // half) % 2
        k = i % half
        return (jnp.where(k < half - 1, chip * (images - 2) + k, half - 1 + chip), 0, 0)

    one = pl.BlockSpec((1, *cot.shape[1:]), image)
    return pl.pallas_call(
        join_kernel,
        grid_spec=pltpu.PrefetchScalarGridSpec(
            num_scalar_prefetch=1,
            grid=(images,),
            in_specs=[one, one],
            out_specs=pl.BlockSpec((1, rows, width), lambda i, at: (i, 0, 0)),
        ),
        out_shape=in_hbm((images, rows, width), BF16),
        compiler_params=params(24),
        cost_estimate=TINY,
        name="join_cots",
    )(*placed(at, cot, got))


BLOCKS = (
    ((1, 0), (1, 1)),
    ((3, 0), (3, 1)),
    ((1, 2), (0, 2)),
    ((3, 2), (2, 2)),
    ((0, 0), (0, 1)),
    ((2, 0), (2, 1)),
)
EARLY = 4


def load_weights(parts_ref, up_ref, down_ref, sem):
    part = up_ref.shape[0] // 8
    width, units = down_ref.shape[1], up_ref.shape[1] // 8
    copies = []
    for index in range(8):
        base = slice(index * part, index * part + part)
        for block in range(up_ref.shape[1] // width):
            copies.append(
                pltpu.make_async_copy(
                    parts_ref.at[index, block * part : (block + 1) * part, :],
                    up_ref.at[base, block * width : (block + 1) * width],
                    sem.at[0],
                )
            )
        base = slice(index * units, (index + 1) * units)
        first = up_ref.shape[1] // width * part
        copies.append(
            pltpu.make_async_copy(
                parts_ref.at[index, first : first + units, :], down_ref.at[base, :], sem.at[1]
            )
        )
    return copies


def hidden_units(splits, xs, g_ref, up_ref, down_ref, act_ref, gp_ref):
    ff = up_ref.shape[1]
    chunk = ff // splits
    ret = dx = None
    for part in range(splits):
        cols = slice(part * chunk, (part + 1) * chunk)
        pre = dot(xs, up_ref[:, cols])
        back = dot_nt(g_ref[...], down_ref[cols, :])
        cdf = 0.5 + 0.5 * lax.erf(pre * math.sqrt(0.5))
        pdf = jnp.exp(-0.5 * pre * pre) * (1.0 / math.sqrt(2.0 * math.pi))
        act = (pre * cdf).astype(BF16)
        gp = (back * (cdf + pre * pdf)).astype(BF16)
        act_ref[:, cols] = act
        gp_ref[:, cols] = gp
        ret_part = dot(act, down_ref[cols, :])
        dx_part = dot_nt(gp, up_ref[:, cols])
        ret = ret_part if ret is None else ret + ret_part
        dx = dx_part if dx is None else dx + dx_part
    return ret, dx


def routing(hidden, wr_ref):
    logits = dot(hidden, wr_ref[...])
    lane = lax.broadcasted_iota(jnp.int32, (1, 128), 1)
    logits = jnp.where((lane >= 4) & (lane < 4 + E), logits, BIG)
    grown = jnp.exp(logits - jnp.max(logits, axis=-1, keepdims=True))
    return grown / jnp.sum(grown, axis=-1, keepdims=True)


def weight_of(hidden, wr_ref, mine):
    lane = lax.broadcasted_iota(jnp.int32, (1, 128), 1)
    router = jnp.where(lane == 4 + mine, routing(hidden, wr_ref), 0.0)
    return jnp.sum(router, axis=-1, keepdims=True)


def two_parts(values):
    high = values.astype(BF16)
    return high, (values - high.astype(F32)).astype(BF16)


def expert_first_kernel(
    splits, filled, blocks, kinds, at_ref, wr_ref, parts_ref, *refs
):
    step = pl.program_id(0)
    hs = dict(zip(kinds, refs))
    cots = refs[len(kinds) : len(kinds) + 2]
    cs = {k: cots[k // 2].at[pl.ds(k % 2 * (cots[0].shape[0] // 2), cots[0].shape[0] // 2)] for k in kinds}
    refs = refs[len(kinds) + 2 :]
    *refs, up_ref, down_ref, sem, piece_ref, piece_sem, act_ref, gp_ref, gu_ref, gd_ref = refs
    late = len(blocks) == EARLY
    if late:
        gu_in, gd_in, pos_ref, xs_ref, cs_ref, g_ref, ret_ref, dx_ref, out_ref = refs
    else:
        pos_ref, xs_ref, cs_ref, g_ref, ret_ref, dx_ref, gu_out, gd_out = refs
    rows = xs_ref.shape[0]
    mine = at_ref[2]

    def pieces_of(number):
        copies = []
        for k, (piece, image) in enumerate(blocks[number]):
            for j, kind in enumerate((hs, cs)):
                spot = number * 4 + 2 * k + j
                copies.append(
                    pltpu.make_async_copy(
                        kind[piece].at[image], piece_ref.at[spot], piece_sem.at[number]
                    )
                )
        return copies

    def sum_copies():
        return [
            pltpu.make_async_copy(gu_in, gu_ref, sem.at[2]),
            pltpu.make_async_copy(gd_in, gd_ref, sem.at[3]),
        ]

    def copies():
        return load_weights(parts_ref, up_ref, down_ref, sem)

    @pl.when(step == 0)
    def _():
        for number in range(len(blocks)):
            for copy in pieces_of(number):
                copy.start()
            if number == 0:
                for copy in copies():
                    copy.start()
        if late:
            for copy in sum_copies():
                copy.start()

    token = lax.broadcasted_iota(jnp.int32, (1, rows), 1)
    slot = lax.broadcasted_iota(jnp.int32, (rows, rows), 0)
    before = (slot < lax.broadcasted_iota(jnp.int32, (rows, rows), 1)).astype(F32).astype(BF16)
    for number, block in enumerate(blocks):

        @pl.when(step == number)
        def _(number=number, block=block):
            for copy in pieces_of(number):
                copy.wait()
            base, xs, got = 0.0, None, None
            for k in range(2):
                spot = number * 4 + 2 * k
                code = piece_ref[spot + 1, filled // 16 * 16 : filled // 16 * 16 + 16, :rows]
                code = code.astype(F32)[filled % 16 : filled % 16 + 1, :]
                first = jnp.floor(code * (1.0 / E))
                second = code - E * first
                own = mine.astype(F32)
                named = ((first == own) | (second == own)) & (token < filled)
                flag = jnp.where(named, 1.0, 0.0)
                rank = dot(jnp.broadcast_to(flag, (16, rows)).astype(BF16), before)[0:1, :] + base
                rank = jnp.where(named, rank, -1.0)
                base = base + jnp.sum(flag, axis=-1, keepdims=True)
                pos_ref[k : k + 1, :] = rank
                pick = (slot.astype(F32) == rank).astype(F32).astype(BF16)
                a, b = dot(pick, piece_ref[spot]), dot(pick, piece_ref[spot + 1])
                xs, got = (a, b) if xs is None else (xs + a, got + b)
            xs_ref[...] = xs.astype(BF16)
            cs_ref[...] = got.astype(BF16)

    xs = xs_ref[...]
    weight = weight_of(xs, wr_ref, mine)
    g_ref[...] = (cs_ref[...].astype(F32) * weight).astype(BF16)

    @pl.when(step == 0)
    def _():
        for copy in copies():
            copy.wait()

    ret, dx = hidden_units(splits, xs, g_ref, up_ref, down_ref, act_ref, gp_ref)
    ret_ref[...] = ret.astype(BF16)
    dx_ref[...] = dx.astype(BF16)
    gu, gd = dot_tn(xs, gp_ref[...]), dot_tn(g_ref[...], act_ref[...])

    @pl.when(step == 0)
    def _():
        if late:
            for copy in sum_copies():
                copy.wait()
            gu_ref[...] += gu
            gd_ref[...] += gd
        else:
            gu_ref[...] = gu
            gd_ref[...] = gd

    @pl.when(step > 0)
    def _():
        gu_ref[...] += gu
        gd_ref[...] += gd

    if not late:

        @pl.when(step == len(blocks) - 1)
        def _():
            gu_out[...] = gu_ref[...]
            gd_out[...] = gd_ref[...]

        return

    @pl.when(step == len(blocks) - 1)
    def _():
        width, ff = gu_ref.shape
        part, units = width // 8, ff // 8
        for index in range(8):
            own = gu_ref[index * part : (index + 1) * part, :].astype(BF16)
            for block in range(ff // width):
                into = slice(block * part, (block + 1) * part)
                out_ref[index, into, :] = own[:, block * width : (block + 1) * width]
            down = gd_ref[:, index * units : (index + 1) * units].T.astype(BF16)
            out_ref[index, ff // width * part :, :] = down


def slot_block(rows, cols, first=0):
    return pl.BlockSpec((rows, cols), lambda i: (i + first, 0))


def expert_first(at, hidden, cots, wr, parts, filled, start, count, sums=()):
    _, rows, width = hidden[0].shape
    ff = (parts.shape[1] - 2 * width // 8) * 8
    blocks = BLOCKS[start : start + count]
    kinds = tuple(sorted({piece for block in blocks for piece, _ in block}))
    outs = [(8, rows, F32), *[(rows, width, BF16)] * 5]
    anywhere = pl.BlockSpec(memory_space=pl.ANY)
    if sums:
        more_specs, more = [whole(parts.shape)], [in_hbm(parts.shape, BF16)]
    else:
        more_specs, more = [whole((width, ff))] * 2, [in_hbm((width, ff), F32)] * 2
    return pl.pallas_call(
        functools.partial(expert_first_kernel, 2, filled, blocks, kinds),
        grid=(count,),
        in_specs=[
            SCALARS,
            whole(wr.shape),
            *[anywhere] * (3 + len(kinds) + len(sums)),
        ],
        out_specs=[slot_block(a, b) for a, b, _ in outs] + more_specs,
        out_shape=[in_hbm((count * a, b), kind) for a, b, kind in outs] + more,
        scratch_shapes=[
            pltpu.VMEM((width, ff), BF16),
            pltpu.VMEM((ff, width), BF16),
            pltpu.SemaphoreType.DMA((4,)),
            pltpu.VMEM((4 * count, rows, width), BF16),
            pltpu.SemaphoreType.DMA((count,)),
            pltpu.VMEM((rows, ff), BF16),
            pltpu.VMEM((rows, ff), BF16),
            pltpu.VMEM((width, ff), F32),
            pltpu.VMEM((width, ff), F32),
        ],
        compiler_params=params(48),
        cost_estimate=TINY,
        name="expert_first",
    )(*placed(at, wr, parts, *[hidden[k] for k in kinds], *cots, *sums))


def expert_second_kernel(
    splits, step_count, filled, at_ref, pos_ref, xs_ref, cs_ref, g_ref, ret0_ref, dx0_ref, wr_ref,
    parts_ref, *refs,
):
    step = pl.program_id(0)
    rows = xs_ref.shape[0]
    *refs, up_ref, down_ref, sem = refs
    early = step_count == EARLY
    if early:
        act_ref, gp_ref, dh_m, dh_o, ret_m, ret_o, extra_m, extra_o = refs
        firsts = [((dh_m, ret_m), 0), ((dh_o, ret_o), 0)]
        targets = [[(dh, 0, back, 0), (dh, 1, back, 1)] for (dh, back), _ in firsts]
        targets += [
            [(dh, 2, back, 2), (extra, 0, extra, 1)]
            for ((dh, back), _), extra in zip(firsts, (extra_m, extra_o))
        ]
    else:
        act_ref, gp_ref, dh_m, dh_o, ret_m, ret_o = refs
        targets = [[(a, 0, b, 0), (a, 1, b, 1)] for a, b in ((dh_m, ret_m), (dh_o, ret_o))]

    @pl.when(step == 0)
    def _():
        copies = load_weights(parts_ref, up_ref, down_ref, sem)
        for copy in copies:
            copy.start()
        for copy in copies:
            copy.wait()

    ret, dx = hidden_units(splits, xs_ref[...], g_ref, up_ref, down_ref, act_ref, gp_ref)
    ret = ret + ret0_ref[...].astype(F32)
    weight = weight_of(xs_ref[...], wr_ref, at_ref[2])
    gate = jnp.sum(cs_ref[...].astype(F32) * ret, axis=-1, keepdims=True)
    dxb = (dx + dx0_ref[...].astype(F32)).astype(BF16)
    high, middle = two_parts(gate)
    low = (gate - high.astype(F32) - middle.astype(F32)).astype(BF16)
    lane = lax.broadcasted_iota(jnp.int32, (1, 128), 1) - filled % 16 - 3 * at_ref[2]
    gates = jnp.where(lane == 0, high.astype(F32), 0.0)
    gates = jnp.where(lane == 1, middle.astype(F32), gates)
    gates = jnp.where(lane == 2, low.astype(F32), gates).astype(BF16)
    retb = (ret * weight).astype(BF16)
    slot = lax.broadcasted_iota(jnp.int32, (rows, rows), 0).astype(F32)
    picks = [(slot == pos_ref[k : k + 1, :]).astype(F32).astype(BF16) for k in range(2)]
    for number, target in enumerate(targets):

        @pl.when(step == number)
        def _(target=target):
            for pick, (dh, i, back, j) in zip(picks, target):
                back[j] = dot_tn(pick, retb).astype(BF16)
                out = dot_tn(pick, dxb)
                dh[i] = out.astype(BF16)
                tail = dot_tn(gates, pick)[:16]
                tail = jnp.concatenate(
                    [tail, jnp.zeros((16, out.shape[1] - rows), F32)], axis=1
                )
                start = filled // 16 * 16
                dh[i, start : start + 16, :] = (out[start : start + 16] + tail).astype(BF16)


def expert_second(at, first, wr, parts, filled):
    pos, xs, cs, g, ret, dx = first
    rows, width = pos.shape[1], xs.shape[1]
    count = xs.shape[0] // rows
    ff = (parts.shape[1] - 2 * width // 8) * 8
    sizes = (3, 3, 3, 3, 2, 2) if count == EARLY else (2, 2, 2, 2)
    return pl.pallas_call(
        functools.partial(expert_second_kernel, 2, count, filled),
        grid=(count,),
        in_specs=[
            SCALARS,
            slot_block(8, rows),
            slot_block(rows, width),
            slot_block(rows, width),
            slot_block(rows, width),
            slot_block(rows, width),
            slot_block(rows, width),
            whole(wr.shape),
            pl.BlockSpec(memory_space=pl.ANY),
        ],
        out_specs=[slot_block(rows, ff), slot_block(rows, ff)]
        + [whole((n, rows, width)) for n in sizes],
        out_shape=[
            in_hbm((count * rows, ff), BF16),
            in_hbm((count * rows, ff), BF16),
        ]
        + [jax.ShapeDtypeStruct((n, rows, width), BF16) for n in sizes],
        scratch_shapes=[
            pltpu.VMEM((width, ff), BF16),
            pltpu.VMEM((ff, width), BF16),
            pltpu.SemaphoreType.DMA((2,)),
        ],
        compiler_params=params(30),
        cost_estimate=TINY,
        name="expert_second",
    )(*placed(at, pos, xs, cs, g, ret, dx, wr, parts))


def weight_grad_kernel(ends, *refs):
    count = len(ends)
    xs, gs, gps, acts = (refs[i * count : (i + 1) * count] for i in range(4))
    out_ref, xs_t, g_t, turned = refs[4 * count :]
    step = pl.program_id(0)
    width = xs_t.shape[0]
    part, cols = width // 8, gps[0].shape[1]
    spans = list(zip((0, *ends[:-1]), ends))

    @pl.when(step == 0)
    def _():
        for (low, high), x_ref, g_ref in zip(spans, xs, gs):
            xs_t[:, low:high] = x_ref[...].T
            g_t[:, low:high] = g_ref[...].T

    up = down = None
    for (low, high), gp, act in zip(spans, gps, acts):
        one, two = dot(xs_t[:, low:high], gp[...]), dot(g_t[:, low:high], act[...])
        up, down = (one, two) if up is None else (up + one, down + two)
    turned[:width, :] = up.astype(BF16)
    block = step * cols // width
    lanes = pl.ds(pl.multiple_of(step * cols % width, cols), cols)
    into = pl.ds(pl.multiple_of(block * part, part), part)
    for index in range(8):
        out_ref[index, into, lanes] = turned[index * part : (index + 1) * part, :]
    half = cols // 2
    first = out_ref.shape[1] - half
    tall = down.T.astype(BF16)
    out_ref[2 * step, first:, :] = tall[:half]
    out_ref[2 * step + 1, first:, :] = tall[half:]


def weight_grad(xs, g, gps, acts):
    width, ff = xs[0].shape[1], gps[0].shape[1]
    cols = ff // 4
    out = (8, ff // width * (width // 8) + ff // 8, width)
    ends = []
    for gp in gps:
        ends.append(gp.shape[0] + (ends[-1] if ends else 0))
    slots = ends[-1]
    return pl.pallas_call(
        functools.partial(weight_grad_kernel, tuple(ends)),
        grid=(4,),
        in_specs=[whole(a.shape) for a in (*xs, *g)]
        + [pl.BlockSpec((a.shape[0], cols), lambda i: (0, i)) for a in (*gps, *acts)],
        out_specs=whole(out),
        out_shape=in_hbm(out, BF16),
        scratch_shapes=[
            pltpu.VMEM((width, slots), BF16),
            pltpu.VMEM((width, slots), BF16),
            pltpu.VMEM((width, cols), BF16),
        ],
        compiler_params=params(30),
        cost_estimate=TINY,
        name="weight_grad",
    )(*placed(*xs, *g, *gps, *acts))


def settle_kernel(at_ref, zero_ref, one_ref, up_ref, down_ref):
    part, units = up_ref.shape[1], zero_ref.shape[1] - 2 * up_ref.shape[1]
    for half, ref in enumerate((zero_ref, one_ref)):
        for index in range(8):
            rows = slice(index // 4 * part, index // 4 * part + part)
            to = (2 * index + half) * units
            from_ = index % 4 * units
            up_ref[0, :, to : to + units] = ref[0, rows, from_ : from_ + units].astype(F32)
        down_ref[0, half * units : (half + 1) * units, :] = ref[0, 2 * part :, :].astype(F32)


def settle_experts(at, zero, one):
    _, rows, width = zero.shape
    part = width // 8
    units = rows - 2 * part
    piece = pl.BlockSpec((1, rows, width), lambda i, at: (i ^ at[2], 0, 0))
    return pl.pallas_call(
        settle_kernel,
        grid_spec=pltpu.PrefetchScalarGridSpec(
            num_scalar_prefetch=1,
            grid=(E,),
            in_specs=[piece, piece],
            out_specs=[
                pl.BlockSpec((1, part, 16 * units), lambda i, at: (i, 0, 0)),
                pl.BlockSpec((1, 2 * units, width), lambda i, at: (i, 0, 0)),
            ],
        ),
        out_shape=[
            jax.ShapeDtypeStruct((E, part, 16 * units), F32),
            jax.ShapeDtypeStruct((E, 2 * units, width), F32),
        ],
        compiler_params=params(24),
        cost_estimate=TINY,
        name="settle_experts",
    )(*placed(at, zero, one))


def early_images(images, rows, width):
    return pl.BlockSpec((1, rows, width), lambda i: (jnp.minimum(i, images - 2), 0, 0))


def middle_back_kernel(
    filled, at_ref, a_ref, ar_ref, b_ref, br_ref, xr_ref, mid_ref, cot_ref, vec_ref, am_ref,
    got_ref, hidden_ref, wr_ref,
    gm_ref, low_ref, parts_ref, sums_ref, proj_ref, router_ref,
):
    rows, width = mid_ref.shape[1:]
    group = am_ref.shape[2]

    @pl.when(pl.program_id(0) == 0)
    def _():
        sums_ref[...] = jnp.zeros_like(sums_ref)
        proj_ref[...] = jnp.zeros_like(proj_ref)
        router_ref[...] = jnp.zeros_like(router_ref)

    last = pl.program_id(0) == pl.num_programs(0) - 1
    grad = jnp.where(
        last,
        b_ref[0].astype(F32) + br_ref[0].astype(F32),
        a_ref[0].astype(F32) + ar_ref[0].astype(F32),
    )
    grad = grad + xr_ref[0].astype(F32)
    gates = [grad[filled + 3 * e : filled + 3 * e + 3, :384] for e in range(E)]
    gates = [jnp.sum(g, axis=0, keepdims=True) for g in gates]
    gates = jnp.concatenate([jnp.zeros((4, 384), F32), *gates, jnp.zeros((120, 384), F32)], axis=0)
    gates = gates.T[:rows]
    router = routing(hidden_ref[0], wr_ref)
    mean = jnp.sum(router * gates, axis=-1, keepdims=True)
    logit_grad = (router * (gates - mean)).astype(BF16)
    row = lax.broadcasted_iota(jnp.int32, (rows, 1), 0)
    grad = jnp.where(row < filled, grad, 0.0) + dot_nt(logit_grad, wr_ref[...])
    router_ref[...] += dot_tn(hidden_ref[0], logit_grad)
    xhat, rstd = norm_parts(mid_ref[0])
    sums_ref[2:3, :] += jnp.sum(grad * xhat, axis=0, keepdims=True)
    sums_ref[3:4, :] += jnp.sum(grad, axis=0, keepdims=True)
    out = cot_ref[0].astype(F32) + norm_back(grad * vec_ref[2:3, :], xhat, rstd)
    out = jnp.where(row < filled, out, 0.0)
    gm_ref[0] = out
    low = out.astype(BF16)
    low_ref[0] = low
    proj_ref[:group, :] += dot_tn(am_ref[0], low)
    att_r = got_ref[pl.ds(pl.multiple_of(pl.program_id(0) * rows, 16), rows), :]
    proj_ref[group:, :] += dot_tn(att_r, low)

    @pl.when(pl.program_id(0) == pl.num_programs(0) - 1)
    def _():
        part = width // 8
        router = router_ref[...].T[:8]
        lines = jnp.concatenate(two_parts(sums_ref[...] + router), axis=0)
        row = lax.broadcasted_iota(jnp.int32, (width, 128), 0)
        col = lax.broadcasted_iota(jnp.int32, (width, 128), 1)
        for index in range(8):
            base = index * part
            from_ = pl.multiple_of(base ^ (at_ref[1] * group), part)
            parts_ref[index, :part, :] = proj_ref[pl.ds(from_, part), :].astype(BF16)
            pick = ((row == col + base) & (col < part)).astype(F32).astype(BF16)
            parts_ref[index, part:, :128] = dot(lines, pick).astype(BF16)
            parts_ref[index, part:, 128:] = jnp.zeros((16, width - 128), BF16)


def middle_back(at, mine, near, extra, extra_near, from_x, middle, cots, vecs, att_m, got, hidden, wr, filled):
    images, rows, width = middle.shape
    one = per_image(rows, width)
    group = att_m.shape[2]
    piece = (8, width // 8 + 16, width)
    return pl.pallas_call(
        functools.partial(middle_back_kernel, filled),
        grid=(images,),
        in_specs=[SCALARS]
        + [early_images(images, rows, width)] * 2
        + [pl.BlockSpec((1, rows, width), lambda i: (0, 0, 0))] * 2
        + [one] * 2
        + [one, whole(vecs.shape), per_image(rows, group), whole(got.shape)]
        + [one, whole(wr.shape)],
        out_specs=[one, one, whole(piece)],
        out_shape=[
            in_hbm(middle.shape, F32),
            jax.ShapeDtypeStruct(middle.shape, BF16),
            in_hbm(piece, BF16),
        ],
        scratch_shapes=[
            pltpu.VMEM((8, width), F32),
            pltpu.VMEM((width, width), F32),
            pltpu.VMEM((width, 128), F32),
        ],
        compiler_params=params(32),
        cost_estimate=TINY,
        name="middle_back",
    )(*placed(at, mine, near, extra, extra_near, from_x, middle, cots, vecs, att_m, got, hidden, wr))


def mix_kernel(
    mid_ref, a_ref, ar_ref, b_ref, br_ref, x_ref, xr_ref, mine_ref, theirs_ref, send_ref
):
    last = pl.program_id(0) == pl.num_programs(0) - 1
    total = jnp.where(
        last,
        b_ref[0].astype(F32) + br_ref[0].astype(F32),
        a_ref[0].astype(F32) + ar_ref[0].astype(F32),
    )
    total = total + mid_ref[0]
    other = x_ref[0].astype(F32) + xr_ref[0].astype(F32)
    count = mine_ref.shape[1]
    mine_ref[0] = total[:count]
    theirs_ref[0] = other[count : 2 * count]
    send_ref[0, 0] = other[:count].astype(BF16)
    send_ref[0, 1] = total[count : 2 * count].astype(BF16)


def layer_mix(at, middle, mine, near, extra, extra_near, other, other_near, quarter):
    images, rows, width = middle.shape
    one, part = per_image(rows, width), per_image(quarter, width)
    return pl.pallas_call(
        lambda at_ref, *refs: mix_kernel(*refs),
        grid=(images,),
        in_specs=[
            SCALARS,
            one,
            *[early_images(images, rows, width)] * 2,
            *[pl.BlockSpec((1, rows, width), lambda i: (1, 0, 0))] * 2,
            one,
            one,
        ],
        out_specs=[part, part, per_image(2, quarter, width)],
        out_shape=[
            in_hbm((images, quarter, width), F32),
            in_hbm((images, quarter, width), F32),
            jax.ShapeDtypeStruct((images, 2, quarter, width), BF16),
        ],
        compiler_params=params(24),
        cost_estimate=TINY,
        name="layer_mix",
    )(*placed(at, middle, mine, near, extra, extra_near, other, other_near))


def combine_kernel(at_ref, mine_ref, theirs_ref, got_ref, out_ref):
    ours = pl.program_id(0) // (pl.num_programs(0) // 2) == at_ref[2] // 2
    value = jnp.where(
        ours,
        mine_ref[0] + got_ref[0, 0].astype(F32),
        theirs_ref[0] + got_ref[0, 1].astype(F32),
    )
    out_ref[0] = value.astype(BF16)


def layer_combine(at, mine, theirs, got):
    half, quarter, width = mine.shape

    def image(i, at):
        return (jnp.where(i < half, i, (i + half - 1) % half), 0, 0)

    part = pl.BlockSpec((1, quarter, width), image)
    return pl.pallas_call(
        combine_kernel,
        grid_spec=pltpu.PrefetchScalarGridSpec(
            num_scalar_prefetch=1,
            grid=(2 * half,),
            in_specs=[
                part,
                part,
                pl.BlockSpec((1, 2, quarter, width), lambda i, at: (*image(i, at), 0)),
            ],
            out_specs=pl.BlockSpec((1, quarter, width), lambda i, at: (i, 0, 0)),
        ),
        out_shape=jax.ShapeDtypeStruct((2 * half, quarter, width), BF16),
        compiler_params=params(24),
        cost_estimate=TINY,
        name="layer_combine",
    )(*placed(at, mine, theirs, got))


def attend_back_kernel(
    head_dim, at_ref, lm_ref, lo_ref, pm_ref, qkv_ref, lse_ref, bias_ref, h1_ref, wq_ref,
    dm_ref, do_ref, gq_ref, grad_ref, low_ref,
):
    rows = lm_ref.shape[1]
    low_ref[:rows, :] = lm_ref[0]
    low_ref[rows:, :] = lo_ref[0]
    out_grad = dot_nt(low_ref[...], pm_ref[...]).astype(BF16)
    width = pm_ref.shape[0]
    bias = bias_ref[0]
    lane = lax.broadcasted_iota(jnp.int32, (1, 128), 1)
    sub = lax.broadcasted_iota(jnp.int32, (128, 1), 0)
    scaling = 1.0 / math.sqrt(head_dim)
    for pair in range(width // 128):
        cols = slice(pair * 128, pair * 128 + 128)
        k_cols = slice(width + pair * 128, width + pair * 128 + 128)
        v_cols = slice(2 * width + pair * 128, 2 * width + pair * 128 + 128)
        q2, k2, v2 = qkv_ref[0, :, cols], qkv_ref[0, :, k_cols], qkv_ref[0, :, v_cols]
        o2 = out_grad[:, cols]
        k_t = k2.T
        dv = dk = None
        both = []
        for part in range(2):
            mine = (lane >= head_dim * part) & (lane < head_dim * (part + 1))
            qm = jnp.where(mine, q2, jnp.zeros_like(q2))
            om = jnp.where(mine, o2, jnp.zeros_like(o2))
            head = 2 * pair + part
            probs = jnp.exp(dot_nt(k2, qm) + bias - lse_ref[0, head : head + 1, :])
            prob_grad = dot_nt(v2, om)
            delta = jnp.sum(probs * prob_grad, axis=0, keepdims=True)
            score_grad = (probs * (prob_grad - delta)).astype(BF16)
            dv_part = dot(probs.astype(BF16), om)
            dk_part = dot(score_grad, qm)
            dv = dv_part if dv is None else dv + dv_part
            dk = dk_part if dk is None else dk + dk_part
            both.append(dot(k_t, score_grad))
        dq = (jnp.where(sub < head_dim, both[0], both[1]) * scaling).astype(BF16).T
        grad_ref[:, cols] = dq
        grad_ref[:, k_cols] = dk.astype(BF16)
        grad_ref[:, v_cols] = dv.astype(BF16)
    hidden_grad = dot_nt(grad_ref[...], wq_ref[...]).astype(BF16)
    dm_ref[0] = hidden_grad[:rows]
    do_ref[0] = hidden_grad[rows:]
    grad_qkv = dot_tn(h1_ref[0], grad_ref[...])

    @pl.when(pl.program_id(0) == 0)
    def _():
        gq_ref[...] = grad_qkv

    @pl.when(pl.program_id(0) > 0)
    def _():
        gq_ref[...] += grad_qkv


def attend_back(at, low_m, low_o, proj_m, qkv, lse, bias, hidden_one, wq, head_dim):
    images, rows, width = low_m.shape
    group = proj_m.shape[0]
    return pl.pallas_call(
        functools.partial(attend_back_kernel, head_dim),
        grid=(images,),
        in_specs=[
            SCALARS,
            per_image(rows, width),
            per_image(rows, width),
            whole(proj_m.shape),
            per_image(2 * rows, 3 * group),
            per_image(8, 2 * rows),
            per_image(2 * rows, 1),
            per_image(2 * rows, width),
            whole(wq.shape),
        ],
        out_specs=[
            per_image(rows, width),
            per_image(rows, width),
            whole((width, 3 * group)),
        ],
        out_shape=[
            in_hbm((images, rows, width), BF16),
            jax.ShapeDtypeStruct((images, rows, width), BF16),
            in_hbm((width, 3 * group), F32),
        ],
        scratch_shapes=[
            pltpu.VMEM((2 * rows, 3 * group), BF16),
            pltpu.VMEM((2 * rows, width), BF16),
        ],
        compiler_params=params(48),
        cost_estimate=TINY,
        name="attend_back",
    )(*placed(at, low_m, low_o, proj_m, qkv, lse, bias, hidden_one, wq))


def input_back_kernel(
    x_ref, gm_ref, vec_ref, a_ref, ar_ref, gq_ref, r_ref,
    out_ref, go_ref, parts_ref, sums_ref,
):
    step, images = pl.program_id(0), pl.num_programs(0)
    grad = a_ref[0].astype(F32) + ar_ref[0].astype(F32)
    xhat, rstd = norm_parts(x_ref[0].astype(F32))
    out = gm_ref[0] + norm_back(grad * vec_ref[0:1, :], xhat, rstd)
    count = out_ref.shape[1]
    out_ref[0] = out[:count]
    go_ref[0] = out[count : 2 * count].astype(BF16)

    @pl.when(step == 0)
    def _():
        sums_ref[...] = jnp.zeros_like(sums_ref)

    sums_ref[0:1, :] += jnp.sum(grad * xhat, axis=0, keepdims=True)
    sums_ref[1:2, :] += jnp.sum(grad, axis=0, keepdims=True)

    @pl.when(step == images - 1)
    def _():
        total = gq_ref[...]
        width = grad.shape[1]
        part = width // 8
        lines = jnp.concatenate(two_parts(sums_ref[...]), axis=0)
        row = lax.broadcasted_iota(jnp.int32, (width, 128), 0)
        col = lax.broadcasted_iota(jnp.int32, (width, 128), 1)
        for index in range(8):
            base = index * part
            own = total[base : base + part].astype(BF16)
            half = jnp.concatenate([own[: part // 2, width:], own[part // 2 :, width:]], axis=1)
            pick_line = ((row == col + base) & (col < part)).astype(F32).astype(BF16)
            line = dot(lines, pick_line).astype(BF16)
            tail = jnp.concatenate([line, jnp.zeros((16, width - 128), BF16)], axis=1)
            block = jnp.concatenate([own[:, :width], half], axis=0)
            last = part + block.shape[0]
            parts_ref[index, part:last] = block
            parts_ref[index, last + 16 :] = tail

        last = parts_ref.shape[1] - 32
        parts_ref[:, :part] = r_ref[:, :part]
        parts_ref[:, last : last + 16] = r_ref[:, part:]


def input_back(x_own, grad_middle, vecs, mine, near, grads, r_parts, quarter):
    images, rows, width = x_own.shape
    one, part = per_image(rows, width), per_image(quarter, width)
    more = r_parts.shape[1] + width // 8 + (grads.shape[1] - width) * (width // 8) // width + 16
    more = (8, more, width)
    return pl.pallas_call(
        input_back_kernel,
        grid=(images,),
        in_specs=[one, one, whole(vecs.shape), one, one, whole(grads.shape), whole(r_parts.shape)],
        out_specs=[part, part, whole(more)],
        out_shape=[
            jax.ShapeDtypeStruct((images, quarter, width), F32),
            jax.ShapeDtypeStruct((images, quarter, width), BF16),
            in_hbm(more, BF16),
        ],
        scratch_shapes=[pltpu.VMEM((8, width), F32)],
        compiler_params=params(32),
        cost_estimate=TINY,
        name="input_back",
    )(*placed(x_own, grad_middle, vecs, mine, near, grads, r_parts))


def shards(
    tokens,
    key_mask,
    expert_ids,
    ln1_gain,
    ln1_bias,
    qkv_weight,
    proj_weight,
    ln2_gain,
    ln2_bias,
    router_weight,
    up_weight,
    down_weight,
    cotangent,
):
    n_seq, n_wide = lax.axis_size("seq"), lax.axis_size("wide")
    images, quarter, width = tokens.shape
    head_dim = width // H
    group = width // 2
    filled = 2 * quarter
    rows = -(-(filled + 3 * E) // 16) * 16
    place = lax.axis_index("seq")
    chip, core = place // 2, place % 2
    direct = n_wide == 8
    spot = lax.axis_index("wide") if direct else 0
    at = jnp.stack([jnp.int32(spot), core, place, jnp.int32(spot) % 2])
    part = width // 8

    def over_seq(a, turn):
        return lax.ppermute(a, "seq", [(i, i ^ turn) for i in range(n_seq)])

    def over_x(a):
        return over_seq(a, 2)

    def over_core(a):
        return over_seq(a, 1)

    def over_wide(a, turn):
        return lax.ppermute(a, "wide", [(i, i ^ turn) for i in range(n_wide)])

    def after(value, *first):
        return lax.optimization_barrier((value, *first))[0]

    def images_of(a, of_chip):
        pair = lax.dynamic_slice_in_dim(a, of_chip * (images - 2), 2, 0)
        single = lax.dynamic_slice_in_dim(a, images // 2 - 1 + of_chip, 1, 0)
        return jnp.concatenate([pair, single], axis=0)

    def joined(first, second):
        both = jnp.concatenate([first, second], axis=1)
        return jnp.pad(both, ((0, 0), (0, rows - filled)) + ((0, 0),) * (both.ndim - 2))

    def cells(quarters, of_chip, of_core):
        first = lax.dynamic_index_in_dim(quarters, 2 * of_chip + of_core, 1, False)
        second = lax.dynamic_index_in_dim(quarters, 2 * (1 - of_chip) + of_core, 1, False)
        return joined(images_of(first, of_chip), images_of(second, of_chip))

    mask = key_mask.reshape(images, n_seq, quarter)
    valid = jnp.concatenate([cells(mask, chip, core), cells(mask, chip, 1 - core)], axis=1)
    bias = jnp.where(valid > 0, 0.0, BIG).astype(F32)[..., None]

    def heads_of(a):
        return jnp.concatenate(
            [lax.dynamic_slice_in_dim(a, (2 * i + core) * group, group, 1) for i in range(3)],
            axis=1,
        )

    wq = heads_of(qkv_weight)
    proj = lax.dynamic_slice_in_dim(proj_weight, core * group, group, 1)
    lines = jnp.stack([ln1_gain, ln1_bias, ln2_gain, ln2_bias])
    lines = jnp.concatenate([lines, router_weight.T], axis=0)
    up = lax.dynamic_index_in_dim(up_weight, place, 0, False)
    down = lax.dynamic_index_in_dim(down_weight, place, 0, False)
    units = down.shape[0] // 2

    def first_parts(wq, proj, lines):
        both = jnp.concatenate([wq, proj], axis=1)
        fill = ((0, 16 - lines.shape[0]), (0, both.shape[1] - lines.shape[1]))
        return jnp.concatenate([both, jnp.pad(lines, fill)], axis=0)

    def half_of(up, down, half):
        cols = up.reshape(up.shape[0], n_wide, 2, units)[:, :, half].reshape(up.shape[0], -1)
        down = down.reshape(-1, 2, units, width)[:, half].reshape(-1, width)
        blocks = [cols[:, i : i + width] for i in range(0, cols.shape[1], width)]
        return jnp.concatenate([*blocks, down], axis=0)

    one_all = first_parts(wq, proj, lines)
    one_all = jnp.broadcast_to(one_all[None], (4, *one_all.shape))
    codes = (expert_ids[..., 0] * E + expert_ids[..., 1]).astype(BF16)
    codes = jnp.pad(codes, ((0, 0), (0, width - quarter)))[:, None, :]
    cot = jnp.concatenate([cotangent, codes], axis=1)
    x_got = over_x(images_of(after(tokens, one_all), 1 - chip))
    x_own = joined(images_of(tokens, chip), x_got)
    x_oth = over_core(after(x_own, bias, cot))
    cot_got = over_x(after(cot, x_got))

    z_groups = [[y + 2 * z for z in range(4)] for y in range(2)]

    def all_of(a, axis=0):
        return lax.all_gather(a, "wide", axis=axis, tiled=True)

    if direct:
        ones = lax.all_to_all(one_all, "wide", 0, 0, axis_index_groups=z_groups, tiled=True)
        ones_y = over_wide(ones, 1)
        twos, threes = (
            lax.all_gather(after(half_of(up, down, half), ones, x_oth), "wide") for half in range(2)
        )
    else:

        def eight(a, axis=0):
            return jnp.split(a, 8, axis=axis)

        ones = jnp.stack([first_parts(*a) for a in zip(eight(all_of(wq)), eight(all_of(proj)), eight(all_of(lines, 1), 1))])
        ones, ones_y = ones[::2], ones[1::2]
        ups, downs = eight(all_of(up)), eight(all_of(down))
        twos, threes = (
            jnp.stack([half_of(a, b, half) for a, b in zip(ups, downs)]) for half in range(2)
        )

    att_m, mail, qkv, hidden_one, lse, wq, small, vecs = attend(
        at, x_own, x_oth, bias, ones, ones_y, head_dim
    )
    mail_got = over_core(mail)
    middle, hidden_two, proj_m = project(at, att_m, mail, mail_got, x_own, vecs)
    cots_m = join_cots(at, cot, after(cot_got, hidden_two), rows)
    cots_o = over_core(cots_m)
    hidden_b = over_x(hidden_two)
    hidden_c = over_core(hidden_two)
    ours = (hidden_two, None, hidden_c, None)
    *first_a, gu_a, gd_a = expert_first(
        at, ours, (cots_m, cots_o), small, twos, filled, EARLY, len(BLOCKS) - EARLY
    )
    hidden_d = over_core(after(hidden_b, gu_a))
    hidden = (hidden_two, hidden_b, hidden_c, hidden_d)
    *first_b, parts0 = expert_first(
        at, hidden, (cots_m, cots_o), small, twos, filled, 0, EARLY, (gu_a, gd_a)
    )
    act1, gp1, dh_m, dh_o, ret_m, ret_o, extra_m, extra_o = expert_second(
        after(at, parts0), first_b, small, threes, filled
    )
    dh_r = over_core(dh_o)
    dh_b = dh_m + dh_r
    dh_x = over_x(dh_b)
    ret_r = over_core(ret_o)
    def over_y(send, keep, *first):
        if not direct:
            return jnp.stack([keep, send], axis=1)
        got = over_wide(send, 1)
        return after(keep, *first) + after(got, *first)

    def over_z(both):
        return lax.all_to_all(both, "wide", 0, 0, axis_index_groups=z_groups, tiled=True)

    def expert_sum(both):
        both = both.reshape(8, -1, width)
        cut = 2 * part
        cols = jnp.moveaxis(both[:, :cut].reshape(8, 2, part, width), 1, 2).reshape(width, -1)
        rows = both[:, cut:].reshape(-1, width)
        return tuple(
            lax.psum_scatter(a, "wide", scatter_dimension=0, tiled=True) for a in (cols, rows)
        )

    def near_pair(a):
        return jnp.stack([a, over_core(a)])

    def near_experts(pairs):
        return jnp.concatenate([pairs, over_x(pairs)], axis=0)

    extra_r = over_core(extra_o)
    act2, gp2, late_m, late_o, late_ret_m, late_ret_o = expert_second(
        after(at, dh_b), first_a, small, threes, filled
    )
    late_r = over_core(late_o)
    late_ret_r = over_core(late_ret_o)
    if direct:
        sum0 = lax.all_to_all(parts0, "wide", 0, 0, tiled=True)

    xs = (first_b[1], first_a[1])
    parts1 = weight_grad(xs, (first_b[3], first_a[3]), [gp1, gp2], [act1, act2])
    layer_mine, layer_theirs, layer_send = layer_mix(
        after(at, parts1), middle, late_ret_m, late_ret_r, extra_m, extra_r, ret_m, ret_r, quarter
    )
    layer_got = over_x(after(layer_send, dh_x))

    grad_middle, low_m, r_parts = middle_back(
        at,
        late_m,
        late_r,
        extra_m,
        extra_r,
        dh_x,
        middle,
        cots_m,
        vecs,
        att_m,
        mail_got,
        hidden_two,
        small,
        filled,
    )
    low_o = over_core(low_m)
    if direct:
        sum1 = lax.all_to_all(after(parts1, dh_x, layer_send), "wide", 0, 0, tiled=True)
    dh1_m, dh1_o, grad_qkv = attend_back(
        at, low_m, low_o, proj_m, qkv, lse, bias, hidden_one, wq, head_dim
    )
    dh1_o = after(dh1_o, layer_got)
    dh1_r = over_core(dh1_o)
    input_mine, input_send, q_parts = input_back(
        x_own, grad_middle, vecs, dh1_m, dh1_r, grad_qkv, r_parts, quarter
    )
    last = q_parts.shape[1] - 32
    input_got = over_x(input_send)
    if direct:
        rest = lax.all_to_all(q_parts, "wide", 0, 0, tiled=True)
        sum0, sum1 = (
            jnp.sum(after(a, q_parts).astype(F32), axis=0).astype(BF16) for a in (sum0, sum1)
        )
        near0, near1 = near_experts(near_pair(sum0)), near_experts(after(near_pair(sum1), input_got))
    else:
        sum0 = expert_sum(parts0)
        sum1 = expert_sum(parts1)

    def settle(mine, got):
        got = got.astype(mine.dtype)
        pair, rest = slice(0, 2), slice(2, 3)
        return jnp.where(
            chip == 0,
            jnp.concatenate([mine[pair], mine[rest], got[rest], got[pair]], axis=0),
            jnp.concatenate([got[pair], got[rest], mine[rest], mine[pair]], axis=0),
        )

    input_grad = settle(input_mine, input_got)
    if not direct:

        def in_order(a):
            four = near_experts(near_pair(a))
            return jnp.stack(
                [lax.dynamic_index_in_dim(four, place ^ e, 0, False) for e in range(E)]
            ).astype(F32)

        up0, up1, down0, down1 = (in_order(s[i]) for i in range(2) for s in (sum0, sum1))
        halves = [a.reshape(E, -1, n_wide, units) for a in (up0, up1)]
        grad_up = jnp.stack(halves, axis=3).reshape(E, -1, up.shape[1])
        grad_down = jnp.concatenate([down0, down1], axis=1)

    def over_seq_group(rows, lines):
        count = rows.shape[0]

        def sent(over, rows, lines):
            got = over(jnp.concatenate([rows.astype(BF16), *two_parts(lines)])).astype(F32)
            low = got[count : count + lines.shape[0]] + got[count + lines.shape[0] :]
            return got[:count], lines + low

        got, lines = sent(over_x, rows, lines)
        rows = rows + got
        other, lines = sent(over_core, rows, lines)
        return rows, other, lines

    owned = proj_weight.shape[0]
    if direct:
        rest = after(rest, input_got)
        rest = jnp.sum(rest.astype(F32), axis=0)
        rows, lines = rest[:last], rest[last:].reshape(2, 2, 8, width)
        lines = jnp.sum(lines, axis=1).reshape(16, width)
    else:
        both = q_parts.astype(F32)
        rows = [both[:, :part], both[:, part : 2 * part]]
        halves = both[:, 2 * part : last].reshape(8, -1, 2, group)
        rows.append(jnp.moveaxis(halves, 2, 1).reshape(8, part, group))
        for low in (last, last + 16):
            two = both[:, low : low + 8, :part] + both[:, low + 8 : low + 16, :part]
            rows.append(jnp.moveaxis(two, 1, 2))
        rows = jnp.concatenate(rows, axis=2).reshape(width, -1)
        rows = lax.psum_scatter(rows, "wide", scatter_dimension=0, tiled=True)
        lines = jnp.pad(rows[:, -16:].T, ((0, 0), (0, width - owned)))
        more = rows[:, 2 * width : -16]
        more = jnp.concatenate([more[: owned // 2], more[owned // 2 :]], axis=1)
        rows = jnp.concatenate([rows[:, :width], rows[:, width : 2 * width], more])
    total, other, lines = over_seq_group(rows, lines)
    if direct:
        grad_up, grad_down = settle_experts(after(at, rows), near0, near1)
    layer_out = layer_combine(after(at, q_parts), layer_mine, layer_theirs, layer_got)
    grad_proj = total[:owned] + other[:owned]

    def thirds(a):
        more = a[2 * owned :]
        more = jnp.concatenate([more[:, :group], more[:, group:]])
        return [a[owned : 2 * owned, :group], a[owned : 2 * owned, group:], more]

    lines = lines[:, :owned]
    pairs = zip(thirds(total), thirds(other))
    ordered = [(jnp.where(core == 0, a, b), jnp.where(core == 0, b, a)) for a, b in pairs]
    grad_qkv = jnp.concatenate([a for pair in ordered for a in pair], axis=1)
    return (
        layer_out,
        input_grad,
        lines[8],
        lines[9],
        grad_qkv,
        grad_proj,
        lines[2],
        lines[3],
        lines[4 : 4 + E].T,
        grad_up,
        grad_down,
    )


def solution(mesh):
    placed = (
        P("wide", "seq", None),
        P("wide", None),
        P("wide", "seq", None),
        P("wide"),
        P("wide"),
        P("wide", None),
        P("wide", None),
        P("wide"),
        P("wide"),
        P("wide", None),
        P(None, "wide", None),
        P(None, "wide", None),
        P("wide", "seq", None),
    )
    return jax.shard_map(
        shards,
        mesh=mesh,
        in_specs=placed,
        out_specs=(
            P("wide", "seq", None),
            P("wide", "seq", None),
            P("wide"),
            P("wide"),
            P("wide", None),
            P("wide", None),
            P("wide"),
            P("wide"),
            P("wide", None),
            P(None, "wide", None),
            P(None, "wide", None),
        ),
        check_vma=False,
    )
```

```python
import functools
import math

import jax
import jax.numpy as jnp
from jax import lax
from jax.experimental import pallas as pl
from jax.experimental.pallas import tpu as pltpu
from jax.sharding import PartitionSpec as P

H = 8
E = 4
EPSILON = 1e-06
BIG = -1e30
MIB = 1024 * 1024
F32 = jnp.float32
BF16 = jnp.bfloat16


def dot(a, b, dims=((1,), (0,))):
    return lax.dot_general(a, b, (dims, ((), ())), preferred_element_type=F32)


def dot_nt(a, b):
    return dot(a, b, ((1,), (1,)))


def dot_tn(a, b):
    return dot(a, b, ((0,), (0,)))


def norm_parts(values):
    center = values - jnp.mean(values, axis=-1, keepdims=True)
    spread = jnp.mean(center * center, axis=-1, keepdims=True)
    rstd = lax.rsqrt(spread + EPSILON)
    return center * rstd, rstd


def norm_back(grad, xhat, rstd):
    return rstd * (
        grad
        - jnp.mean(grad, axis=-1, keepdims=True)
        - xhat * jnp.mean(grad * xhat, axis=-1, keepdims=True)
    )


TINY = pl.CostEstimate(flops=1000, bytes_accessed=1000, transcendentals=0)


def params(limit, **more):
    return pltpu.CompilerParams(vmem_limit_bytes=limit * MIB, **more)


def placed(*arrays, free=()):
    return [
        pltpu.with_memory_space_constraint(a, pltpu.HBM)
        if a.size > 1 << 15 and not any(a is f for f in free)
        else a
        for a in arrays
    ]


def in_hbm(shape, dtype):
    return pltpu.HBM(shape, dtype)


def whole(shape):
    return pl.BlockSpec(shape, lambda *_: (0,) * len(shape))


def per_image(*shape):
    return pl.BlockSpec((1, *shape), lambda i: (i,) + (0,) * len(shape))


SCALARS = pl.BlockSpec(memory_space=pltpu.SMEM)


def attend_kernel(
    images, head_dim, at_ref, own_ref, oth_ref, bias_ref, here_ref, there_ref,
    att_m_ref, mail_ref, qkv_ref, hidden_ref, lse_ref, wq_ref, small_ref, vec_ref,
):
    rows = own_ref.shape[1]
    features = wq_ref.shape[0]

    @pl.when(pl.program_id(0) == 0)
    def _():
        part = features // 8
        vec = jnp.zeros((8, features), F32)
        row = lax.broadcasted_iota(jnp.int32, (part, features), 0)
        col = lax.broadcasted_iota(jnp.int32, (part, features), 1)
        for index in range(8):
            side = at_ref[3] if index % 2 == 0 else 1 - at_ref[3]
            ref = (here_ref, there_ref)[index % 2].at[index // 2]
            base = pl.multiple_of((index // 2 * 2 + side) * part, part)
            wq_ref[pl.ds(base, part), :] = ref[:part, : wq_ref.shape[1]]
            mail_ref[pl.ds(images * rows + base, part), :] = ref[:part, wq_ref.shape[1] :]
            spread = (col == row + base).astype(F32).astype(BF16)
            vec = vec + dot(ref[part:, :part], spread)[:8]
        vec_ref[...] = vec
        tall = jnp.concatenate([vec, jnp.zeros((120, features), F32)], axis=0)
        small_ref[...] = tall.T.astype(BF16)

    gain, offset = vec_ref[0:1, :], vec_ref[1:2, :]
    for half, ref in enumerate((own_ref, oth_ref)):
        xhat, _ = norm_parts(ref[0].astype(F32))
        hidden_ref[0, half * rows : (half + 1) * rows, :] = (xhat * gain + offset).astype(BF16)
    width = wq_ref.shape[1] // 3
    packed = dot(hidden_ref[0], wq_ref[...]).astype(BF16)
    scaling = 1.0 / math.sqrt(head_dim)
    qkv_ref[0, :, :width] = (packed[:, :width].astype(F32) * scaling).astype(BF16)
    qkv_ref[0, :, width:] = packed[:, width:]
    bias = bias_ref[0]
    lane = lax.broadcasted_iota(jnp.int32, (1, 128), 1)
    sub = lax.broadcasted_iota(jnp.int32, (128, 1), 0)
    for pair in range(width // 128):
        cols = slice(pair * 128, pair * 128 + 128)
        q2 = qkv_ref[0, :, cols]
        k2 = qkv_ref[0, :, width + pair * 128 : width + pair * 128 + 128]
        v2 = qkv_ref[0, :, 2 * width + pair * 128 : 2 * width + pair * 128 + 128]
        v_t = v2.T
        both = []
        for part in range(2):
            mine = (lane >= head_dim * part) & (lane < head_dim * (part + 1))
            qm = jnp.where(mine, q2, jnp.zeros_like(q2))
            scores = dot_nt(k2, qm) + bias
            peak = jnp.max(scores, axis=0, keepdims=True)
            expo = jnp.exp(scores - peak)
            total = jnp.sum(expo, axis=0, keepdims=True)
            lse_ref[0, 2 * pair + part : 2 * pair + part + 1, :] = peak + jnp.log(total)
            both.append(dot(v_t, (expo * (1.0 / total)).astype(BF16)))
        out = jnp.where(sub < head_dim, both[0], both[1]).astype(BF16).T
        att_m_ref[0, :, cols] = out[:rows]
        mail_ref[pl.ds(pl.multiple_of(pl.program_id(0) * rows, 16), rows), cols] = out[rows:]


def attend(at, x_own, x_oth, bias, here, there, head_dim):
    images, rows, width = x_own.shape
    group = width // 2
    return pl.pallas_call(
        functools.partial(attend_kernel, images, head_dim),
        grid=(images,),
        in_specs=[
            SCALARS,
            per_image(rows, width),
            per_image(rows, width),
            per_image(2 * rows, 1),
            whole(here.shape),
            whole(there.shape),
        ],
        out_specs=[
            per_image(rows, group),
            whole((images * rows + width, group)),
            per_image(2 * rows, 3 * group),
            per_image(2 * rows, width),
            per_image(8, 2 * rows),
            whole((width, 3 * group)),
            whole((width, 128)),
            whole((8, width)),
        ],
        out_shape=[
            jax.ShapeDtypeStruct((images, rows, group), BF16),
            jax.ShapeDtypeStruct((images * rows + width, group), BF16),
            in_hbm((images, 2 * rows, 3 * group), BF16),
            in_hbm((images, 2 * rows, width), BF16),
            in_hbm((images, 8, 2 * rows), F32),
            in_hbm((width, 3 * group), BF16),
            in_hbm((width, 128), BF16),
            jax.ShapeDtypeStruct((8, width), F32),
        ],
        compiler_params=params(40),
        cost_estimate=TINY,
        name="attend",
    )(*placed(at, x_own, x_oth, bias, here, there, free=(x_oth, there)))


def project_kernel(
    at_ref, att_m_ref, sent_ref, got_ref, x_ref, vec_ref, middle_ref, hidden_ref, proj_ref
):
    rows, group = att_m_ref.shape[1:]
    core, first = at_ref[1], pl.num_programs(0) * rows
    mine = pl.ds(pl.multiple_of(core * group + first, 16), group)
    other = pl.ds(pl.multiple_of((1 - core) * group + first, 16), group)

    def in_order(a, b):
        return jnp.concatenate([jnp.where(core == 0, a, b), jnp.where(core == 0, b, a)], axis=1)

    @pl.when(pl.program_id(0) == 0)
    def _():
        proj_ref[...] = in_order(sent_ref[mine, :], got_ref[mine, :])

    att_r = got_ref[pl.ds(pl.multiple_of(pl.program_id(0) * rows, 16), rows), :]
    halves = [
        dot(att_m_ref[0], ref[mine, :]) + dot(att_r, ref[other, :]) for ref in (sent_ref, got_ref)
    ]
    middle = x_ref[0].astype(F32) + in_order(*halves)
    middle_ref[0] = middle
    xhat, _ = norm_parts(middle)
    hidden_ref[0] = (xhat * vec_ref[2:3, :] + vec_ref[3:4, :]).astype(BF16)


def project(at, att_m, sent, got, x_own, vecs):
    images, rows, width = x_own.shape
    group = att_m.shape[2]
    return pl.pallas_call(
        project_kernel,
        grid=(images,),
        in_specs=[
            SCALARS,
            per_image(rows, group),
            whole(sent.shape),
            whole(got.shape),
            per_image(rows, width),
            whole(vecs.shape),
        ],
        out_specs=[per_image(rows, width), per_image(rows, width), whole((group, width))],
        out_shape=[
            in_hbm(x_own.shape, F32),
            jax.ShapeDtypeStruct(x_own.shape, BF16),
            in_hbm((group, width), BF16),
        ],
        compiler_params=params(24),
        cost_estimate=TINY,
        name="project",
    )(*placed(at, att_m, sent, got, x_own, vecs, free=(got,)))


def join_kernel(at_ref, cot_ref, got_ref, out_ref):
    images, rows, width = out_ref.shape
    half, count = images // 2, cot_ref.shape[1] - 1
    start = count // 16 * 16
    for index in range(images):
        chip = (at_ref[2] // 2 + index // half) % 2
        k = index % half
        image = chip * (images - 2) + k if k < half - 1 else half - 1 + chip
        refs = (cot_ref, got_ref) if index < half else (got_ref, cot_ref)
        first, second = (ref[image] for ref in refs)
        second = second.astype(F32)
        out_ref[index, :start, :] = first[:start]
        tail = first[start:].astype(F32)
        codes = jnp.concatenate(
            [
                tail[count - start :, :count],
                second[count:, :count],
                jnp.zeros((1, width - 2 * count), F32),
            ],
            axis=1,
        )
        fill = jnp.zeros((rows - 2 * count - 1, width), F32)
        rest = jnp.concatenate([tail[: count - start], second[:count], codes, fill], axis=0)
        out_ref[index, start:, :] = rest.astype(BF16)


def join_cots(at, cot, got, rows):
    images, _, width = cot.shape
    return pl.pallas_call(
        join_kernel,
        in_specs=[SCALARS, *[pl.BlockSpec(memory_space=pltpu.VMEM)] * 2],
        out_specs=pl.BlockSpec(memory_space=pltpu.VMEM),
        out_shape=jax.ShapeDtypeStruct((images, rows, width), BF16),
        compiler_params=params(16),
        cost_estimate=TINY,
        name="join_cots",
    )(at, cot, got)


BLOCKS = (
    ((1, 0), (1, 1)),
    ((3, 0), (3, 1)),
    ((1, 2), (0, 2)),
    ((3, 2), (2, 2)),
    ((0, 0), (0, 1)),
    ((2, 0), (2, 1)),
)
EARLY = 4


def load_weights(parts_ref, up_ref, down_ref, sem):
    part = up_ref.shape[0] // 8
    width, units = down_ref.shape[1], up_ref.shape[1] // 8
    copies = []
    for index in range(8):
        base = slice(index * part, index * part + part)
        for block in range(up_ref.shape[1] // width):
            copies.append(
                pltpu.make_async_copy(
                    parts_ref.at[index, block * part : (block + 1) * part, :],
                    up_ref.at[base, block * width : (block + 1) * width],
                    sem.at[0],
                )
            )
        base = slice(index * units, (index + 1) * units)
        first = up_ref.shape[1] // width * part
        copies.append(
            pltpu.make_async_copy(
                parts_ref.at[index, first : first + units, :], down_ref.at[base, :], sem.at[1]
            )
        )
    return copies


def hidden_units(splits, xs, g_ref, up_ref, down_ref, act_ref, gp_ref):
    ff = up_ref.shape[1]
    chunk = ff // splits
    ret = dx = None
    for part in range(splits):
        cols = slice(part * chunk, (part + 1) * chunk)
        pre = dot(xs, up_ref[:, cols])
        back = dot_nt(g_ref[...], down_ref[cols, :])
        cdf = 0.5 + 0.5 * lax.erf(pre * math.sqrt(0.5))
        pdf = jnp.exp(-0.5 * pre * pre) * (1.0 / math.sqrt(2.0 * math.pi))
        act = (pre * cdf).astype(BF16)
        gp = (back * (cdf + pre * pdf)).astype(BF16)
        act_ref[:, cols] = act
        gp_ref[:, cols] = gp
        ret_part = dot(act, down_ref[cols, :])
        dx_part = dot_nt(gp, up_ref[:, cols])
        ret = ret_part if ret is None else ret + ret_part
        dx = dx_part if dx is None else dx + dx_part
    return ret, dx


def routing(hidden, wr_ref):
    logits = dot(hidden, wr_ref[...])
    lane = lax.broadcasted_iota(jnp.int32, (1, 128), 1)
    logits = jnp.where((lane >= 4) & (lane < 4 + E), logits, BIG)
    grown = jnp.exp(logits - jnp.max(logits, axis=-1, keepdims=True))
    return grown / jnp.sum(grown, axis=-1, keepdims=True)


def weight_of(hidden, wr_ref, mine):
    lane = lax.broadcasted_iota(jnp.int32, (1, 128), 1)
    router = jnp.where(lane == 4 + mine, routing(hidden, wr_ref), 0.0)
    return jnp.sum(router, axis=-1, keepdims=True)


def two_parts(values):
    high = values.astype(BF16)
    return high, (values - high.astype(F32)).astype(BF16)


def expert_first_kernel(
    splits, filled, blocks, kinds, at_ref, wr_ref, parts_ref, *refs
):
    step = pl.program_id(0)
    hs = dict(zip(kinds, refs))
    cots = refs[len(kinds) : len(kinds) + 2]
    cs = {k: cots[k // 2].at[pl.ds(k % 2 * (cots[0].shape[0] // 2), cots[0].shape[0] // 2)] for k in kinds}
    refs = refs[len(kinds) + 2 :]
    *refs, up_ref, down_ref, sem, piece_ref, piece_sem, act_ref, gp_ref, gu_ref, gd_ref = refs
    late = len(blocks) == EARLY
    if late:
        gu_in, gd_in, pos_ref, xs_ref, cs_ref, g_ref, ret_ref, dx_ref, out_ref = refs
    else:
        pos_ref, xs_ref, cs_ref, g_ref, ret_ref, dx_ref, gu_out, gd_out = refs
    rows = xs_ref.shape[0]
    mine = at_ref[2]

    def pieces_of(number):
        copies = []
        for k, (piece, image) in enumerate(blocks[number]):
            for j, kind in enumerate((hs, cs)):
                spot = number * 4 + 2 * k + j
                copies.append(
                    pltpu.make_async_copy(
                        kind[piece].at[image], piece_ref.at[spot], piece_sem.at[number]
                    )
                )
        return copies

    def sum_copies():
        return [
            pltpu.make_async_copy(gu_in, gu_ref, sem.at[2]),
            pltpu.make_async_copy(gd_in, gd_ref, sem.at[3]),
        ]

    def copies():
        return load_weights(parts_ref, up_ref, down_ref, sem)

    @pl.when(step == 0)
    def _():
        for number in range(len(blocks)):
            for copy in pieces_of(number):
                copy.start()
            if number == 0:
                for copy in copies():
                    copy.start()
        if late:
            for copy in sum_copies():
                copy.start()

    token = lax.broadcasted_iota(jnp.int32, (1, rows), 1)
    slot = lax.broadcasted_iota(jnp.int32, (rows, rows), 0)
    before = (slot < lax.broadcasted_iota(jnp.int32, (rows, rows), 1)).astype(F32).astype(BF16)
    for number, block in enumerate(blocks):

        @pl.when(step == number)
        def _(number=number, block=block):
            for copy in pieces_of(number):
                copy.wait()
            base, xs, got = 0.0, None, None
            for k in range(2):
                spot = number * 4 + 2 * k
                code = piece_ref[spot + 1, filled // 16 * 16 : filled // 16 * 16 + 16, :rows]
                code = code.astype(F32)[filled % 16 : filled % 16 + 1, :]
                first = jnp.floor(code * (1.0 / E))
                second = code - E * first
                own = mine.astype(F32)
                named = ((first == own) | (second == own)) & (token < filled)
                flag = jnp.where(named, 1.0, 0.0)
                rank = dot(jnp.broadcast_to(flag, (16, rows)).astype(BF16), before)[0:1, :] + base
                rank = jnp.where(named, rank, -1.0)
                base = base + jnp.sum(flag, axis=-1, keepdims=True)
                pos_ref[k : k + 1, :] = rank
                pick = (slot.astype(F32) == rank).astype(F32).astype(BF16)
                a, b = dot(pick, piece_ref[spot]), dot(pick, piece_ref[spot + 1])
                xs, got = (a, b) if xs is None else (xs + a, got + b)
            xs_ref[...] = xs.astype(BF16)
            cs_ref[...] = got.astype(BF16)

    xs = xs_ref[...]
    weight = weight_of(xs, wr_ref, mine)
    g_ref[...] = (cs_ref[...].astype(F32) * weight).astype(BF16)

    @pl.when(step == 0)
    def _():
        for copy in copies():
            copy.wait()

    ret, dx = hidden_units(splits, xs, g_ref, up_ref, down_ref, act_ref, gp_ref)
    ret_ref[...] = ret.astype(BF16)
    dx_ref[...] = dx.astype(BF16)
    gu, gd = dot_tn(xs, gp_ref[...]), dot_tn(g_ref[...], act_ref[...])

    @pl.when(step == 0)
    def _():
        if late:
            for copy in sum_copies():
                copy.wait()
            gu_ref[...] += gu
            gd_ref[...] += gd
        else:
            gu_ref[...] = gu
            gd_ref[...] = gd

    @pl.when(step > 0)
    def _():
        gu_ref[...] += gu
        gd_ref[...] += gd

    if not late:

        @pl.when(step == len(blocks) - 1)
        def _():
            gu_out[...] = gu_ref[...]
            gd_out[...] = gd_ref[...]

        return

    @pl.when(step == len(blocks) - 1)
    def _():
        width, ff = gu_ref.shape
        part, units = width // 8, ff // 8
        for index in range(8):
            own = gu_ref[index * part : (index + 1) * part, :].astype(BF16)
            for block in range(ff // width):
                into = slice(block * part, (block + 1) * part)
                out_ref[index, into, :] = own[:, block * width : (block + 1) * width]
            down = gd_ref[:, index * units : (index + 1) * units].T.astype(BF16)
            out_ref[index, ff // width * part :, :] = down


def slot_block(rows, cols, first=0):
    return pl.BlockSpec((rows, cols), lambda i: (i + first, 0))


def expert_first(at, hidden, cots, wr, parts, filled, start, count, sums=()):
    _, rows, width = hidden[0].shape
    ff = (parts.shape[1] - 2 * width // 8) * 8
    blocks = BLOCKS[start : start + count]
    kinds = tuple(sorted({piece for block in blocks for piece, _ in block}))
    outs = [(8, rows, F32), *[(rows, width, BF16)] * 5]
    anywhere = pl.BlockSpec(memory_space=pl.ANY)
    if sums:
        more_specs, more = [whole(parts.shape)], [in_hbm(parts.shape, BF16)]
    else:
        more_specs, more = [whole((width, ff))] * 2, [in_hbm((width, ff), F32)] * 2
    return pl.pallas_call(
        functools.partial(expert_first_kernel, 2, filled, blocks, kinds),
        grid=(count,),
        in_specs=[
            SCALARS,
            whole(wr.shape),
            *[anywhere] * (3 + len(kinds) + len(sums)),
        ],
        out_specs=[slot_block(a, b) for a, b, _ in outs] + more_specs,
        out_shape=[in_hbm((count * a, b), kind) for a, b, kind in outs] + more,
        scratch_shapes=[
            pltpu.VMEM((width, ff), BF16),
            pltpu.VMEM((ff, width), BF16),
            pltpu.SemaphoreType.DMA((4,)),
            pltpu.VMEM((4 * count, rows, width), BF16),
            pltpu.SemaphoreType.DMA((count,)),
            pltpu.VMEM((rows, ff), BF16),
            pltpu.VMEM((rows, ff), BF16),
            pltpu.VMEM((width, ff), F32),
            pltpu.VMEM((width, ff), F32),
        ],
        compiler_params=params(48),
        cost_estimate=TINY,
        name="expert_first",
    )(*placed(at, wr, parts, *[hidden[k] for k in kinds], *cots, *sums, free=(*hidden, cots[1])))


def expert_second_kernel(
    splits, step_count, filled, at_ref, pos_ref, xs_ref, cs_ref, g_ref, ret0_ref, dx0_ref, wr_ref,
    parts_ref, *refs,
):
    step = pl.program_id(0)
    rows = xs_ref.shape[0]
    *refs, up_ref, down_ref, sem = refs
    early = step_count == EARLY
    if early:
        act_ref, gp_ref, dh_m, dh_o, ret_m, ret_o, extra_m, extra_o = refs
        firsts = [((dh_m, ret_m), 0), ((dh_o, ret_o), 0)]
        targets = [[(dh, 0, back, 0), (dh, 1, back, 1)] for (dh, back), _ in firsts]
        targets += [
            [(dh, 2, back, 2), (extra, 0, extra, 1)]
            for ((dh, back), _), extra in zip(firsts, (extra_m, extra_o))
        ]
    else:
        act_ref, gp_ref, dh_m, dh_o, ret_m, ret_o = refs
        targets = [[(a, 0, b, 0), (a, 1, b, 1)] for a, b in ((dh_m, ret_m), (dh_o, ret_o))]

    @pl.when(step == 0)
    def _():
        copies = load_weights(parts_ref, up_ref, down_ref, sem)
        for copy in copies:
            copy.start()
        for copy in copies:
            copy.wait()

    ret, dx = hidden_units(splits, xs_ref[...], g_ref, up_ref, down_ref, act_ref, gp_ref)
    ret = ret + ret0_ref[...].astype(F32)
    weight = weight_of(xs_ref[...], wr_ref, at_ref[2])
    gate = jnp.sum(cs_ref[...].astype(F32) * ret, axis=-1, keepdims=True)
    dxb = (dx + dx0_ref[...].astype(F32)).astype(BF16)
    high, middle = two_parts(gate)
    low = (gate - high.astype(F32) - middle.astype(F32)).astype(BF16)
    lane = lax.broadcasted_iota(jnp.int32, (1, 128), 1) - filled % 16 - 3 * at_ref[2]
    gates = jnp.where(lane == 0, high.astype(F32), 0.0)
    gates = jnp.where(lane == 1, middle.astype(F32), gates)
    gates = jnp.where(lane == 2, low.astype(F32), gates).astype(BF16)
    retb = (ret * weight).astype(BF16)
    slot = lax.broadcasted_iota(jnp.int32, (rows, rows), 1).astype(F32)
    lanes = -(-rows // 128) * 128
    tall = jnp.concatenate([pos_ref[...], jnp.zeros((8, lanes - rows), F32)], axis=1)
    tall = jnp.concatenate([tall, jnp.zeros((120, lanes), F32)], axis=0).T
    picks = [(slot == tall[:rows, k : k + 1]).astype(F32).astype(BF16) for k in range(2)]
    for number, target in enumerate(targets):

        @pl.when(step == number)
        def _(target=target):
            for pick, (dh, i, back, j) in zip(picks, target):
                back[j] = dot(pick, retb).astype(BF16)
                out = dot(pick, dxb)
                dh[i] = out.astype(BF16)
                tail = dot(pick, gates)
                tail = jnp.concatenate([tail, jnp.zeros((lanes - rows, 128), F32)], axis=0).T[:16, :rows]
                tail = jnp.concatenate(
                    [tail, jnp.zeros((16, out.shape[1] - rows), F32)], axis=1
                )
                start = filled // 16 * 16
                dh[i, start : start + 16, :] = (out[start : start + 16] + tail).astype(BF16)


def expert_second(at, first, wr, parts, filled):
    pos, xs, cs, g, ret, dx = first
    rows, width = pos.shape[1], xs.shape[1]
    count = xs.shape[0] // rows
    ff = (parts.shape[1] - 2 * width // 8) * 8
    sizes = (3, 3, 3, 3, 2, 2) if count == EARLY else (2, 2, 2, 2)
    return pl.pallas_call(
        functools.partial(expert_second_kernel, 2, count, filled),
        grid=(count,),
        in_specs=[
            SCALARS,
            slot_block(8, rows),
            slot_block(rows, width),
            slot_block(rows, width),
            slot_block(rows, width),
            slot_block(rows, width),
            slot_block(rows, width),
            whole(wr.shape),
            pl.BlockSpec(memory_space=pl.ANY),
        ],
        out_specs=[slot_block(rows, ff), slot_block(rows, ff)]
        + [whole((n, rows, width)) for n in sizes],
        out_shape=[
            in_hbm((count * rows, ff), BF16),
            in_hbm((count * rows, ff), BF16),
        ]
        + [jax.ShapeDtypeStruct((n, rows, width), BF16) for n in sizes],
        scratch_shapes=[
            pltpu.VMEM((width, ff), BF16),
            pltpu.VMEM((ff, width), BF16),
            pltpu.SemaphoreType.DMA((2,)),
        ],
        compiler_params=params(30),
        cost_estimate=TINY,
        name="expert_second",
    )(*placed(at, pos, xs, cs, g, ret, dx, wr, parts))


def weight_grad_kernel(ends, *refs):
    count = len(ends)
    xs, gs, gps, acts = (refs[i * count : (i + 1) * count] for i in range(4))
    out_ref, xs_t, g_t, turned = refs[4 * count :]
    step = pl.program_id(0)
    width = xs_t.shape[0]
    part, cols = width // 8, gps[0].shape[1]
    spans = list(zip((0, *ends[:-1]), ends))

    @pl.when(step == 0)
    def _():
        for (low, high), x_ref, g_ref in zip(spans, xs, gs):
            xs_t[:, low:high] = x_ref[...].T
            g_t[:, low:high] = g_ref[...].T

    up = down = None
    for (low, high), gp, act in zip(spans, gps, acts):
        one, two = dot(xs_t[:, low:high], gp[...]), dot(g_t[:, low:high], act[...])
        up, down = (one, two) if up is None else (up + one, down + two)
    turned[:width, :] = up.astype(BF16)
    block = step * cols // width
    lanes = pl.ds(pl.multiple_of(step * cols % width, cols), cols)
    into = pl.ds(pl.multiple_of(block * part, part), part)
    for index in range(8):
        out_ref[index, into, lanes] = turned[index * part : (index + 1) * part, :]
    half = cols // 2
    first = out_ref.shape[1] - half
    tall = down.T.astype(BF16)
    out_ref[2 * step, first:, :] = tall[:half]
    out_ref[2 * step + 1, first:, :] = tall[half:]


def weight_grad(xs, g, gps, acts):
    width, ff = xs[0].shape[1], gps[0].shape[1]
    cols = ff // 4
    out = (8, ff // width * (width // 8) + ff // 8, width)
    ends = []
    for gp in gps:
        ends.append(gp.shape[0] + (ends[-1] if ends else 0))
    slots = ends[-1]
    return pl.pallas_call(
        functools.partial(weight_grad_kernel, tuple(ends)),
        grid=(4,),
        in_specs=[whole(a.shape) for a in (*xs, *g)]
        + [pl.BlockSpec((a.shape[0], cols), lambda i: (0, i)) for a in (*gps, *acts)],
        out_specs=whole(out),
        out_shape=in_hbm(out, BF16),
        scratch_shapes=[
            pltpu.VMEM((width, slots), BF16),
            pltpu.VMEM((width, slots), BF16),
            pltpu.VMEM((width, cols), BF16),
        ],
        compiler_params=params(30),
        cost_estimate=TINY,
        name="weight_grad",
    )(*placed(*xs, *g, *gps, *acts))


def settle_kernel(at_ref, zero_ref, one_ref, up_ref, down_ref):
    part, units = up_ref.shape[1], zero_ref.shape[1] - 2 * up_ref.shape[1]
    for half, ref in enumerate((zero_ref, one_ref)):
        for index in range(8):
            rows = slice(index // 4 * part, index // 4 * part + part)
            to = (2 * index + half) * units
            from_ = index % 4 * units
            up_ref[0, :, to : to + units] = ref[0, rows, from_ : from_ + units].astype(F32)
        down_ref[0, half * units : (half + 1) * units, :] = ref[0, 2 * part :, :].astype(F32)


def settle_experts(at, zero, one):
    _, rows, width = zero.shape
    part = width // 8
    units = rows - 2 * part
    piece = pl.BlockSpec((1, rows, width), lambda i, at: (i ^ at[2], 0, 0))
    return pl.pallas_call(
        settle_kernel,
        grid_spec=pltpu.PrefetchScalarGridSpec(
            num_scalar_prefetch=1,
            grid=(E,),
            in_specs=[piece, piece],
            out_specs=[
                pl.BlockSpec((1, part, 16 * units), lambda i, at: (i, 0, 0)),
                pl.BlockSpec((1, 2 * units, width), lambda i, at: (i, 0, 0)),
            ],
        ),
        out_shape=[
            jax.ShapeDtypeStruct((E, part, 16 * units), F32),
            jax.ShapeDtypeStruct((E, 2 * units, width), F32),
        ],
        compiler_params=params(24),
        cost_estimate=TINY,
        name="settle_experts",
    )(*placed(at, zero, one))


def early_images(images, rows, width):
    return pl.BlockSpec((1, rows, width), lambda i: (jnp.minimum(i, images - 2), 0, 0))


def middle_back_kernel(
    filled, at_ref, a_ref, ar_ref, b_ref, br_ref, xr_ref, mid_ref, cot_ref, vec_ref, am_ref,
    got_ref, hidden_ref, wr_ref,
    gm_ref, low_ref, parts_ref, sums_ref, proj_ref, router_ref,
):
    rows, width = mid_ref.shape[1:]
    group = am_ref.shape[2]

    @pl.when(pl.program_id(0) == 0)
    def _():
        sums_ref[...] = jnp.zeros_like(sums_ref)
        proj_ref[...] = jnp.zeros_like(proj_ref)
        router_ref[...] = jnp.zeros_like(router_ref)

    last = pl.program_id(0) == pl.num_programs(0) - 1
    grad = jnp.where(
        last,
        b_ref[0].astype(F32) + br_ref[0].astype(F32),
        a_ref[0].astype(F32) + ar_ref[0].astype(F32),
    )
    grad = grad + xr_ref[0].astype(F32)
    gates = [grad[filled + 3 * e : filled + 3 * e + 3, :384] for e in range(E)]
    gates = [jnp.sum(g, axis=0, keepdims=True) for g in gates]
    gates = jnp.concatenate([jnp.zeros((4, 384), F32), *gates, jnp.zeros((120, 384), F32)], axis=0)
    gates = gates.T[:rows]
    router = routing(hidden_ref[0], wr_ref)
    mean = jnp.sum(router * gates, axis=-1, keepdims=True)
    logit_grad = (router * (gates - mean)).astype(BF16)
    row = lax.broadcasted_iota(jnp.int32, (rows, 1), 0)
    grad = jnp.where(row < filled, grad, 0.0) + dot_nt(logit_grad, wr_ref[...])
    router_ref[...] += dot_tn(hidden_ref[0], logit_grad)
    xhat, rstd = norm_parts(mid_ref[0])
    sums_ref[2:3, :] += jnp.sum(grad * xhat, axis=0, keepdims=True)
    sums_ref[3:4, :] += jnp.sum(grad, axis=0, keepdims=True)
    out = cot_ref[0].astype(F32) + norm_back(grad * vec_ref[2:3, :], xhat, rstd)
    out = jnp.where(row < filled, out, 0.0)
    gm_ref[0] = out
    low = out.astype(BF16)
    low_ref[0] = low
    proj_ref[:group, :] += dot_tn(am_ref[0], low)
    att_r = got_ref[pl.ds(pl.multiple_of(pl.program_id(0) * rows, 16), rows), :]
    proj_ref[group:, :] += dot_tn(att_r, low)

    @pl.when(pl.program_id(0) == pl.num_programs(0) - 1)
    def _():
        part = width // 8
        router = router_ref[...].T[:8]
        lines = jnp.concatenate(two_parts(sums_ref[...] + router), axis=0)
        row = lax.broadcasted_iota(jnp.int32, (width, 128), 0)
        col = lax.broadcasted_iota(jnp.int32, (width, 128), 1)
        for index in range(8):
            base = index * part
            from_ = pl.multiple_of(base ^ (at_ref[1] * group), part)
            parts_ref[index, :part, :] = proj_ref[pl.ds(from_, part), :].astype(BF16)
            pick = ((row == col + base) & (col < part)).astype(F32).astype(BF16)
            parts_ref[index, part:, :128] = dot(lines, pick).astype(BF16)
            parts_ref[index, part:, 128:] = jnp.zeros((16, width - 128), BF16)


def middle_back(at, mine, near, extra, extra_near, from_x, middle, cots, vecs, att_m, got, hidden, wr, filled):
    images, rows, width = middle.shape
    one = per_image(rows, width)
    group = att_m.shape[2]
    piece = (8, width // 8 + 16, width)
    return pl.pallas_call(
        functools.partial(middle_back_kernel, filled),
        grid=(images,),
        in_specs=[SCALARS]
        + [early_images(images, rows, width)] * 2
        + [pl.BlockSpec((1, rows, width), lambda i: (0, 0, 0))] * 2
        + [one] * 2
        + [one, whole(vecs.shape), per_image(rows, group), whole(got.shape)]
        + [one, whole(wr.shape)],
        out_specs=[one, one, whole(piece)],
        out_shape=[
            in_hbm(middle.shape, F32),
            jax.ShapeDtypeStruct(middle.shape, BF16),
            in_hbm(piece, BF16),
        ],
        scratch_shapes=[
            pltpu.VMEM((8, width), F32),
            pltpu.VMEM((width, width), F32),
            pltpu.VMEM((width, 128), F32),
        ],
        compiler_params=params(32),
        cost_estimate=TINY,
        name="middle_back",
    )(*placed(at, mine, near, extra, extra_near, from_x, middle, cots, vecs, att_m, got, hidden, wr, free=(near, extra_near, from_x)))


def mix_kernel(
    mid_ref, a_ref, ar_ref, b_ref, br_ref, x_ref, xr_ref, mine_ref, theirs_ref, send_ref
):
    last = pl.program_id(0) == pl.num_programs(0) - 1
    total = jnp.where(
        last,
        b_ref[0].astype(F32) + br_ref[0].astype(F32),
        a_ref[0].astype(F32) + ar_ref[0].astype(F32),
    )
    total = total + mid_ref[0]
    other = x_ref[0].astype(F32) + xr_ref[0].astype(F32)
    count = mine_ref.shape[1]
    mine_ref[0] = total[:count]
    theirs_ref[0] = other[count : 2 * count]
    send_ref[0, 0] = other[:count].astype(BF16)
    send_ref[0, 1] = total[count : 2 * count].astype(BF16)


def layer_mix(at, middle, mine, near, extra, extra_near, other, other_near, quarter):
    images, rows, width = middle.shape
    one, part = per_image(rows, width), per_image(quarter, width)
    return pl.pallas_call(
        lambda at_ref, *refs: mix_kernel(*refs),
        grid=(images,),
        in_specs=[
            SCALARS,
            one,
            *[early_images(images, rows, width)] * 2,
            *[pl.BlockSpec((1, rows, width), lambda i: (1, 0, 0))] * 2,
            one,
            one,
        ],
        out_specs=[part, part, per_image(2, quarter, width)],
        out_shape=[
            in_hbm((images, quarter, width), F32),
            in_hbm((images, quarter, width), F32),
            jax.ShapeDtypeStruct((images, 2, quarter, width), BF16),
        ],
        compiler_params=params(24),
        cost_estimate=TINY,
        name="layer_mix",
    )(*placed(at, middle, mine, near, extra, extra_near, other, other_near, free=(near, extra_near, other_near)))


def combine_kernel(at_ref, mine_ref, theirs_ref, got_ref, out_ref):
    ours = pl.program_id(0) // (pl.num_programs(0) // 2) == at_ref[2] // 2
    value = jnp.where(
        ours,
        mine_ref[0] + got_ref[0, 0].astype(F32),
        theirs_ref[0] + got_ref[0, 1].astype(F32),
    )
    out_ref[0] = value.astype(BF16)


def layer_combine(at, mine, theirs, got):
    half, quarter, width = mine.shape

    def image(i, at):
        return (jnp.where(i < half, i, (i + half - 1) % half), 0, 0)

    part = pl.BlockSpec((1, quarter, width), image)
    return pl.pallas_call(
        combine_kernel,
        grid_spec=pltpu.PrefetchScalarGridSpec(
            num_scalar_prefetch=1,
            grid=(2 * half,),
            in_specs=[
                part,
                part,
                pl.BlockSpec((1, 2, quarter, width), lambda i, at: (*image(i, at), 0)),
            ],
            out_specs=pl.BlockSpec((1, quarter, width), lambda i, at: (i, 0, 0)),
        ),
        out_shape=jax.ShapeDtypeStruct((2 * half, quarter, width), BF16),
        compiler_params=params(24),
        cost_estimate=TINY,
        name="layer_combine",
    )(*placed(at, mine, theirs, got))


def attend_back_kernel(
    head_dim, at_ref, lm_ref, lo_ref, pm_ref, qkv_ref, lse_ref, bias_ref, h1_ref, wq_ref,
    dm_ref, do_ref, gq_ref, grad_ref, low_ref,
):
    rows = lm_ref.shape[1]
    low_ref[:rows, :] = lm_ref[0]
    low_ref[rows:, :] = lo_ref[0]
    out_grad = dot_nt(low_ref[...], pm_ref[...]).astype(BF16)
    width = pm_ref.shape[0]
    bias = bias_ref[0]
    lane = lax.broadcasted_iota(jnp.int32, (1, 128), 1)
    sub = lax.broadcasted_iota(jnp.int32, (128, 1), 0)
    scaling = 1.0 / math.sqrt(head_dim)
    for pair in range(width // 128):
        cols = slice(pair * 128, pair * 128 + 128)
        k_cols = slice(width + pair * 128, width + pair * 128 + 128)
        v_cols = slice(2 * width + pair * 128, 2 * width + pair * 128 + 128)
        q2, k2, v2 = qkv_ref[0, :, cols], qkv_ref[0, :, k_cols], qkv_ref[0, :, v_cols]
        o2 = out_grad[:, cols]
        k_t = k2.T
        dv = dk = None
        both = []
        for part in range(2):
            mine = (lane >= head_dim * part) & (lane < head_dim * (part + 1))
            qm = jnp.where(mine, q2, jnp.zeros_like(q2))
            om = jnp.where(mine, o2, jnp.zeros_like(o2))
            head = 2 * pair + part
            probs = jnp.exp(dot_nt(k2, qm) + bias - lse_ref[0, head : head + 1, :])
            prob_grad = dot_nt(v2, om)
            delta = jnp.sum(probs * prob_grad, axis=0, keepdims=True)
            score_grad = (probs * (prob_grad - delta)).astype(BF16)
            dv_part = dot(probs.astype(BF16), om)
            dk_part = dot(score_grad, qm)
            dv = dv_part if dv is None else dv + dv_part
            dk = dk_part if dk is None else dk + dk_part
            both.append(dot(k_t, score_grad))
        dq = (jnp.where(sub < head_dim, both[0], both[1]) * scaling).astype(BF16).T
        grad_ref[:, cols] = dq
        grad_ref[:, k_cols] = dk.astype(BF16)
        grad_ref[:, v_cols] = dv.astype(BF16)
    hidden_grad = dot_nt(grad_ref[...], wq_ref[...]).astype(BF16)
    dm_ref[0] = hidden_grad[:rows]
    do_ref[0] = hidden_grad[rows:]
    grad_qkv = dot_tn(h1_ref[0], grad_ref[...])

    @pl.when(pl.program_id(0) == 0)
    def _():
        gq_ref[...] = grad_qkv

    @pl.when(pl.program_id(0) > 0)
    def _():
        gq_ref[...] += grad_qkv


def attend_back(at, low_m, low_o, proj_m, qkv, lse, bias, hidden_one, wq, head_dim):
    images, rows, width = low_m.shape
    group = proj_m.shape[0]
    return pl.pallas_call(
        functools.partial(attend_back_kernel, head_dim),
        grid=(images,),
        in_specs=[
            SCALARS,
            per_image(rows, width),
            per_image(rows, width),
            whole(proj_m.shape),
            per_image(2 * rows, 3 * group),
            per_image(8, 2 * rows),
            per_image(2 * rows, 1),
            per_image(2 * rows, width),
            whole(wq.shape),
        ],
        out_specs=[
            per_image(rows, width),
            per_image(rows, width),
            whole((width, 3 * group)),
        ],
        out_shape=[
            in_hbm((images, rows, width), BF16),
            jax.ShapeDtypeStruct((images, rows, width), BF16),
            in_hbm((width, 3 * group), F32),
        ],
        scratch_shapes=[
            pltpu.VMEM((2 * rows, 3 * group), BF16),
            pltpu.VMEM((2 * rows, width), BF16),
        ],
        compiler_params=params(48),
        cost_estimate=TINY,
        name="attend_back",
    )(*placed(at, low_m, low_o, proj_m, qkv, lse, bias, hidden_one, wq, free=(low_m, low_o)))


def input_back_kernel(
    x_ref, gm_ref, vec_ref, a_ref, ar_ref, gq_ref, r_ref,
    out_ref, go_ref, parts_ref, sums_ref,
):
    step, images = pl.program_id(0), pl.num_programs(0)
    grad = a_ref[0].astype(F32) + ar_ref[0].astype(F32)
    xhat, rstd = norm_parts(x_ref[0].astype(F32))
    out = gm_ref[0] + norm_back(grad * vec_ref[0:1, :], xhat, rstd)
    count = out_ref.shape[1]
    out_ref[0] = out[:count]
    go_ref[0] = out[count : 2 * count].astype(BF16)

    @pl.when(step == 0)
    def _():
        sums_ref[...] = jnp.zeros_like(sums_ref)

    sums_ref[0:1, :] += jnp.sum(grad * xhat, axis=0, keepdims=True)
    sums_ref[1:2, :] += jnp.sum(grad, axis=0, keepdims=True)

    @pl.when(step == images - 1)
    def _():
        total = gq_ref[...]
        width = grad.shape[1]
        part = width // 8
        lines = jnp.concatenate(two_parts(sums_ref[...]), axis=0)
        row = lax.broadcasted_iota(jnp.int32, (width, 128), 0)
        col = lax.broadcasted_iota(jnp.int32, (width, 128), 1)
        for index in range(8):
            base = index * part
            own = total[base : base + part].astype(BF16)
            half = jnp.concatenate([own[: part // 2, width:], own[part // 2 :, width:]], axis=1)
            into = (col >= part) & (col < 2 * part)
            pick_line = ((row == col - part + base) & into).astype(F32).astype(BF16)
            line = dot(lines, pick_line).astype(BF16)
            tail = jnp.concatenate([line, jnp.zeros((16, width - 128), BF16)], axis=1)
            block = jnp.concatenate([own[:, :width], half], axis=0)
            last = part + block.shape[0]
            parts_ref[index, part:last] = block
            parts_ref[index, last:] = r_ref[index, part:] + tail

        parts_ref[:, :part] = r_ref[:, :part]


def input_back(x_own, grad_middle, vecs, mine, near, grads, r_parts, quarter):
    images, rows, width = x_own.shape
    one, part = per_image(rows, width), per_image(quarter, width)
    more = r_parts.shape[1] + width // 8 + (grads.shape[1] - width) * (width // 8) // width
    more = (8, more, width)
    return pl.pallas_call(
        input_back_kernel,
        grid=(images,),
        in_specs=[one, one, whole(vecs.shape), one, one, whole(grads.shape), whole(r_parts.shape)],
        out_specs=[part, part, whole(more)],
        out_shape=[
            jax.ShapeDtypeStruct((images, quarter, width), F32),
            jax.ShapeDtypeStruct((images, quarter, width), BF16),
            in_hbm(more, BF16),
        ],
        scratch_shapes=[pltpu.VMEM((8, width), F32)],
        compiler_params=params(32),
        cost_estimate=TINY,
        name="input_back",
    )(*placed(x_own, grad_middle, vecs, mine, near, grads, r_parts, free=(near,)))


def shards(
    tokens,
    key_mask,
    expert_ids,
    ln1_gain,
    ln1_bias,
    qkv_weight,
    proj_weight,
    ln2_gain,
    ln2_bias,
    router_weight,
    up_weight,
    down_weight,
    cotangent,
):
    n_seq, n_wide = lax.axis_size("seq"), lax.axis_size("wide")
    images, quarter, width = tokens.shape
    head_dim = width // H
    group = width // 2
    filled = 2 * quarter
    rows = -(-(filled + 3 * E) // 16) * 16
    place = lax.axis_index("seq")
    chip, core = place // 2, place % 2
    direct = n_wide == 8
    spot = lax.axis_index("wide") if direct else 0
    at = jnp.stack([jnp.int32(spot), core, place, jnp.int32(spot) % 2])
    part = width // 8

    def over_seq(a, turn):
        return lax.ppermute(a, "seq", [(i, i ^ turn) for i in range(n_seq)])

    def over_x(a):
        return over_seq(a, 2)

    def over_core(a):
        return over_seq(a, 1)

    def over_wide(a, turn):
        return lax.ppermute(a, "wide", [(i, i ^ turn) for i in range(n_wide)])

    def after(value, *first):
        return lax.optimization_barrier((value, *first))[0]

    def images_of(a, of_chip):
        pair = lax.dynamic_slice_in_dim(a, of_chip * (images - 2), 2, 0)
        single = lax.dynamic_slice_in_dim(a, images // 2 - 1 + of_chip, 1, 0)
        return jnp.concatenate([pair, single], axis=0)

    def joined(first, second):
        both = jnp.concatenate([first, second], axis=1)
        return jnp.pad(both, ((0, 0), (0, rows - filled)) + ((0, 0),) * (both.ndim - 2))

    def cells(quarters, of_chip, of_core):
        first = lax.dynamic_index_in_dim(quarters, 2 * of_chip + of_core, 1, False)
        second = lax.dynamic_index_in_dim(quarters, 2 * (1 - of_chip) + of_core, 1, False)
        return joined(images_of(first, of_chip), images_of(second, of_chip))

    mask = key_mask.reshape(images, n_seq, quarter)
    valid = jnp.concatenate([cells(mask, chip, core), cells(mask, chip, 1 - core)], axis=1)
    bias = jnp.where(valid > 0, 0.0, BIG).astype(F32)[..., None]

    def heads_of(a):
        return jnp.concatenate(
            [lax.dynamic_slice_in_dim(a, (2 * i + core) * group, group, 1) for i in range(3)],
            axis=1,
        )

    wq = heads_of(qkv_weight)
    proj = lax.dynamic_slice_in_dim(proj_weight, core * group, group, 1)
    lines = jnp.stack([ln1_gain, ln1_bias, ln2_gain, ln2_bias])
    lines = jnp.concatenate([lines, router_weight.T], axis=0)
    up = lax.dynamic_index_in_dim(up_weight, place, 0, False)
    down = lax.dynamic_index_in_dim(down_weight, place, 0, False)
    units = down.shape[0] // 2

    def first_parts(wq, proj, lines):
        both = jnp.concatenate([wq, proj], axis=1)
        fill = ((0, 16 - lines.shape[0]), (0, both.shape[1] - lines.shape[1]))
        return jnp.concatenate([both, jnp.pad(lines, fill)], axis=0)

    def half_of(up, down, half):
        cols = up.reshape(up.shape[0], n_wide, 2, units)[:, :, half].reshape(up.shape[0], -1)
        down = down.reshape(-1, 2, units, width)[:, half].reshape(-1, width)
        blocks = [cols[:, i : i + width] for i in range(0, cols.shape[1], width)]
        return jnp.concatenate([*blocks, down], axis=0)

    one_all = first_parts(wq, proj, lines)
    one_all = jnp.broadcast_to(one_all[None], (4, *one_all.shape))
    codes = (expert_ids[..., 0] * E + expert_ids[..., 1]).astype(BF16)
    codes = jnp.pad(codes, ((0, 0), (0, width - quarter)))[:, None, :]
    cot = jnp.concatenate([cotangent, codes], axis=1)
    x_got = over_x(images_of(after(tokens, one_all), 1 - chip))
    x_own = joined(images_of(tokens, chip), x_got)
    x_oth = over_core(after(x_own, bias, cot))
    cot_got = over_x(after(cot, x_got))

    z_groups = [[y + 2 * z for z in range(4)] for y in range(2)]

    def all_of(a, axis=0):
        return lax.all_gather(a, "wide", axis=axis, tiled=True)

    if direct:
        ones = lax.all_to_all(one_all, "wide", 0, 0, axis_index_groups=z_groups, tiled=True)
        ones_y = over_wide(ones, 1)
        twos, threes = (
            lax.all_gather(after(half_of(up, down, half), ones, x_oth), "wide") for half in range(2)
        )
    else:

        def eight(a, axis=0):
            return jnp.split(a, 8, axis=axis)

        ones = jnp.stack([first_parts(*a) for a in zip(eight(all_of(wq)), eight(all_of(proj)), eight(all_of(lines, 1), 1))])
        ones, ones_y = ones[::2], ones[1::2]
        ups, downs = eight(all_of(up)), eight(all_of(down))
        twos, threes = (
            jnp.stack([half_of(a, b, half) for a, b in zip(ups, downs)]) for half in range(2)
        )

    att_m, mail, qkv, hidden_one, lse, wq, small, vecs = attend(
        at, x_own, x_oth, bias, ones, ones_y, head_dim
    )
    mail_got = over_core(mail)
    middle, hidden_two, proj_m = project(at, att_m, mail, mail_got, x_own, vecs)
    cots_m = join_cots(at, cot, after(cot_got, hidden_two), rows)
    cots_o = over_core(cots_m)
    hidden_b = over_x(hidden_two)
    hidden_c = over_core(hidden_two)
    ours = (hidden_two, None, hidden_c, None)
    *first_a, gu_a, gd_a = expert_first(
        at, ours, (cots_m, cots_o), small, twos, filled, EARLY, len(BLOCKS) - EARLY
    )
    hidden_d = over_core(after(hidden_b, gu_a))
    hidden = (hidden_two, hidden_b, hidden_c, hidden_d)
    *first_b, parts0 = expert_first(
        at, hidden, (cots_m, cots_o), small, twos, filled, 0, EARLY, (gu_a, gd_a)
    )
    act1, gp1, dh_m, dh_o, ret_m, ret_o, extra_m, extra_o = expert_second(
        after(at, parts0), first_b, small, threes, filled
    )
    dh_r = over_core(dh_o)
    dh_b = dh_m + dh_r
    dh_x = over_x(dh_b)
    ret_r = over_core(ret_o)
    def over_y(send, keep, *first):
        if not direct:
            return jnp.stack([keep, send], axis=1)
        got = over_wide(send, 1)
        return after(keep, *first) + after(got, *first)

    def over_z(both):
        return lax.all_to_all(both, "wide", 0, 0, axis_index_groups=z_groups, tiled=True)

    def expert_sum(both):
        both = both.reshape(8, -1, width)
        cut = 2 * part
        cols = jnp.moveaxis(both[:, :cut].reshape(8, 2, part, width), 1, 2).reshape(width, -1)
        rows = both[:, cut:].reshape(-1, width)
        return tuple(
            lax.psum_scatter(a, "wide", scatter_dimension=0, tiled=True) for a in (cols, rows)
        )

    def near_pair(a):
        return jnp.stack([a, over_core(a)])

    def near_experts(pairs):
        return jnp.concatenate([pairs, over_x(pairs)], axis=0)

    extra_r = over_core(extra_o)
    act2, gp2, late_m, late_o, late_ret_m, late_ret_o = expert_second(
        after(at, dh_b), first_a, small, threes, filled
    )
    late_r = over_core(late_o)
    late_ret_r = over_core(late_ret_o)
    if direct:
        sum0 = lax.all_to_all(parts0, "wide", 0, 0, tiled=True)

    xs = (first_b[1], first_a[1])
    parts1 = weight_grad(xs, (first_b[3], first_a[3]), [gp1, gp2], [act1, act2])
    layer_mine, layer_theirs, layer_send = layer_mix(
        after(at, parts1), middle, late_ret_m, late_ret_r, extra_m, extra_r, ret_m, ret_r, quarter
    )
    layer_got = over_x(after(layer_send, dh_x))

    grad_middle, low_m, r_parts = middle_back(
        at,
        late_m,
        late_r,
        extra_m,
        extra_r,
        dh_x,
        middle,
        cots_m,
        vecs,
        att_m,
        mail_got,
        hidden_two,
        small,
        filled,
    )
    low_o = over_core(low_m)
    if direct:
        sum1 = lax.all_to_all(after(parts1, dh_x, layer_send), "wide", 0, 0, tiled=True)
    dh1_m, dh1_o, grad_qkv = attend_back(
        at, low_m, low_o, proj_m, qkv, lse, bias, hidden_one, wq, head_dim
    )
    dh1_o = after(dh1_o, layer_got)
    dh1_r = over_core(dh1_o)
    input_mine, input_send, q_parts = input_back(
        x_own, grad_middle, vecs, dh1_m, dh1_r, grad_qkv, r_parts, quarter
    )
    last = q_parts.shape[1] - 16
    input_got = over_x(input_send)
    if direct:
        rest = lax.all_to_all(q_parts, "wide", 0, 0, tiled=True)
        sum0, sum1 = (
            jnp.sum(after(a, q_parts).astype(F32), axis=0).astype(BF16) for a in (sum0, sum1)
        )
        near0, near1 = near_experts(near_pair(sum0)), near_experts(after(near_pair(sum1), input_got))
    else:
        sum0 = expert_sum(parts0)
        sum1 = expert_sum(parts1)

    def settle(mine, got):
        got = got.astype(mine.dtype)
        pair, rest = slice(0, 2), slice(2, 3)
        return jnp.where(
            chip == 0,
            jnp.concatenate([mine[pair], mine[rest], got[rest], got[pair]], axis=0),
            jnp.concatenate([got[pair], got[rest], mine[rest], mine[pair]], axis=0),
        )

    input_grad = settle(input_mine, input_got)
    if not direct:

        def in_order(a):
            four = near_experts(near_pair(a))
            return jnp.stack(
                [lax.dynamic_index_in_dim(four, place ^ e, 0, False) for e in range(E)]
            ).astype(F32)

        up0, up1, down0, down1 = (in_order(s[i]) for i in range(2) for s in (sum0, sum1))
        halves = [a.reshape(E, -1, n_wide, units) for a in (up0, up1)]
        grad_up = jnp.stack(halves, axis=3).reshape(E, -1, up.shape[1])
        grad_down = jnp.concatenate([down0, down1], axis=1)

    def over_seq_group(rows, lines):
        count = rows.shape[0]

        def sent(over, rows, lines):
            got = over(jnp.concatenate([rows.astype(BF16), *two_parts(lines)])).astype(F32)
            low = got[count : count + lines.shape[0]] + got[count + lines.shape[0] :]
            return got[:count], lines + low

        got, lines = sent(over_x, rows, lines)
        rows = rows + got
        other, lines = sent(over_core, rows, lines)
        return rows, other, lines

    owned = proj_weight.shape[0]
    if direct:
        rest = after(rest, input_got)
        rest = jnp.sum(rest.astype(F32), axis=0)
        rows, lines = rest[:last], rest[last : last + 8] + rest[last + 8 :]
        lines = jnp.concatenate([lines[:, :part], lines[:, part : 2 * part]])
        lines = jnp.pad(lines, ((0, 0), (0, width - part)))
    else:
        both = q_parts.astype(F32)
        rows = [both[:, :part], both[:, part : 2 * part]]
        halves = both[:, 2 * part : last].reshape(8, -1, 2, group)
        rows.append(jnp.moveaxis(halves, 2, 1).reshape(8, part, group))
        two = both[:, last : last + 8] + both[:, last + 8 :]
        for low in (0, part):
            rows.append(jnp.moveaxis(two[:, :, low : low + part], 1, 2))
        rows = jnp.concatenate(rows, axis=2).reshape(width, -1)
        rows = lax.psum_scatter(rows, "wide", scatter_dimension=0, tiled=True)
        lines = jnp.pad(rows[:, -16:].T, ((0, 0), (0, width - owned)))
        more = rows[:, 2 * width : -16]
        more = jnp.concatenate([more[: owned // 2], more[owned // 2 :]], axis=1)
        rows = jnp.concatenate([rows[:, :width], rows[:, width : 2 * width], more])
    total, other, lines = over_seq_group(rows, lines)
    if direct:
        grad_up, grad_down = settle_experts(after(at, rows), near0, near1)
    layer_out = layer_combine(after(at, q_parts), layer_mine, layer_theirs, layer_got)
    grad_proj = total[:owned] + other[:owned]

    def thirds(a):
        more = a[2 * owned :]
        more = jnp.concatenate([more[:, :group], more[:, group:]])
        return [a[owned : 2 * owned, :group], a[owned : 2 * owned, group:], more]

    lines = lines[:, :owned]
    pairs = zip(thirds(total), thirds(other))
    ordered = [(jnp.where(core == 0, a, b), jnp.where(core == 0, b, a)) for a, b in pairs]
    grad_qkv = jnp.concatenate([a for pair in ordered for a in pair], axis=1)
    return (
        layer_out,
        input_grad,
        lines[8],
        lines[9],
        grad_qkv,
        grad_proj,
        lines[2],
        lines[3],
        lines[4 : 4 + E].T,
        grad_up,
        grad_down,
    )


def solution(mesh):
    placed = (
        P("wide", "seq", None),
        P("wide", None),
        P("wide", "seq", None),
        P("wide"),
        P("wide"),
        P("wide", None),
        P("wide", None),
        P("wide"),
        P("wide"),
        P("wide", None),
        P(None, "wide", None),
        P(None, "wide", None),
        P("wide", "seq", None),
    )
    return jax.shard_map(
        shards,
        mesh=mesh,
        in_specs=placed,
        out_specs=(
            P("wide", "seq", None),
            P("wide", "seq", None),
            P("wide"),
            P("wide"),
            P("wide", None),
            P("wide", None),
            P("wide"),
            P("wide"),
            P("wide", None),
            P(None, "wide", None),
            P(None, "wide", None),
        ),
        check_vma=False,
    )
```

```python
import functools
import math

import jax
import jax.numpy as jnp
from jax import lax
from jax.experimental import pallas as pl
from jax.experimental.pallas import tpu as pltpu
from jax.sharding import PartitionSpec as P

H = 8
E = 4
EPSILON = 1e-06
BIG = -1e30
MIB = 1024 * 1024
F32 = jnp.float32
BF16 = jnp.bfloat16


def dot(a, b, dims=((1,), (0,))):
    return lax.dot_general(a, b, (dims, ((), ())), preferred_element_type=F32)


def dot_nt(a, b):
    return dot(a, b, ((1,), (1,)))


def dot_tn(a, b):
    return dot(a, b, ((0,), (0,)))


def norm_parts(values):
    center = values - jnp.mean(values, axis=-1, keepdims=True)
    spread = jnp.mean(center * center, axis=-1, keepdims=True)
    rstd = lax.rsqrt(spread + EPSILON)
    return center * rstd, rstd


def norm_back(grad, xhat, rstd):
    return rstd * (
        grad
        - jnp.mean(grad, axis=-1, keepdims=True)
        - xhat * jnp.mean(grad * xhat, axis=-1, keepdims=True)
    )


TINY = pl.CostEstimate(flops=1000, bytes_accessed=1000, transcendentals=0)


def params(limit, **more):
    return pltpu.CompilerParams(vmem_limit_bytes=limit * MIB, **more)


def placed(*arrays, free=()):
    return [
        pltpu.with_memory_space_constraint(a, pltpu.HBM)
        if a.size > 1 << 15 and not any(a is f for f in free)
        else a
        for a in arrays
    ]


def in_hbm(shape, dtype):
    return pltpu.HBM(shape, dtype)


def whole(shape):
    return pl.BlockSpec(shape, lambda *_: (0,) * len(shape))


def per_image(*shape):
    return pl.BlockSpec((1, *shape), lambda i: (i,) + (0,) * len(shape))


SCALARS = pl.BlockSpec(memory_space=pltpu.SMEM)


def attend_kernel(
    images, head_dim, at_ref, own_ref, oth_ref, bias_ref, here_ref, there_ref,
    att_m_ref, mail_ref, qkv_ref, hidden_ref, lse_ref, wq_ref, small_ref, vec_ref,
):
    rows = own_ref.shape[1]
    features = wq_ref.shape[0]

    @pl.when(pl.program_id(0) == 0)
    def _():
        part = features // 8
        vec = jnp.zeros((8, features), F32)
        row = lax.broadcasted_iota(jnp.int32, (part, features), 0)
        col = lax.broadcasted_iota(jnp.int32, (part, features), 1)
        for index in range(8):
            side = at_ref[3] if index % 2 == 0 else 1 - at_ref[3]
            ref = (here_ref, there_ref)[index % 2].at[index // 2]
            base = pl.multiple_of((index // 2 * 2 + side) * part, part)
            wq_ref[pl.ds(base, part), :] = ref[:part, : wq_ref.shape[1]]
            mail_ref[pl.ds(images * rows + base, part), :] = ref[:part, wq_ref.shape[1] :]
            spread = (col == row + base).astype(F32).astype(BF16)
            vec = vec + dot(ref[part:, :part], spread)[:8]
        vec_ref[...] = vec
        tall = jnp.concatenate([vec, jnp.zeros((120, features), F32)], axis=0)
        small_ref[...] = tall.T.astype(BF16)

    gain, offset = vec_ref[0:1, :], vec_ref[1:2, :]
    for half, ref in enumerate((own_ref, oth_ref)):
        xhat, _ = norm_parts(ref[0].astype(F32))
        hidden_ref[0, half * rows : (half + 1) * rows, :] = (xhat * gain + offset).astype(BF16)
    width = wq_ref.shape[1] // 3
    packed = dot(hidden_ref[0], wq_ref[...]).astype(BF16)
    scaling = 1.0 / math.sqrt(head_dim)
    qkv_ref[0, :, :width] = (packed[:, :width].astype(F32) * scaling).astype(BF16)
    qkv_ref[0, :, width:] = packed[:, width:]
    bias = bias_ref[0]
    lane = lax.broadcasted_iota(jnp.int32, (1, 128), 1)
    sub = lax.broadcasted_iota(jnp.int32, (128, 1), 0)
    for pair in range(width // 128):
        cols = slice(pair * 128, pair * 128 + 128)
        q2 = qkv_ref[0, :, cols]
        k2 = qkv_ref[0, :, width + pair * 128 : width + pair * 128 + 128]
        v2 = qkv_ref[0, :, 2 * width + pair * 128 : 2 * width + pair * 128 + 128]
        v_t = v2.T
        both = []
        for part in range(2):
            mine = (lane >= head_dim * part) & (lane < head_dim * (part + 1))
            qm = jnp.where(mine, q2, jnp.zeros_like(q2))
            scores = dot_nt(k2, qm) + bias
            peak = jnp.max(scores, axis=0, keepdims=True)
            expo = jnp.exp(scores - peak)
            total = jnp.sum(expo, axis=0, keepdims=True)
            lse_ref[0, 2 * pair + part : 2 * pair + part + 1, :] = peak + jnp.log(total)
            both.append(dot(v_t, (expo * (1.0 / total)).astype(BF16)))
        out = jnp.where(sub < head_dim, both[0], both[1]).astype(BF16).T
        att_m_ref[0, :, cols] = out[:rows]
        mail_ref[pl.ds(pl.multiple_of(pl.program_id(0) * rows, 16), rows), cols] = out[rows:]


def attend(at, x_own, x_oth, bias, here, there, head_dim):
    images, rows, width = x_own.shape
    group = width // 2
    return pl.pallas_call(
        functools.partial(attend_kernel, images, head_dim),
        grid=(images,),
        in_specs=[
            SCALARS,
            per_image(rows, width),
            per_image(rows, width),
            per_image(2 * rows, 1),
            whole(here.shape),
            whole(there.shape),
        ],
        out_specs=[
            per_image(rows, group),
            whole((images * rows + width, group)),
            per_image(2 * rows, 3 * group),
            per_image(2 * rows, width),
            per_image(8, 2 * rows),
            whole((width, 3 * group)),
            whole((width, 128)),
            whole((8, width)),
        ],
        out_shape=[
            jax.ShapeDtypeStruct((images, rows, group), BF16),
            jax.ShapeDtypeStruct((images * rows + width, group), BF16),
            in_hbm((images, 2 * rows, 3 * group), BF16),
            in_hbm((images, 2 * rows, width), BF16),
            in_hbm((images, 8, 2 * rows), F32),
            in_hbm((width, 3 * group), BF16),
            in_hbm((width, 128), BF16),
            jax.ShapeDtypeStruct((8, width), F32),
        ],
        compiler_params=params(40),
        cost_estimate=TINY,
        name="attend",
    )(*placed(at, x_own, x_oth, bias, here, there, free=(x_oth, there)))


def project_kernel(
    at_ref, att_m_ref, sent_ref, got_ref, x_ref, vec_ref, middle_ref, hidden_ref, proj_ref
):
    rows, group = att_m_ref.shape[1:]
    core, first = at_ref[1], pl.num_programs(0) * rows
    mine = pl.ds(pl.multiple_of(core * group + first, 16), group)
    other = pl.ds(pl.multiple_of((1 - core) * group + first, 16), group)

    def in_order(a, b):
        return jnp.concatenate([jnp.where(core == 0, a, b), jnp.where(core == 0, b, a)], axis=1)

    @pl.when(pl.program_id(0) == 0)
    def _():
        proj_ref[...] = in_order(sent_ref[mine, :], got_ref[mine, :])

    att_r = got_ref[pl.ds(pl.multiple_of(pl.program_id(0) * rows, 16), rows), :]
    halves = [
        dot(att_m_ref[0], ref[mine, :]) + dot(att_r, ref[other, :]) for ref in (sent_ref, got_ref)
    ]
    middle = x_ref[0].astype(F32) + in_order(*halves)
    middle_ref[0] = middle
    xhat, _ = norm_parts(middle)
    hidden_ref[0] = (xhat * vec_ref[2:3, :] + vec_ref[3:4, :]).astype(BF16)


def project(at, att_m, sent, got, x_own, vecs):
    images, rows, width = x_own.shape
    group = att_m.shape[2]
    return pl.pallas_call(
        project_kernel,
        grid=(images,),
        in_specs=[
            SCALARS,
            per_image(rows, group),
            whole(sent.shape),
            whole(got.shape),
            per_image(rows, width),
            whole(vecs.shape),
        ],
        out_specs=[per_image(rows, width), per_image(rows, width), whole((group, width))],
        out_shape=[
            in_hbm(x_own.shape, F32),
            jax.ShapeDtypeStruct(x_own.shape, BF16),
            in_hbm((group, width), BF16),
        ],
        compiler_params=params(24),
        cost_estimate=TINY,
        name="project",
    )(*placed(at, att_m, sent, got, x_own, vecs, free=(got,)))


def join_kernel(at_ref, cot_ref, got_ref, out_ref):
    images, rows, width = out_ref.shape
    half, count = images // 2, cot_ref.shape[1] - 1
    start = count // 16 * 16
    for index in range(images):
        chip = (at_ref[2] // 2 + index // half) % 2
        k = index % half
        image = chip * (images - 2) + k if k < half - 1 else half - 1 + chip
        refs = (cot_ref, got_ref) if index < half else (got_ref, cot_ref)
        first, second = (ref[image] for ref in refs)
        second = second.astype(F32)
        out_ref[index, :start, :] = first[:start]
        tail = first[start:].astype(F32)
        codes = jnp.concatenate(
            [
                tail[count - start :, :count],
                second[count:, :count],
                jnp.zeros((1, width - 2 * count), F32),
            ],
            axis=1,
        )
        fill = jnp.zeros((rows - 2 * count - 1, width), F32)
        rest = jnp.concatenate([tail[: count - start], second[:count], codes, fill], axis=0)
        out_ref[index, start:, :] = rest.astype(BF16)


def join_cots(at, cot, got, rows):
    images, _, width = cot.shape
    return pl.pallas_call(
        join_kernel,
        in_specs=[SCALARS, *[pl.BlockSpec(memory_space=pltpu.VMEM)] * 2],
        out_specs=pl.BlockSpec(memory_space=pltpu.VMEM),
        out_shape=jax.ShapeDtypeStruct((images, rows, width), BF16),
        compiler_params=params(16),
        cost_estimate=TINY,
        name="join_cots",
    )(at, cot, got)


BLOCKS = (
    ((1, 0), (1, 1)),
    ((3, 0), (3, 1)),
    ((1, 2), (0, 2)),
    ((3, 2), (2, 2)),
    ((0, 0), (0, 1)),
    ((2, 0), (2, 1)),
)
EARLY = 4


def load_weights(parts_ref, up_ref, down_ref, sem):
    part = up_ref.shape[0] // 8
    width, units = down_ref.shape[1], up_ref.shape[1] // 8
    copies = []
    for index in range(8):
        base = slice(index * part, index * part + part)
        for block in range(up_ref.shape[1] // width):
            copies.append(
                pltpu.make_async_copy(
                    parts_ref.at[index, block * part : (block + 1) * part, :],
                    up_ref.at[base, block * width : (block + 1) * width],
                    sem.at[0],
                )
            )
        base = slice(index * units, (index + 1) * units)
        first = up_ref.shape[1] // width * part
        copies.append(
            pltpu.make_async_copy(
                parts_ref.at[index, first : first + units, :], down_ref.at[base, :], sem.at[1]
            )
        )
    return copies


def hidden_units(splits, xs, g_ref, up_ref, down_ref, act_ref, gp_ref):
    ff = up_ref.shape[1]
    chunk = ff // splits
    ret = dx = None
    for part in range(splits):
        cols = slice(part * chunk, (part + 1) * chunk)
        pre = dot(xs, up_ref[:, cols])
        back = dot_nt(g_ref[...], down_ref[cols, :])
        cdf = 0.5 + 0.5 * lax.erf(pre * math.sqrt(0.5))
        pdf = jnp.exp(-0.5 * pre * pre) * (1.0 / math.sqrt(2.0 * math.pi))
        act = (pre * cdf).astype(BF16)
        gp = (back * (cdf + pre * pdf)).astype(BF16)
        act_ref[:, cols] = act
        gp_ref[:, cols] = gp
        ret_part = dot(act, down_ref[cols, :])
        dx_part = dot_nt(gp, up_ref[:, cols])
        ret = ret_part if ret is None else ret + ret_part
        dx = dx_part if dx is None else dx + dx_part
    return ret, dx


def routing(hidden, wr_ref):
    logits = dot(hidden, wr_ref[...])
    lane = lax.broadcasted_iota(jnp.int32, (1, 128), 1)
    logits = jnp.where((lane >= 4) & (lane < 4 + E), logits, BIG)
    grown = jnp.exp(logits - jnp.max(logits, axis=-1, keepdims=True))
    return grown / jnp.sum(grown, axis=-1, keepdims=True)


def weight_of(hidden, wr_ref, mine):
    lane = lax.broadcasted_iota(jnp.int32, (1, 128), 1)
    router = jnp.where(lane == 4 + mine, routing(hidden, wr_ref), 0.0)
    return jnp.sum(router, axis=-1, keepdims=True)


def two_parts(values):
    high = values.astype(BF16)
    return high, (values - high.astype(F32)).astype(BF16)


def expert_first_kernel(
    splits, filled, blocks, kinds, at_ref, wr_ref, parts_ref, *refs
):
    step = pl.program_id(0)
    hs = dict(zip(kinds, refs))
    cots = refs[len(kinds) : len(kinds) + 2]
    cs = {k: cots[k // 2].at[pl.ds(k % 2 * (cots[0].shape[0] // 2), cots[0].shape[0] // 2)] for k in kinds}
    refs = refs[len(kinds) + 2 :]
    *refs, up_ref, down_ref, sem, piece_ref, piece_sem, act_ref, gp_ref, gu_ref, gd_ref = refs
    late = len(blocks) == EARLY
    if late:
        gu_in, gd_in, pos_ref, xs_ref, cs_ref, g_ref, ret_ref, dx_ref, out_ref = refs
    else:
        pos_ref, xs_ref, cs_ref, g_ref, ret_ref, dx_ref, gu_out, gd_out = refs
    rows = xs_ref.shape[0]
    mine = at_ref[2]

    def pieces_of(number):
        copies = []
        for k, (piece, image) in enumerate(blocks[number]):
            for j, kind in enumerate((hs, cs)):
                spot = number * 4 + 2 * k + j
                copies.append(
                    pltpu.make_async_copy(
                        kind[piece].at[image], piece_ref.at[spot], piece_sem.at[number]
                    )
                )
        return copies

    def sum_copies():
        return [
            pltpu.make_async_copy(gu_in, gu_ref, sem.at[2]),
            pltpu.make_async_copy(gd_in, gd_ref, sem.at[3]),
        ]

    def copies():
        return load_weights(parts_ref, up_ref, down_ref, sem)

    @pl.when(step == 0)
    def _():
        for number in range(len(blocks)):
            for copy in pieces_of(number):
                copy.start()
            if number == 0:
                for copy in copies():
                    copy.start()
        if late:
            for copy in sum_copies():
                copy.start()

    token = lax.broadcasted_iota(jnp.int32, (1, rows), 1)
    slot = lax.broadcasted_iota(jnp.int32, (rows, rows), 0)
    before = (slot < lax.broadcasted_iota(jnp.int32, (rows, rows), 1)).astype(F32).astype(BF16)
    for number, block in enumerate(blocks):

        @pl.when(step == number)
        def _(number=number, block=block):
            for copy in pieces_of(number):
                copy.wait()
            base, xs, got = 0.0, None, None
            for k in range(2):
                spot = number * 4 + 2 * k
                code = piece_ref[spot + 1, filled // 16 * 16 : filled // 16 * 16 + 16, :rows]
                code = code.astype(F32)[filled % 16 : filled % 16 + 1, :]
                first = jnp.floor(code * (1.0 / E))
                second = code - E * first
                own = mine.astype(F32)
                named = ((first == own) | (second == own)) & (token < filled)
                flag = jnp.where(named, 1.0, 0.0)
                rank = dot(jnp.broadcast_to(flag, (16, rows)).astype(BF16), before)[0:1, :] + base
                rank = jnp.where(named, rank, -1.0)
                base = base + jnp.sum(flag, axis=-1, keepdims=True)
                pos_ref[k : k + 1, :] = rank
                pick = (slot.astype(F32) == rank).astype(F32).astype(BF16)
                a, b = dot(pick, piece_ref[spot]), dot(pick, piece_ref[spot + 1])
                xs, got = (a, b) if xs is None else (xs + a, got + b)
            xs_ref[...] = xs.astype(BF16)
            cs_ref[...] = got.astype(BF16)

    xs = xs_ref[...]
    weight = weight_of(xs, wr_ref, mine)
    g_ref[...] = (cs_ref[...].astype(F32) * weight).astype(BF16)

    @pl.when(step == 0)
    def _():
        for copy in copies():
            copy.wait()

    ret, dx = hidden_units(splits, xs, g_ref, up_ref, down_ref, act_ref, gp_ref)
    ret_ref[...] = ret.astype(BF16)
    dx_ref[...] = dx.astype(BF16)
    gu, gd = dot_tn(xs, gp_ref[...]), dot_tn(g_ref[...], act_ref[...])

    @pl.when(step == 0)
    def _():
        if late:
            for copy in sum_copies():
                copy.wait()
            gu_ref[...] += gu
            gd_ref[...] += gd
        else:
            gu_ref[...] = gu
            gd_ref[...] = gd

    @pl.when(step > 0)
    def _():
        gu_ref[...] += gu
        gd_ref[...] += gd

    if not late:

        @pl.when(step == len(blocks) - 1)
        def _():
            gu_out[...] = gu_ref[...]
            gd_out[...] = gd_ref[...]

        return

    @pl.when(step == len(blocks) - 1)
    def _():
        width, ff = gu_ref.shape
        part, units = width // 8, ff // 8
        for index in range(8):
            own = gu_ref[index * part : (index + 1) * part, :].astype(BF16)
            for block in range(ff // width):
                into = slice(block * part, (block + 1) * part)
                out_ref[index, into, :] = own[:, block * width : (block + 1) * width]
            down = gd_ref[:, index * units : (index + 1) * units].T.astype(BF16)
            out_ref[index, ff // width * part :, :] = down


def slot_block(rows, cols, first=0):
    return pl.BlockSpec((rows, cols), lambda i: (i + first, 0))


def expert_first(at, hidden, cots, wr, parts, filled, start, count, sums=()):
    _, rows, width = hidden[0].shape
    ff = (parts.shape[1] - 2 * width // 8) * 8
    blocks = BLOCKS[start : start + count]
    kinds = tuple(sorted({piece for block in blocks for piece, _ in block}))
    outs = [(8, rows, F32), *[(rows, width, BF16)] * 5]
    anywhere = pl.BlockSpec(memory_space=pl.ANY)
    if sums:
        more_specs, more = [whole(parts.shape)], [in_hbm(parts.shape, BF16)]
    else:
        more_specs, more = [whole((width, ff))] * 2, [in_hbm((width, ff), F32)] * 2
    return pl.pallas_call(
        functools.partial(expert_first_kernel, 2, filled, blocks, kinds),
        grid=(count,),
        in_specs=[
            SCALARS,
            whole(wr.shape),
            *[anywhere] * (3 + len(kinds) + len(sums)),
        ],
        out_specs=[slot_block(a, b) for a, b, _ in outs] + more_specs,
        out_shape=[in_hbm((count * a, b), kind) for a, b, kind in outs] + more,
        scratch_shapes=[
            pltpu.VMEM((width, ff), BF16),
            pltpu.VMEM((ff, width), BF16),
            pltpu.SemaphoreType.DMA((4,)),
            pltpu.VMEM((4 * count, rows, width), BF16),
            pltpu.SemaphoreType.DMA((count,)),
            pltpu.VMEM((rows, ff), BF16),
            pltpu.VMEM((rows, ff), BF16),
            pltpu.VMEM((width, ff), F32),
            pltpu.VMEM((width, ff), F32),
        ],
        compiler_params=params(48),
        cost_estimate=TINY,
        name="expert_first",
    )(*placed(at, wr, parts, *[hidden[k] for k in kinds], *cots, *sums, free=(*hidden, cots[1])))


def expert_second_kernel(
    splits, step_count, filled, at_ref, pos_ref, xs_ref, cs_ref, g_ref, ret0_ref, dx0_ref, wr_ref,
    parts_ref, *refs,
):
    step = pl.program_id(0)
    rows = xs_ref.shape[0]
    *refs, up_ref, down_ref, sem = refs
    early = step_count == EARLY
    if early:
        act_ref, gp_ref, dh_m, dh_o, ret_m, ret_o, extra_m, extra_o = refs
        firsts = [((dh_m, ret_m), 0), ((dh_o, ret_o), 0)]
        targets = [[(dh, 0, back, 0), (dh, 1, back, 1)] for (dh, back), _ in firsts]
        targets += [
            [(dh, 2, back, 2), (extra, 0, extra, 1)]
            for ((dh, back), _), extra in zip(firsts, (extra_m, extra_o))
        ]
    else:
        act_ref, gp_ref, dh_m, dh_o, ret_m, ret_o = refs
        targets = [[(a, 0, b, 0), (a, 1, b, 1)] for a, b in ((dh_m, ret_m), (dh_o, ret_o))]

    @pl.when(step == 0)
    def _():
        copies = load_weights(parts_ref, up_ref, down_ref, sem)
        for copy in copies:
            copy.start()
        for copy in copies:
            copy.wait()

    ret, dx = hidden_units(splits, xs_ref[...], g_ref, up_ref, down_ref, act_ref, gp_ref)
    ret = ret + ret0_ref[...].astype(F32)
    weight = weight_of(xs_ref[...], wr_ref, at_ref[2])
    gate = jnp.sum(cs_ref[...].astype(F32) * ret, axis=-1, keepdims=True)
    dxb = (dx + dx0_ref[...].astype(F32)).astype(BF16)
    high, middle = two_parts(gate)
    low = (gate - high.astype(F32) - middle.astype(F32)).astype(BF16)
    lane = lax.broadcasted_iota(jnp.int32, (1, 128), 1) - filled % 16 - 3 * at_ref[2]
    gates = jnp.where(lane == 0, high.astype(F32), 0.0)
    gates = jnp.where(lane == 1, middle.astype(F32), gates)
    gates = jnp.where(lane == 2, low.astype(F32), gates).astype(BF16)
    retb = (ret * weight).astype(BF16)
    slot = lax.broadcasted_iota(jnp.int32, (rows, rows), 1).astype(F32)
    lanes = -(-rows // 128) * 128
    tall = jnp.concatenate([pos_ref[...], jnp.zeros((8, lanes - rows), F32)], axis=1)
    tall = jnp.concatenate([tall, jnp.zeros((120, lanes), F32)], axis=0).T
    picks = [(slot == tall[:rows, k : k + 1]).astype(F32).astype(BF16) for k in range(2)]
    for number, target in enumerate(targets):

        @pl.when(step == number)
        def _(target=target):
            for pick, (dh, i, back, j) in zip(picks, target):
                back[j] = dot(pick, retb).astype(BF16)
                out = dot(pick, dxb)
                dh[i] = out.astype(BF16)
                tail = dot(pick, gates)
                tail = jnp.concatenate([tail, jnp.zeros((lanes - rows, 128), F32)], axis=0).T[:16, :rows]
                tail = jnp.concatenate(
                    [tail, jnp.zeros((16, out.shape[1] - rows), F32)], axis=1
                )
                start = filled // 16 * 16
                dh[i, start : start + 16, :] = (out[start : start + 16] + tail).astype(BF16)


def expert_second(at, first, wr, parts, filled):
    pos, xs, cs, g, ret, dx = first
    rows, width = pos.shape[1], xs.shape[1]
    count = xs.shape[0] // rows
    ff = (parts.shape[1] - 2 * width // 8) * 8
    sizes = (3, 3, 3, 3, 2, 2) if count == EARLY else (2, 2, 2, 2)
    return pl.pallas_call(
        functools.partial(expert_second_kernel, 2, count, filled),
        grid=(count,),
        in_specs=[
            SCALARS,
            slot_block(8, rows),
            slot_block(rows, width),
            slot_block(rows, width),
            slot_block(rows, width),
            slot_block(rows, width),
            slot_block(rows, width),
            whole(wr.shape),
            pl.BlockSpec(memory_space=pl.ANY),
        ],
        out_specs=[slot_block(rows, ff), slot_block(rows, ff)]
        + [whole((n, rows, width)) for n in sizes],
        out_shape=[
            in_hbm((count * rows, ff), BF16),
            in_hbm((count * rows, ff), BF16),
        ]
        + [jax.ShapeDtypeStruct((n, rows, width), BF16) for n in sizes],
        scratch_shapes=[
            pltpu.VMEM((width, ff), BF16),
            pltpu.VMEM((ff, width), BF16),
            pltpu.SemaphoreType.DMA((2,)),
        ],
        compiler_params=params(30),
        cost_estimate=TINY,
        name="expert_second",
    )(*placed(at, pos, xs, cs, g, ret, dx, wr, parts))


def weight_grad_kernel(ends, *refs):
    count = len(ends)
    xs, gs, gps, acts = (refs[i * count : (i + 1) * count] for i in range(4))
    out_ref, xs_t, g_t, turned = refs[4 * count :]
    step = pl.program_id(0)
    width = xs_t.shape[0]
    part, cols = width // 8, gps[0].shape[1]
    spans = list(zip((0, *ends[:-1]), ends))

    @pl.when(step == 0)
    def _():
        for (low, high), x_ref, g_ref in zip(spans, xs, gs):
            xs_t[:, low:high] = x_ref[...].T
            g_t[:, low:high] = g_ref[...].T

    up = down = None
    for (low, high), gp, act in zip(spans, gps, acts):
        one, two = dot(xs_t[:, low:high], gp[...]), dot(g_t[:, low:high], act[...])
        up, down = (one, two) if up is None else (up + one, down + two)
    turned[:width, :] = up.astype(BF16)
    block = step * cols // width
    lanes = pl.ds(pl.multiple_of(step * cols % width, cols), cols)
    into = pl.ds(pl.multiple_of(block * part, part), part)
    for index in range(8):
        out_ref[index, into, lanes] = turned[index * part : (index + 1) * part, :]
    half = cols // 2
    first = out_ref.shape[1] - half
    tall = down.T.astype(BF16)
    out_ref[2 * step, first:, :] = tall[:half]
    out_ref[2 * step + 1, first:, :] = tall[half:]


def weight_grad(xs, g, gps, acts):
    width, ff = xs[0].shape[1], gps[0].shape[1]
    cols = ff // 4
    out = (8, ff // width * (width // 8) + ff // 8, width)
    ends = []
    for gp in gps:
        ends.append(gp.shape[0] + (ends[-1] if ends else 0))
    slots = ends[-1]
    return pl.pallas_call(
        functools.partial(weight_grad_kernel, tuple(ends)),
        grid=(4,),
        in_specs=[whole(a.shape) for a in (*xs, *g)]
        + [pl.BlockSpec((a.shape[0], cols), lambda i: (0, i)) for a in (*gps, *acts)],
        out_specs=whole(out),
        out_shape=in_hbm(out, BF16),
        scratch_shapes=[
            pltpu.VMEM((width, slots), BF16),
            pltpu.VMEM((width, slots), BF16),
            pltpu.VMEM((width, cols), BF16),
        ],
        compiler_params=params(30),
        cost_estimate=TINY,
        name="weight_grad",
    )(*placed(*xs, *g, *gps, *acts))


def settle_kernel(at_ref, zero_ref, one_ref, up_ref, down_ref):
    part, units = up_ref.shape[1], zero_ref.shape[1] - 2 * up_ref.shape[1]
    for half, ref in enumerate((zero_ref, one_ref)):
        for index in range(8):
            rows = slice(index // 4 * part, index // 4 * part + part)
            to = (2 * index + half) * units
            from_ = index % 4 * units
            up_ref[0, :, to : to + units] = ref[0, rows, from_ : from_ + units].astype(F32)
        down_ref[0, half * units : (half + 1) * units, :] = ref[0, 2 * part :, :].astype(F32)


def settle_experts(at, zero, one):
    _, rows, width = zero.shape
    part = width // 8
    units = rows - 2 * part
    piece = pl.BlockSpec((1, rows, width), lambda i, at: (i ^ at[2], 0, 0))
    return pl.pallas_call(
        settle_kernel,
        grid_spec=pltpu.PrefetchScalarGridSpec(
            num_scalar_prefetch=1,
            grid=(E,),
            in_specs=[piece, piece],
            out_specs=[
                pl.BlockSpec((1, part, 16 * units), lambda i, at: (i, 0, 0)),
                pl.BlockSpec((1, 2 * units, width), lambda i, at: (i, 0, 0)),
            ],
        ),
        out_shape=[
            jax.ShapeDtypeStruct((E, part, 16 * units), F32),
            jax.ShapeDtypeStruct((E, 2 * units, width), F32),
        ],
        compiler_params=params(24),
        cost_estimate=TINY,
        name="settle_experts",
    )(*placed(at, zero, one))


def early_images(images, rows, width):
    return pl.BlockSpec((1, rows, width), lambda i: (jnp.minimum(i, images - 2), 0, 0))


def middle_back_kernel(
    filled, at_ref, a_ref, ar_ref, b_ref, br_ref, xr_ref, mid_ref, cot_ref, vec_ref, am_ref,
    got_ref, hidden_ref, wr_ref,
    gm_ref, low_ref, parts_ref, sums_ref, proj_ref, router_ref,
):
    rows, width = mid_ref.shape[1:]
    group = am_ref.shape[2]

    @pl.when(pl.program_id(0) == 0)
    def _():
        sums_ref[...] = jnp.zeros_like(sums_ref)
        proj_ref[...] = jnp.zeros_like(proj_ref)
        router_ref[...] = jnp.zeros_like(router_ref)

    last = pl.program_id(0) == pl.num_programs(0) - 1
    grad = jnp.where(
        last,
        b_ref[0].astype(F32) + br_ref[0].astype(F32),
        a_ref[0].astype(F32) + ar_ref[0].astype(F32),
    )
    grad = grad + xr_ref[0].astype(F32)
    gates = [grad[filled + 3 * e : filled + 3 * e + 3, :384] for e in range(E)]
    gates = [jnp.sum(g, axis=0, keepdims=True) for g in gates]
    gates = jnp.concatenate([jnp.zeros((4, 384), F32), *gates, jnp.zeros((120, 384), F32)], axis=0)
    gates = gates.T[:rows]
    router = routing(hidden_ref[0], wr_ref)
    mean = jnp.sum(router * gates, axis=-1, keepdims=True)
    logit_grad = (router * (gates - mean)).astype(BF16)
    row = lax.broadcasted_iota(jnp.int32, (rows, 1), 0)
    grad = jnp.where(row < filled, grad, 0.0) + dot_nt(logit_grad, wr_ref[...])
    router_ref[...] += dot_tn(hidden_ref[0], logit_grad)
    xhat, rstd = norm_parts(mid_ref[0])
    sums_ref[2:3, :] += jnp.sum(grad * xhat, axis=0, keepdims=True)
    sums_ref[3:4, :] += jnp.sum(grad, axis=0, keepdims=True)
    out = cot_ref[0].astype(F32) + norm_back(grad * vec_ref[2:3, :], xhat, rstd)
    out = jnp.where(row < filled, out, 0.0)
    gm_ref[0] = out
    low = out.astype(BF16)
    low_ref[0] = low
    proj_ref[:group, :] += dot_tn(am_ref[0], low)
    att_r = got_ref[pl.ds(pl.multiple_of(pl.program_id(0) * rows, 16), rows), :]
    proj_ref[group:, :] += dot_tn(att_r, low)

    @pl.when(pl.program_id(0) == pl.num_programs(0) - 1)
    def _():
        part = width // 8
        router = router_ref[...].T[:8]
        lines = jnp.concatenate(two_parts(sums_ref[...] + router), axis=0)
        row = lax.broadcasted_iota(jnp.int32, (width, 128), 0)
        col = lax.broadcasted_iota(jnp.int32, (width, 128), 1)
        for index in range(8):
            base = index * part
            from_ = pl.multiple_of(base ^ (at_ref[1] * group), part)
            parts_ref[index, :part, :] = proj_ref[pl.ds(from_, part), :].astype(BF16)
            pick = ((row == col + base) & (col < part)).astype(F32).astype(BF16)
            parts_ref[index, part:, :128] = dot(lines, pick).astype(BF16)
            parts_ref[index, part:, 128:] = jnp.zeros((16, width - 128), BF16)


def middle_back(at, mine, near, extra, extra_near, from_x, middle, cots, vecs, att_m, got, hidden, wr, filled):
    images, rows, width = middle.shape
    one = per_image(rows, width)
    group = att_m.shape[2]
    piece = (8, width // 8 + 16, width)
    return pl.pallas_call(
        functools.partial(middle_back_kernel, filled),
        grid=(images,),
        in_specs=[SCALARS]
        + [early_images(images, rows, width)] * 2
        + [pl.BlockSpec((1, rows, width), lambda i: (0, 0, 0))] * 2
        + [one] * 2
        + [one, whole(vecs.shape), per_image(rows, group), whole(got.shape)]
        + [one, whole(wr.shape)],
        out_specs=[one, one, whole(piece)],
        out_shape=[
            in_hbm(middle.shape, F32),
            jax.ShapeDtypeStruct(middle.shape, BF16),
            in_hbm(piece, BF16),
        ],
        scratch_shapes=[
            pltpu.VMEM((8, width), F32),
            pltpu.VMEM((width, width), F32),
            pltpu.VMEM((width, 128), F32),
        ],
        compiler_params=params(32),
        cost_estimate=TINY,
        name="middle_back",
    )(*placed(at, mine, near, extra, extra_near, from_x, middle, cots, vecs, att_m, got, hidden, wr, free=(near, extra_near, from_x)))


def mix_kernel(
    mid_ref, a_ref, ar_ref, b_ref, br_ref, x_ref, xr_ref, mine_ref, theirs_ref, send_ref
):
    last = pl.program_id(0) == pl.num_programs(0) - 1
    total = jnp.where(
        last,
        b_ref[0].astype(F32) + br_ref[0].astype(F32),
        a_ref[0].astype(F32) + ar_ref[0].astype(F32),
    )
    total = total + mid_ref[0]
    other = x_ref[0].astype(F32) + xr_ref[0].astype(F32)
    count = mine_ref.shape[1]
    mine_ref[0] = total[:count]
    theirs_ref[0] = other[count : 2 * count]
    send_ref[0, 0] = other[:count].astype(BF16)
    send_ref[0, 1] = total[count : 2 * count].astype(BF16)


def layer_mix(at, middle, mine, near, extra, extra_near, other, other_near, quarter):
    images, rows, width = middle.shape
    one, part = per_image(rows, width), per_image(quarter, width)
    return pl.pallas_call(
        lambda at_ref, *refs: mix_kernel(*refs),
        grid=(images,),
        in_specs=[
            SCALARS,
            one,
            *[early_images(images, rows, width)] * 2,
            *[pl.BlockSpec((1, rows, width), lambda i: (1, 0, 0))] * 2,
            one,
            one,
        ],
        out_specs=[part, part, per_image(2, quarter, width)],
        out_shape=[
            in_hbm((images, quarter, width), F32),
            in_hbm((images, quarter, width), F32),
            jax.ShapeDtypeStruct((images, 2, quarter, width), BF16),
        ],
        compiler_params=params(24),
        cost_estimate=TINY,
        name="layer_mix",
    )(*placed(at, middle, mine, near, extra, extra_near, other, other_near, free=(near, extra_near, other_near)))


def combine_kernel(at_ref, mine_ref, theirs_ref, got_ref, out_ref):
    ours = pl.program_id(0) // (pl.num_programs(0) // 2) == at_ref[2] // 2
    value = jnp.where(
        ours,
        mine_ref[0] + got_ref[0, 0].astype(F32),
        theirs_ref[0] + got_ref[0, 1].astype(F32),
    )
    out_ref[0] = value.astype(BF16)


def layer_combine(at, mine, theirs, got):
    half, quarter, width = mine.shape

    def image(i, at):
        return (jnp.where(i < half, i, (i + half - 1) % half), 0, 0)

    part = pl.BlockSpec((1, quarter, width), image)
    return pl.pallas_call(
        combine_kernel,
        grid_spec=pltpu.PrefetchScalarGridSpec(
            num_scalar_prefetch=1,
            grid=(2 * half,),
            in_specs=[
                part,
                part,
                pl.BlockSpec((1, 2, quarter, width), lambda i, at: (*image(i, at), 0)),
            ],
            out_specs=pl.BlockSpec((1, quarter, width), lambda i, at: (i, 0, 0)),
        ),
        out_shape=jax.ShapeDtypeStruct((2 * half, quarter, width), BF16),
        compiler_params=params(24),
        cost_estimate=TINY,
        name="layer_combine",
    )(*placed(at, mine, theirs, got))


def attend_back_kernel(
    head_dim, at_ref, lm_ref, lo_ref, pm_ref, qkv_ref, lse_ref, bias_ref, h1_ref, wq_ref,
    dm_ref, do_ref, gq_ref, grad_ref, low_ref,
):
    rows = lm_ref.shape[1]
    low_ref[:rows, :] = lm_ref[0]
    low_ref[rows:, :] = lo_ref[0]
    out_grad = dot_nt(low_ref[...], pm_ref[...]).astype(BF16)
    width = pm_ref.shape[0]
    bias = bias_ref[0]
    lane = lax.broadcasted_iota(jnp.int32, (1, 128), 1)
    sub = lax.broadcasted_iota(jnp.int32, (128, 1), 0)
    scaling = 1.0 / math.sqrt(head_dim)
    for pair in range(width // 128):
        cols = slice(pair * 128, pair * 128 + 128)
        k_cols = slice(width + pair * 128, width + pair * 128 + 128)
        v_cols = slice(2 * width + pair * 128, 2 * width + pair * 128 + 128)
        q2, k2, v2 = qkv_ref[0, :, cols], qkv_ref[0, :, k_cols], qkv_ref[0, :, v_cols]
        o2 = out_grad[:, cols]
        k_t = k2.T
        dv = dk = None
        both = []
        for part in range(2):
            mine = (lane >= head_dim * part) & (lane < head_dim * (part + 1))
            qm = jnp.where(mine, q2, jnp.zeros_like(q2))
            om = jnp.where(mine, o2, jnp.zeros_like(o2))
            head = 2 * pair + part
            probs = jnp.exp(dot_nt(k2, qm) + bias - lse_ref[0, head : head + 1, :])
            prob_grad = dot_nt(v2, om)
            delta = jnp.sum(probs * prob_grad, axis=0, keepdims=True)
            score_grad = (probs * (prob_grad - delta)).astype(BF16)
            dv_part = dot(probs.astype(BF16), om)
            dk_part = dot(score_grad, qm)
            dv = dv_part if dv is None else dv + dv_part
            dk = dk_part if dk is None else dk + dk_part
            both.append(dot(k_t, score_grad))
        dq = (jnp.where(sub < head_dim, both[0], both[1]) * scaling).astype(BF16).T
        grad_ref[:, cols] = dq
        grad_ref[:, k_cols] = dk.astype(BF16)
        grad_ref[:, v_cols] = dv.astype(BF16)
    hidden_grad = dot_nt(grad_ref[...], wq_ref[...]).astype(BF16)
    dm_ref[0] = hidden_grad[:rows]
    do_ref[0] = hidden_grad[rows:]
    grad_qkv = dot_tn(h1_ref[0], grad_ref[...])

    @pl.when(pl.program_id(0) == 0)
    def _():
        gq_ref[...] = grad_qkv

    @pl.when(pl.program_id(0) > 0)
    def _():
        gq_ref[...] += grad_qkv


def attend_back(at, low_m, low_o, proj_m, qkv, lse, bias, hidden_one, wq, head_dim):
    images, rows, width = low_m.shape
    group = proj_m.shape[0]
    return pl.pallas_call(
        functools.partial(attend_back_kernel, head_dim),
        grid=(images,),
        in_specs=[
            SCALARS,
            per_image(rows, width),
            per_image(rows, width),
            whole(proj_m.shape),
            per_image(2 * rows, 3 * group),
            per_image(8, 2 * rows),
            per_image(2 * rows, 1),
            per_image(2 * rows, width),
            whole(wq.shape),
        ],
        out_specs=[
            per_image(rows, width),
            per_image(rows, width),
            whole((width, 3 * group)),
        ],
        out_shape=[
            in_hbm((images, rows, width), BF16),
            jax.ShapeDtypeStruct((images, rows, width), BF16),
            in_hbm((width, 3 * group), F32),
        ],
        scratch_shapes=[
            pltpu.VMEM((2 * rows, 3 * group), BF16),
            pltpu.VMEM((2 * rows, width), BF16),
        ],
        compiler_params=params(48),
        cost_estimate=TINY,
        name="attend_back",
    )(*placed(at, low_m, low_o, proj_m, qkv, lse, bias, hidden_one, wq, free=(low_m, low_o)))


def input_back_kernel(
    x_ref, gm_ref, vec_ref, a_ref, ar_ref, gq_ref, r_ref,
    out_ref, go_ref, parts_ref, sums_ref,
):
    step, images = pl.program_id(0), pl.num_programs(0)
    grad = a_ref[0].astype(F32) + ar_ref[0].astype(F32)
    xhat, rstd = norm_parts(x_ref[0].astype(F32))
    out = gm_ref[0] + norm_back(grad * vec_ref[0:1, :], xhat, rstd)
    count = out_ref.shape[1]
    out_ref[0] = out[:count]
    go_ref[0] = out[count : 2 * count].astype(BF16)

    @pl.when(step == 0)
    def _():
        sums_ref[...] = jnp.zeros_like(sums_ref)

    sums_ref[0:1, :] += jnp.sum(grad * xhat, axis=0, keepdims=True)
    sums_ref[1:2, :] += jnp.sum(grad, axis=0, keepdims=True)

    @pl.when(step == images - 1)
    def _():
        total = gq_ref[...]
        width = grad.shape[1]
        part = width // 8
        lines = jnp.concatenate(two_parts(sums_ref[...]), axis=0)
        row = lax.broadcasted_iota(jnp.int32, (width, 128), 0)
        col = lax.broadcasted_iota(jnp.int32, (width, 128), 1)
        for index in range(8):
            base = index * part
            own = total[base : base + part].astype(BF16)
            half = jnp.concatenate([own[: part // 2, width:], own[part // 2 :, width:]], axis=1)
            into = (col >= part) & (col < 2 * part)
            pick_line = ((row == col - part + base) & into).astype(F32).astype(BF16)
            line = dot(lines, pick_line).astype(BF16)
            tail = jnp.concatenate([line, jnp.zeros((16, width - 128), BF16)], axis=1)
            block = jnp.concatenate([own[:, :width], half], axis=0)
            last = part + block.shape[0]
            parts_ref[index, part:last] = block
            parts_ref[index, last:] = r_ref[index, part:] + tail

        parts_ref[:, :part] = r_ref[:, :part]


def input_back(x_own, grad_middle, vecs, mine, near, grads, r_parts, quarter):
    images, rows, width = x_own.shape
    one, part = per_image(rows, width), per_image(quarter, width)
    more = r_parts.shape[1] + width // 8 + (grads.shape[1] - width) * (width // 8) // width
    more = (8, more, width)
    return pl.pallas_call(
        input_back_kernel,
        grid=(images,),
        in_specs=[one, one, whole(vecs.shape), one, one, whole(grads.shape), whole(r_parts.shape)],
        out_specs=[part, part, whole(more)],
        out_shape=[
            jax.ShapeDtypeStruct((images, quarter, width), F32),
            jax.ShapeDtypeStruct((images, quarter, width), BF16),
            in_hbm(more, BF16),
        ],
        scratch_shapes=[pltpu.VMEM((8, width), F32)],
        compiler_params=params(32),
        cost_estimate=TINY,
        name="input_back",
    )(*placed(x_own, grad_middle, vecs, mine, near, grads, r_parts, free=(near,)))


def shards(
    tokens,
    key_mask,
    expert_ids,
    ln1_gain,
    ln1_bias,
    qkv_weight,
    proj_weight,
    ln2_gain,
    ln2_bias,
    router_weight,
    up_weight,
    down_weight,
    cotangent,
):
    n_seq, n_wide = lax.axis_size("seq"), lax.axis_size("wide")
    images, quarter, width = tokens.shape
    head_dim = width // H
    group = width // 2
    filled = 2 * quarter
    rows = -(-(filled + 3 * E) // 16) * 16
    place = lax.axis_index("seq")
    chip, core = place // 2, place % 2
    direct = n_wide == 8
    spot = lax.axis_index("wide") if direct else 0
    at = jnp.stack([jnp.int32(spot), core, place, jnp.int32(spot) % 2])
    part = width // 8

    def over_seq(a, turn):
        return lax.ppermute(a, "seq", [(i, i ^ turn) for i in range(n_seq)])

    def over_x(a):
        return over_seq(a, 2)

    def over_core(a):
        return over_seq(a, 1)

    def over_wide(a, turn):
        return lax.ppermute(a, "wide", [(i, i ^ turn) for i in range(n_wide)])

    def after(value, *first):
        return lax.optimization_barrier((value, *first))[0]

    def images_of(a, of_chip):
        pair = lax.dynamic_slice_in_dim(a, of_chip * (images - 2), 2, 0)
        single = lax.dynamic_slice_in_dim(a, images // 2 - 1 + of_chip, 1, 0)
        return jnp.concatenate([pair, single], axis=0)

    def joined(first, second):
        both = jnp.concatenate([first, second], axis=1)
        return jnp.pad(both, ((0, 0), (0, rows - filled)) + ((0, 0),) * (both.ndim - 2))

    def cells(quarters, of_chip, of_core):
        first = lax.dynamic_index_in_dim(quarters, 2 * of_chip + of_core, 1, False)
        second = lax.dynamic_index_in_dim(quarters, 2 * (1 - of_chip) + of_core, 1, False)
        return joined(images_of(first, of_chip), images_of(second, of_chip))

    mask = key_mask.reshape(images, n_seq, quarter)
    valid = jnp.concatenate([cells(mask, chip, core), cells(mask, chip, 1 - core)], axis=1)
    bias = jnp.where(valid > 0, 0.0, BIG).astype(F32)[..., None]

    def heads_of(a):
        return jnp.concatenate(
            [lax.dynamic_slice_in_dim(a, (2 * i + core) * group, group, 1) for i in range(3)],
            axis=1,
        )

    wq = heads_of(qkv_weight)
    proj = lax.dynamic_slice_in_dim(proj_weight, core * group, group, 1)
    lines = jnp.stack([ln1_gain, ln1_bias, ln2_gain, ln2_bias])
    lines = jnp.concatenate([lines, router_weight.T], axis=0)
    up = lax.dynamic_index_in_dim(up_weight, place, 0, False)
    down = lax.dynamic_index_in_dim(down_weight, place, 0, False)
    units = down.shape[0] // 2

    def first_parts(wq, proj, lines):
        both = jnp.concatenate([wq, proj], axis=1)
        fill = ((0, 16 - lines.shape[0]), (0, both.shape[1] - lines.shape[1]))
        return jnp.concatenate([both, jnp.pad(lines, fill)], axis=0)

    def half_of(up, down, half):
        cols = up.reshape(up.shape[0], n_wide, 2, units)[:, :, half].reshape(up.shape[0], -1)
        down = down.reshape(-1, 2, units, width)[:, half].reshape(-1, width)
        blocks = [cols[:, i : i + width] for i in range(0, cols.shape[1], width)]
        return jnp.concatenate([*blocks, down], axis=0)

    one_all = first_parts(wq, proj, lines)
    one_all = jnp.broadcast_to(one_all[None], (4, *one_all.shape))
    codes = (expert_ids[..., 0] * E + expert_ids[..., 1]).astype(BF16)
    codes = jnp.pad(codes, ((0, 0), (0, width - quarter)))[:, None, :]
    cot = jnp.concatenate([cotangent, codes], axis=1)
    x_got = over_x(images_of(after(tokens, one_all), 1 - chip))
    x_own = joined(images_of(tokens, chip), x_got)
    x_oth = over_core(after(x_own, bias, cot))
    cot_got = over_x(after(cot, x_got))

    z_groups = [[y + 2 * z for z in range(4)] for y in range(2)]

    def all_of(a, axis=0):
        return lax.all_gather(a, "wide", axis=axis, tiled=True)

    if direct:
        ones = lax.all_to_all(one_all, "wide", 0, 0, axis_index_groups=z_groups, tiled=True)
        ones_y = over_wide(ones, 1)
        twos, threes = (
            lax.all_gather(after(half_of(up, down, half), ones, x_oth), "wide") for half in range(2)
        )
    else:

        def eight(a, axis=0):
            return jnp.split(a, 8, axis=axis)

        ones = jnp.stack([first_parts(*a) for a in zip(eight(all_of(wq)), eight(all_of(proj)), eight(all_of(lines, 1), 1))])
        ones, ones_y = ones[::2], ones[1::2]
        ups, downs = eight(all_of(up)), eight(all_of(down))
        twos, threes = (
            jnp.stack([half_of(a, b, half) for a, b in zip(ups, downs)]) for half in range(2)
        )

    att_m, mail, qkv, hidden_one, lse, wq, small, vecs = attend(
        at, x_own, x_oth, bias, ones, ones_y, head_dim
    )
    mail_got = over_core(mail)
    middle, hidden_two, proj_m = project(at, att_m, mail, mail_got, x_own, vecs)
    cots_m = join_cots(at, cot, after(cot_got, hidden_two), rows)
    cots_o = over_core(cots_m)
    hidden_b = over_x(hidden_two)
    hidden_c = over_core(hidden_two)
    ours = (hidden_two, None, hidden_c, None)
    *first_a, gu_a, gd_a = expert_first(
        at, ours, (cots_m, cots_o), small, twos, filled, EARLY, len(BLOCKS) - EARLY
    )
    hidden_d = over_core(after(hidden_b, gu_a))
    hidden = (hidden_two, hidden_b, hidden_c, hidden_d)
    *first_b, parts0 = expert_first(
        at, hidden, (cots_m, cots_o), small, twos, filled, 0, EARLY, (gu_a, gd_a)
    )
    act1, gp1, dh_m, dh_o, ret_m, ret_o, extra_m, extra_o = expert_second(
        after(at, parts0), first_b, small, threes, filled
    )
    dh_r = over_core(dh_o)
    dh_b = dh_m + dh_r
    dh_x = over_x(dh_b)
    ret_r = over_core(ret_o)
    def over_y(send, keep, *first):
        if not direct:
            return jnp.stack([keep, send], axis=1)
        got = over_wide(send, 1)
        return after(keep, *first) + after(got, *first)

    def over_z(both):
        return lax.all_to_all(both, "wide", 0, 0, axis_index_groups=z_groups, tiled=True)

    def expert_sum(both):
        both = both.reshape(8, -1, width)
        cut = 2 * part
        cols = jnp.moveaxis(both[:, :cut].reshape(8, 2, part, width), 1, 2).reshape(width, -1)
        rows = both[:, cut:].reshape(-1, width)
        return tuple(
            lax.psum_scatter(a, "wide", scatter_dimension=0, tiled=True) for a in (cols, rows)
        )

    def near_pair(a):
        return jnp.stack([a, over_core(a)])

    def near_experts(pairs):
        return jnp.concatenate([pairs, over_x(pairs)], axis=0)

    extra_r = over_core(extra_o)
    act2, gp2, late_m, late_o, late_ret_m, late_ret_o = expert_second(
        after(at, dh_b), first_a, small, threes, filled
    )
    late_r = over_core(late_o)
    late_ret_r = over_core(late_ret_o)
    if direct:
        sum0 = lax.all_to_all(parts0, "wide", 0, 0, tiled=True)

    xs = (first_b[1], first_a[1])
    parts1 = weight_grad(xs, (first_b[3], first_a[3]), [gp1, gp2], [act1, act2])
    layer_mine, layer_theirs, layer_send = layer_mix(
        after(at, parts1), middle, late_ret_m, late_ret_r, extra_m, extra_r, ret_m, ret_r, quarter
    )
    layer_got = over_x(after(layer_send, dh_x))

    grad_middle, low_m, r_parts = middle_back(
        at,
        late_m,
        late_r,
        extra_m,
        extra_r,
        dh_x,
        middle,
        cots_m,
        vecs,
        att_m,
        mail_got,
        hidden_two,
        small,
        filled,
    )
    low_o = over_core(low_m)
    if direct:
        sum1 = lax.all_to_all(after(parts1, dh_x, layer_send), "wide", 0, 0, tiled=True)
    dh1_m, dh1_o, grad_qkv = attend_back(
        at, low_m, low_o, proj_m, qkv, lse, bias, hidden_one, wq, head_dim
    )
    dh1_o = after(dh1_o, layer_got)
    dh1_r = over_core(dh1_o)
    input_mine, input_send, q_parts = input_back(
        x_own, grad_middle, vecs, dh1_m, dh1_r, grad_qkv, r_parts, quarter
    )
    last = q_parts.shape[1] - 16
    input_got = over_x(input_send)
    if direct:
        rest = lax.all_to_all(q_parts, "wide", 0, 0, tiled=True)
        sum0, sum1 = (
            jnp.sum(after(a, q_parts).astype(F32), axis=0).astype(BF16) for a in (sum0, sum1)
        )
        pair0, pair1 = near_pair(sum0), near_pair(sum1)
        near0, near1 = near_experts(pair0), near_experts(pair1)
        at = after(at, pair0, pair1)
    else:
        sum0 = expert_sum(parts0)
        sum1 = expert_sum(parts1)

    def settle(mine, got):
        got = got.astype(mine.dtype)
        pair, rest = slice(0, 2), slice(2, 3)
        return jnp.where(
            chip == 0,
            jnp.concatenate([mine[pair], mine[rest], got[rest], got[pair]], axis=0),
            jnp.concatenate([got[pair], got[rest], mine[rest], mine[pair]], axis=0),
        )

    input_grad = settle(input_mine, input_got)
    layer_out = layer_combine(after(at, q_parts), layer_mine, layer_theirs, layer_got)
    if not direct:

        def in_order(a):
            four = near_experts(near_pair(a))
            return jnp.stack(
                [lax.dynamic_index_in_dim(four, place ^ e, 0, False) for e in range(E)]
            ).astype(F32)

        up0, up1, down0, down1 = (in_order(s[i]) for i in range(2) for s in (sum0, sum1))
        halves = [a.reshape(E, -1, n_wide, units) for a in (up0, up1)]
        grad_up = jnp.stack(halves, axis=3).reshape(E, -1, up.shape[1])
        grad_down = jnp.concatenate([down0, down1], axis=1)

    def over_seq_group(rows, lines):
        count = rows.shape[0]

        def sent(over, rows, lines):
            got = over(jnp.concatenate([rows.astype(BF16), *two_parts(lines)])).astype(F32)
            low = got[count : count + lines.shape[0]] + got[count + lines.shape[0] :]
            return got[:count], lines + low

        got, lines = sent(over_x, rows, lines)
        rows = rows + got
        other, lines = sent(over_core, rows, lines)
        return rows, other, lines

    owned = proj_weight.shape[0]
    if direct:
        rest = after(rest, layer_out, input_grad)
        rest = jnp.sum(rest.astype(F32), axis=0)
        rows, lines = rest[:last], rest[last : last + 8] + rest[last + 8 :]
        lines = jnp.concatenate([lines[:, :part], lines[:, part : 2 * part]])
        lines = jnp.pad(lines, ((0, 0), (0, width - part)))
    else:
        both = q_parts.astype(F32)
        rows = [both[:, :part], both[:, part : 2 * part]]
        halves = both[:, 2 * part : last].reshape(8, -1, 2, group)
        rows.append(jnp.moveaxis(halves, 2, 1).reshape(8, part, group))
        two = both[:, last : last + 8] + both[:, last + 8 :]
        for low in (0, part):
            rows.append(jnp.moveaxis(two[:, :, low : low + part], 1, 2))
        rows = jnp.concatenate(rows, axis=2).reshape(width, -1)
        rows = lax.psum_scatter(rows, "wide", scatter_dimension=0, tiled=True)
        lines = jnp.pad(rows[:, -16:].T, ((0, 0), (0, width - owned)))
        more = rows[:, 2 * width : -16]
        more = jnp.concatenate([more[: owned // 2], more[owned // 2 :]], axis=1)
        rows = jnp.concatenate([rows[:, :width], rows[:, width : 2 * width], more])
    total, other, lines = over_seq_group(rows, lines)
    if direct:
        grad_up, grad_down = settle_experts(after(at, rows), near0, near1)
    grad_proj = total[:owned] + other[:owned]

    def thirds(a):
        more = a[2 * owned :]
        more = jnp.concatenate([more[:, :group], more[:, group:]])
        return [a[owned : 2 * owned, :group], a[owned : 2 * owned, group:], more]

    lines = lines[:, :owned]
    pairs = zip(thirds(total), thirds(other))
    ordered = [(jnp.where(core == 0, a, b), jnp.where(core == 0, b, a)) for a, b in pairs]
    grad_qkv = jnp.concatenate([a for pair in ordered for a in pair], axis=1)
    return (
        layer_out,
        input_grad,
        lines[8],
        lines[9],
        grad_qkv,
        grad_proj,
        lines[2],
        lines[3],
        lines[4 : 4 + E].T,
        grad_up,
        grad_down,
    )


def solution(mesh):
    placed = (
        P("wide", "seq", None),
        P("wide", None),
        P("wide", "seq", None),
        P("wide"),
        P("wide"),
        P("wide", None),
        P("wide", None),
        P("wide"),
        P("wide"),
        P("wide", None),
        P(None, "wide", None),
        P(None, "wide", None),
        P("wide", "seq", None),
    )
    return jax.shard_map(
        shards,
        mesh=mesh,
        in_specs=placed,
        out_specs=(
            P("wide", "seq", None),
            P("wide", "seq", None),
            P("wide"),
            P("wide"),
            P("wide", None),
            P("wide", None),
            P("wide"),
            P("wide"),
            P("wide", None),
            P(None, "wide", None),
            P(None, "wide", None),
        ),
        check_vma=False,
    )
```
